512 devices in a mesh: brick: 128 (over z, y, core), band: 4 (over x).
Axes of the slice: x: 4, y: 4, z: 16, core: 2. Of those that a mesh axis runs over, the one named last changes fastest.
Arguments:
- psi_val: bfloat16 [1024, 256, 2048], P('band', 'brick'), may hold values from -1.1953125 to 1.1953125
- psi_cond: bfloat16 [1024, 256, 2048], P('band', 'brick'), may hold values from -1.1953125 to 1.1953125
- dielectric: float32 [256, 2048], P('brick'), may hold values from 1 to 20
- point_owner: int32 [128], replicated, may hold values from 0 to 127, as said below
- point_cell: int32 [128], replicated, may hold values from 0 to 4095
Outputs:
- pair_field: float32 [128, 256, 2048], P('band', 'brick')
- potential: float32 [128, 256, 2048], P('band', 'brick')
The draws below stay inside these ranges and needn't reach their ends.
Inputs may be any that keep to these rules, and one draw needn't show every extreme that they name: `point_owner`: no brick owns more than 4 points, and one brick owns exactly 4.
All inputs are finite; a program needn't handle non-finite values.
Results may differ from the reference program's by a relative error of at most 0.0003.
Values may be sent and summed in bfloat16 or wider, within the bound.
A program may use at most 64 MiB of HBM per device.

```python
import math
import jax
import jax.numpy as jnp
from jax import lax

NV = 1024
NC = 1024
NP = 128
NY = 32
NZ = 64
SWEEPS = 4
NX = 256
PLANE = 2048
CELLS_DEV = 4096
MOST = 4
N_BRICK = 128


def draw_point_owner(key, part):
    key = jax.random.fold_in(key, 11)
    first_key, second_key = jax.random.split(key)
    total_slots = N_BRICK * MOST
    shuffled = jax.random.permutation(first_key, total_slots)
    leading = shuffled[0] // MOST
    score = jnp.where(shuffled // MOST == leading, -1, jnp.arange(total_slots))
    order = jnp.argsort(score, stable=True)
    chosen = shuffled[order[:NP]] // MOST
    mixing = jax.random.permutation(second_key, NP)
    return chosen[mixing].astype(jnp.int32)


def with_ends(array, key, low, high):
    longest = array.shape.index(max(array.shape))
    spots = []
    for shift in (0, 1):
        where = [jax.random.randint(jax.random.fold_in(key, axis), (), 0, length) for axis, length in enumerate(array.shape)]
        where[longest] = (where[longest] + shift) % array.shape[longest]
        spots.append(tuple(where))
    return array.at[spots[0]].set(low).at[spots[1]].set(high)


def steps_of(key, extent, cuts, smallest, largest):
    factor_of = 1.0
    for axis_at, parts in cuts:
        heights = jax.random.uniform(jax.random.fold_in(jax.random.fold_in(key, 6), axis_at), (parts,), jnp.float32, smallest / len(cuts), largest / len(cuts))
        factor_of = factor_of * jnp.repeat(jnp.exp(heights), extent[axis_at] // parts).reshape((-1,) + (1,) * (len(extent) - 1 - axis_at))
    return factor_of


def noise(key, shape, scale, limit, cuts=(), dtype=jnp.bfloat16):
    entries = jax.random.normal(key, shape, jnp.float32) * scale
    if len(cuts) > 0:
        entries = steps_of(key, shape, cuts, -0.22, 0.18) * entries
    return jnp.clip(entries, min=-limit, max=limit).astype(dtype)


def setup_inputs(seed: int = 0) -> dict:
    seeds = jax.random.split(jax.random.key(seed), 6)
    psi_val = noise(seeds[0], (NV, NX, PLANE), 0.177, 1.1953125, ((0, 4), (1, 128)))
    psi_cond = noise(seeds[1], (NC, NX, PLANE), 0.177, 1.1953125, ((0, 4), (1, 128)))
    dielectric = jnp.clip(jnp.exp(math.log(20.0) - 2.9957323 * jax.random.uniform(seeds[2], (NX, PLANE), jnp.float32) ** steps_of(seeds[2], (NX, PLANE), ((0, 128),), -0.2, 0.2)), 1.0, 20.0)
    point_owner = draw_point_owner(jax.random.fold_in(seeds[5], 71), 0)
    point_cell = with_ends(jax.random.randint(seeds[4], (NP,), 0, CELLS_DEV), jax.random.fold_in(seeds[4], 1), 0, CELLS_DEV - 1).astype(jnp.int32)
    return {"psi_val": psi_val, "psi_cond": psi_cond, "dielectric": dielectric, "point_owner": point_owner, "point_cell": point_cell}


FOURPI = 12.566370614359172
OMEGA = 0.8


def face_terms(eps):
    xplus = 0.5 * (eps + jnp.roll(eps, -1, 0))
    xminus = 0.5 * (eps + jnp.roll(eps, 1, 0))
    yplus = 0.5 * (eps + jnp.roll(eps, -1, 1))
    yminus = 0.5 * (eps + jnp.roll(eps, 1, 1))
    padded = jnp.pad(eps, ((0, 0), (0, 0), (1, 1)), mode="edge")
    zplus = 0.5 * (eps + padded[:, :, 2:])
    zminus = 0.5 * (eps + padded[:, :, :-2])
    return xplus, xminus, yplus, yminus, zplus, zminus


def reference(psi_val, psi_cond, dielectric, point_owner, point_cell):
    flat = (point_owner * CELLS_DEV + point_cell).astype(jnp.int32)
    ncell = NX * NY * NZ
    val = psi_val.reshape(NV, ncell)
    cond = psi_cond.reshape(NC, ncell)
    zv = jnp.take(val, flat, axis=1)
    zc = jnp.take(cond, flat, axis=1)
    pv = lax.dot_general(zv, val, (((0,), (0,)), ((), ())), preferred_element_type=jnp.float32)
    pc = lax.dot_general(zc, cond, (((0,), (0,)), ((), ())), preferred_element_type=jnp.float32)
    pair = (pv * pc).reshape(NP, NX, NY, NZ)
    xplus, xminus, yplus, yminus, zplus, zminus = face_terms(dielectric.reshape(NX, NY, NZ))
    diag = xplus + xminus + yplus + yminus + zplus + zminus
    rhs = FOURPI * pair
    potential = jnp.zeros_like(pair)
    for sweep in range(SWEEPS):
        zpad = jnp.pad(potential, ((0, 0), (0, 0), (0, 0), (1, 1)))
        beside = xplus * jnp.roll(potential, -1, 1) + xminus * jnp.roll(potential, 1, 1)
        beside = beside + yplus * jnp.roll(potential, -1, 2) + yminus * jnp.roll(potential, 1, 2)
        beside = beside + zplus * zpad[:, :, :, 2:] + zminus * zpad[:, :, :, :-2]
        applied = diag * potential - beside
        potential = potential + OMEGA * (rhs - applied) / diag
    return pair.reshape(NP, NX, NY * NZ), potential.reshape(NP, NX, NY * NZ)
```

```python
import functools

import jax
import jax.numpy as jnp
from jax import lax
from jax.experimental import pallas as pl
from jax.experimental.pallas import tpu as pltpu
from jax.sharding import PartitionSpec as P

NZ = 64
FOURPI = 12.566370614359172
OMEGA = 0.8

CORES = 2
CHIPS_Y = 4
MOST = 4
BLOCK = 4 * MOST
GROUP = 512
LANES = 128
STEP = 32700.0
CODE = 128.0
MESH = pl.DeviceIdType.MESH
F32 = jnp.float32
BF16 = jnp.bfloat16


def iota(shape, dim):
    return lax.broadcasted_iota(jnp.int32, shape, dim)


def to(device):
    return dict(device_id=device, device_id_type=MESH)


def ranks(owner_ref):
    npts = owner_ref.shape[1]
    first_index = iota((npts, npts), 0)
    second_index = iota((npts, npts), 1)
    across = jnp.broadcast_to(owner_ref[...].astype(F32), (npts, npts))
    down = jnp.sum(jnp.where(first_index == second_index, across, 0.0), axis=1, keepdims=True)
    same = across == down
    rank_down = jnp.sum(
        jnp.where(same & (second_index < first_index), 1.0, 0.0), axis=1, keepdims=True
    )
    rank_across = jnp.sum(
        jnp.where(same & (first_index < second_index), 1.0, 0.0), axis=0, keepdims=True
    )
    return down.astype(jnp.int32), rank_down.astype(jnp.int32), rank_across


def points_kernel(owner_ref, cell_ref, val_ref, cond_ref, mine_ref, columns, sem):
    nb, _, plane = val_ref.shape
    brick = lax.axis_index("brick")
    _, _, rank_across = ranks(owner_ref)
    own = owner_ref[...] == brick
    cells = [
        jnp.sum(
            jnp.where(own & (rank_across == j), cell_ref[...].astype(F32), 0.0)
        ).astype(jnp.int32)
        for j in range(MOST)
    ]
    copies = []
    for j in range(MOST):
        slot_plane = jnp.where(cells[j] >= plane, 1, 0)
        column = cells[j] - slot_plane * plane
        start = pl.multiple_of(column // LANES * LANES, LANES)
        for s, psi in enumerate((val_ref, cond_ref)):
            copy = pltpu.make_async_copy(
                psi.at[:, :, pl.ds(start, LANES)], columns.at[2 * j + s], sem.at[j, s]
            )
            copy.start()
            copies.append((copy, j, s, slot_plane, lax.rem(column, LANES)))

    fold = jnp.where(iota((2 * nb, nb), 0) // 2 == iota((2 * nb, nb), 1), 1.0, 0.0).astype(BF16)
    half = nb // 2
    row = iota((BLOCK, LANES), 0)
    lane = iota((BLOCK, LANES), 1)
    wide_row = iota((BLOCK, 2 * nb), 0)
    point_plane = jnp.zeros((BLOCK, 2 * nb), jnp.int32)
    taken = jnp.zeros((BLOCK, 2 * nb), F32)
    for copy, j, s, slot_plane, at in copies:
        copy.wait()
        if s == 0:
            point_plane = jnp.where(lax.rem(wide_row, MOST) == j, slot_plane, point_plane)
        pick = (lax.rem(row, MOST) == j) & (row // (2 * MOST) == s) & (lane == at)
        taken = taken + lax.dot_general(
            jnp.where(pick, 1.0, 0.0).astype(BF16), columns[2 * j + s].reshape(2 * nb, LANES),
            (((1,), (1,)), ((), ())), preferred_element_type=F32,
        )
    keep = lax.rem(iota((BLOCK, 2 * nb), 1), 2) == point_plane
    taken = jnp.dot(jnp.where(keep, taken, 0.0).astype(BF16), fold, preferred_element_type=F32)
    mine = jnp.where(lax.rem(row // MOST, 2) == 0, taken[:, :half], taken[:, half:])
    mine_ref[...] = mine.astype(BF16)


def place_of(brick, nz):
    core = lax.rem(brick, CORES)
    y = lax.rem(brick // CORES, CHIPS_Y)
    z = brick // (CORES * CHIPS_Y)
    return z, y, core


def brick_of(z, y, core):
    return (z * CHIPS_Y + y) * CORES + core


def brick_off(brick, o, bricks):
    return lax.rem(brick + o + bricks, bricks)


def gather_kernel(
    nz, owner_ref, mine_ref, eps_ref, z_ref, coef_ref,
    g_buf, sel, spread, eps_all, eps_rows,
    zs, zr, ys, yr, cs, cr, es, er,
):
    brick = lax.axis_index("brick")
    bricks = nz * CHIPS_Y * CORES
    z, y, core = place_of(brick, nz)
    plane = eps_ref.shape[1]
    npts = owner_ref.shape[1]
    half = LANES
    nb = 2 * half
    groups = min(4, nz)
    per = nz // groups

    barrier = pltpu.get_barrier_semaphore()

    @pl.loop(1, nz)
    def _(dz):
        pl.semaphore_signal(barrier, 1, **to({"brick": brick_of(lax.rem(z + dz, nz), y, core)}))

    for dy in range(1, CHIPS_Y):
        pl.semaphore_signal(
            barrier, 1, **to({"brick": brick_of(z, lax.rem(y + dy, CHIPS_Y), core)})
        )
    pl.semaphore_signal(barrier, 1, **to({"brick": brick_of(z, y, 1 - core)}))
    for o in (-2, -1, 1, 2):
        pl.semaphore_signal(barrier, 1, **to({"brick": brick_off(brick, o, bricks)}))

    g_buf[core, y, z] = mine_ref[...]
    pl.semaphore_wait(barrier, nz - 1 + CHIPS_Y - 1 + 1 + 4)

    def z_copy(dz):
        return pltpu.make_async_remote_copy(
            src_ref=g_buf.at[core, y, z], dst_ref=g_buf.at[core, y, z],
            send_sem=zs.at[dz], recv_sem=zr.at[z],
            **to({"brick": brick_of(lax.rem(z + dz, nz), y, core)})
        )

    @pl.loop(1, nz)
    def _(dz):
        z_copy(dz).start()

    eps_copies = []
    for n, o in enumerate((-2, -1, 1, 2)):
        copy = pltpu.make_async_remote_copy(
            src_ref=eps_ref, dst_ref=eps_all.at[2 - o],
            send_sem=es.at[n], recv_sem=er.at[n], **to({"brick": brick_off(brick, o, bricks)})
        )
        copy.start()
        eps_copies.append(copy)

    owner_down, rank_down, _ = ranks(owner_ref)
    place = ((owner_down & 1) * CHIPS_Y + ((owner_down >> 1) & 3)) * nz + (owner_down >> 3)
    place = place * BLOCK + rank_down

    @pl.loop(0, sel.shape[1] // GROUP)
    def _(n):
        column = iota((npts, GROUP), 1) + n * GROUP
        for q in range(4):
            hit = column == place + q * MOST
            sel[pl.ds(q * npts, npts), pl.ds(pl.multiple_of(n * GROUP, GROUP), GROUP)] = (
                jnp.where(hit, 1.0, 0.0).astype(BF16)
            )

    for p in range(2):
        spread[p] = jnp.where(
            iota((nb, 2 * nb), 1) == 2 * iota((nb, 2 * nb), 0) + p, 1.0, 0.0
        ).astype(BF16)

    def y_copy(g, dy):
        part_of = g_buf.at[core, y, pl.ds(g * per, per)]
        return pltpu.make_async_remote_copy(
            src_ref=part_of, dst_ref=part_of, send_sem=ys.at[dy, g], recv_sem=yr.at[y, g],
            **to({"brick": brick_of(z, lax.rem(y + dy, CHIPS_Y), core)})
        )

    @pl.loop(0, groups)
    def _(g):
        @pl.loop(0, per)
        def _(i):
            source = g * per + i

            @pl.when(source != z)
            def _():
                block = g_buf.at[core, y, source]
                pltpu.make_async_remote_copy(
                    src_ref=block, dst_ref=block, send_sem=zs.at[0], recv_sem=zr.at[source],
                    **to({"brick": brick_of(source, y, core)})
                ).wait_recv()

        for dy in (2, 1, 3):
            y_copy(g, dy).start()

    for copy in eps_copies:
        copy.wait()
    for o in range(5):
        eps_rows[2 * o : 2 * o + 2, :] = eps_ref[...] if o == 2 else eps_all[o]
    here = eps_rows[1:9, :]
    xminus = 0.5 * (here + eps_rows[0:8, :])
    xplus = 0.5 * (here + eps_rows[2:10, :])
    depth = lax.rem(iota((8, plane), 1), NZ)
    above = depth < NZ - 1
    below = depth > 0
    yplus = 0.5 * (here + pltpu.roll(here, plane - NZ, 1))
    yminus = 0.5 * (here + pltpu.roll(here, NZ, 1))
    zplus = 0.5 * (here + jnp.where(above, pltpu.roll(here, plane - 1, 1), here))
    zminus = 0.5 * (here + jnp.where(below, pltpu.roll(here, 1, 1), here))
    scale = OMEGA / (xplus + xminus + yplus + yminus + zplus + zminus)
    faces = (
        xminus, xplus, yminus, yplus,
        jnp.where(below, zminus, 0.0), jnp.where(above, zplus, 0.0), FOURPI,
    )
    for n, face in enumerate(faces):
        coef_ref[n] = scale * face

    def core_copy(g):
        part_of = g_buf.at[core, :, pl.ds(g * per, per)]
        return pltpu.make_async_remote_copy(
            src_ref=part_of, dst_ref=part_of, send_sem=cs.at[g], recv_sem=cr.at[g],
            **to({"brick": brick_of(z, y, 1 - core)})
        )

    @pl.loop(0, groups)
    def _(g):
        @pl.loop(0, CHIPS_Y)
        def _(source):
            @pl.when(source != y)
            def _():
                block = g_buf.at[core, source, pl.ds(g * per, per)]
                pltpu.make_async_remote_copy(
                    src_ref=block, dst_ref=block, send_sem=ys.at[0, g], recv_sem=yr.at[source, g],
                    **to({"brick": brick_of(z, source, core)})
                ).wait_recv()

        core_copy(g).start()

    @pl.loop(0, groups)
    def _(g):
        block = g_buf.at[1 - core, :, pl.ds(g * per, per)]
        pltpu.make_async_remote_copy(
            src_ref=block, dst_ref=block, send_sem=cs.at[g], recv_sem=cr.at[g],
            **to({"brick": brick_of(z, y, 1 - core)})
        ).wait_recv()

    found = jnp.dot(
        sel[...], g_buf[...].reshape(sel.shape[1], LANES), preferred_element_type=F32
    ).astype(BF16)
    for s in range(2):
        for p in range(2):
            low = found[2 * s * npts : (2 * s + 1) * npts, :]
            high = found[(2 * s + 1) * npts : (2 * s + 2) * npts, :]
            z_ref[s, p * npts : (p + 1) * npts, :] = (
                jnp.dot(low, spread[p, :half, :], preferred_element_type=F32)
                + jnp.dot(high, spread[p, half:, :], preferred_element_type=F32)
            ).astype(BF16)

    @pl.loop(1, nz)
    def _(dz):
        z_copy(dz).wait_send()

    @pl.loop(0, groups)
    def _(g):
        for dy in range(1, CHIPS_Y):
            y_copy(g, dy).wait_send()
        core_copy(g).wait_send()


def sums_kernel(
    nz, nx, z_ref, coef_ref, val_ref, cond_ref, pair_ref, pot_ref,
    x_buf, coef, part, out_q, in_q, field, first, second, third, result,
    load_sem, xs, xr, hs, hr, out_sem,
):
    brick = lax.axis_index("brick")
    band = lax.axis_index("band")
    bricks = nz * CHIPS_Y * CORES
    nb8, _, _, plane = val_ref.shape
    nb = nb8 * 8
    npts = z_ref.shape[1] // 2
    fields = npts // nx
    chunks = fields // 8
    tiles = plane // LANES
    parts = plane // GROUP

    def band_off(o):
        return lax.rem(band + o, nx)

    loads = []
    for s, psi in enumerate((val_ref, cond_ref)):
        for i in range(8):
            copy = pltpu.make_async_copy(
                psi.at[:, i], x_buf.at[s, :, 2 * i : 2 * i + 2, :], load_sem.at[s, i]
            )
            copy.start()
            loads.append(copy)

    barrier = pltpu.get_barrier_semaphore()
    for dx in (1, 3):
        pl.semaphore_signal(barrier, 1, **to({"band": band_off(dx)}))
    for o in (-2, -1, 1, 2):
        pl.semaphore_signal(barrier, 1, **to({"brick": brick_off(brick, o, bricks)}))

    @pl.loop(0, 7)
    def _(n):
        rows = coef_ref[n]
        for e in range(8):
            coef[n, e] = jnp.broadcast_to(rows[e : e + 1, :], (8, plane))

    for copy in loads:
        copy.wait()

    @pl.loop(0, parts)
    def _(n):
        at = pl.ds(pl.multiple_of(n * GROUP, GROUP), GROUP)
        for s in range(2):
            got = jnp.dot(
                z_ref[s], x_buf[s, :, :, at].reshape(2 * nb, GROUP), preferred_element_type=F32
            )
            part[s, :, :, at] = got.reshape(2, npts, GROUP)

    pl.semaphore_wait(barrier, 6)

    code_lane = iota((16, LANES), 1)

    def pack(values_at, slot, k):
        codes = jnp.zeros((16, LANES), F32)
        for n in range(parts):
            at = slice(n * GROUP, (n + 1) * GROUP)
            values = values_at(n)
            most = jnp.max(jnp.abs(values), axis=1, keepdims=True)
            code = jnp.ceil(jnp.log2(jnp.maximum(most, 1e-30)) * CODE)
            codes = jnp.where(code_lane == n, code, codes)
            whole = jnp.round(values * (STEP * jnp.exp2(code * (-1.0 / CODE))))
            out_q[slot, k, :, at] = whole.astype(jnp.int32).astype(jnp.int16)
        out_q[slot, k, :, plane:] = codes.astype(jnp.int32).astype(jnp.int16)

    def unpacker(slot, k):
        scales = jnp.exp2(in_q[slot, k, :, plane:].astype(jnp.int32).astype(F32) * (1.0 / CODE))
        scales = scales * (1.0 / STEP)

        def values_at(n):
            got = in_q[slot, k, :, n * GROUP : (n + 1) * GROUP].astype(jnp.int32).astype(F32)
            return got * scales[:, n : n + 1]

        return values_at

    def held(target, p, k):
        start = pl.multiple_of(target * fields + k * 8, 8)

        def values_at(n):
            at = slice(n * GROUP, (n + 1) * GROUP)
            return jnp.concatenate(
                [part[0, p, pl.ds(start, 8), at], part[1, p, pl.ds(start, 8), at]], axis=0
            )

        return values_at

    up, down, across = band_off(1), band_off(3), band_off(2)
    heading = (up, down, up, down, up, down)

    def x_copy(k, slot):
        return pltpu.make_async_remote_copy(
            src_ref=out_q.at[slot, k], dst_ref=in_q.at[slot, k],
            send_sem=xs.at[slot, k], recv_sem=xr.at[slot, k], **to({"band": heading[slot]})
        )

    def join(k):
        for way in range(2):
            x_copy(k, way).wait_recv()
            mine_at, got_at = held(heading[way], way, k), unpacker(way, k)
            pack(lambda n: mine_at(n) + got_at(n), 4 + way, k)
            x_copy(k, 4 + way).start()

    @pl.loop(0, chunks)
    def _(k):
        for way in range(2):
            pack(held(across, way, k), way, k)
            x_copy(k, way).start()
        for way in range(2):
            pack(held(heading[way], 1 - way, k), 2 + way, k)
            x_copy(k, 2 + way).start()

        @pl.when(k > 0)
        def _():
            join(k - 1)

    join(chunks - 1)

    sides = ((-2, 3, 1, 7), (-1, 3, 2, 5), (1, 3, 2, 1), (2, 4, 1, 0))

    def h_copy(k, n):
        o, source, count, target = sides[n]
        return pltpu.make_async_remote_copy(
            src_ref=field.at[k, source : source + count],
            dst_ref=field.at[k, target : target + count],
            send_sem=hs.at[k, n], recv_sem=hr.at[k, n], **to({"brick": brick_off(brick, o, bricks)})
        )

    def out_copy(k, p, which):
        source = field.at[k, 3 + p] if which == 0 else result.at[k, p]
        target = (pair_ref, pot_ref)[which].at[pl.ds(pl.multiple_of(k * 8, 8), 8), p, :]
        return pltpu.make_async_copy(source, target, out_sem.at[k, p, which])

    def product(k):
        for p in range(2):
            x_copy(k, 3 - p).wait_recv()
            x_copy(k, 4 + p).wait_recv()
            parts_at = (held(band, p, k), unpacker(3 - p, k), unpacker(4 + p, k))
            for n in range(parts):
                total = sum(values_at(n) for values_at in parts_at)
                pair = total[:8, :] * total[8:, :]
                field[k, 3 + p, :, n * GROUP : (n + 1) * GROUP] = pair
            out_copy(k, p, 0).start()

    low_half = iota((8, LANES), 1) < NZ

    def sweep(k, source, target, e):
        tile_at = [pl.ds(t * LANES, LANES) for t in range(tiles)]
        swapped = [pltpu.roll(source[e, :, at], NZ, 1) for at in tile_at]
        for t, at in enumerate(tile_at):
            v = source[e, :, at]
            new = (1.0 - OMEGA) * v + first[e, :, at]
            new = new + coef[0, e, :, at] * source[e - 1, :, at]
            new = new + coef[1, e, :, at] * source[e + 1, :, at]
            before = swapped[(t - 1) % tiles]
            after = swapped[(t + 1) % tiles]
            new = new + coef[2, e, :, at] * jnp.where(low_half, before, swapped[t])
            new = new + coef[3, e, :, at] * jnp.where(low_half, swapped[t], after)
            new = new + coef[4, e, :, at] * pltpu.roll(v, 1, 1)
            new = new + coef[5, e, :, at] * pltpu.roll(v, LANES - 1, 1)
            target(e, at, new)

    def sweeps(k):
        for n in range(4):
            h_copy(k, n).wait_recv()

        @pl.loop(0, 8)
        def _(e):
            first[e] = coef[6, e, :, :] * field[k, e]

        def into(ref):
            def store(e, at, new):
                ref[e, :, at] = new
            return store

        def into_result(e, at, new):
            result[k, e - 3, :, at] = new

        pl.loop(1, 7)(lambda e: sweep(k, first, into(second), e))
        pl.loop(2, 6)(lambda e: sweep(k, second, into(third), e))
        pl.loop(3, 5)(lambda e: sweep(k, third, into_result, e))
        for p in range(2):
            out_copy(k, p, 1).start()

    @pl.loop(0, chunks)
    def _(k):
        product(k)
        for n in range(4):
            h_copy(k, n).start()

        @pl.when(k > 0)
        def _():
            sweeps(k - 1)

    sweeps(chunks - 1)

    @pl.loop(0, chunks)
    def _(k):
        for slot in range(6):
            x_copy(k, slot).wait_send()
        for n in range(4):
            h_copy(k, n).wait_send()
        for p in range(2):
            for which in range(2):
                out_copy(k, p, which).wait()


def local(bricks, nx, psi_val, psi_cond, dielectric, point_owner, point_cell):
    nb, _, plane = psi_val.shape
    npts = point_owner.shape[0]
    nz = bricks // (CHIPS_Y * CORES)
    groups = min(4, nz)
    fields = npts // nx
    chunks = fields // 8
    rows = bricks * BLOCK
    owner = point_owner.reshape(1, npts)

    vmem = pl.BlockSpec(memory_space=pltpu.VMEM)
    hbm = pl.BlockSpec(memory_space=pl.ANY)
    dma = pltpu.SemaphoreType.DMA
    mine = pl.pallas_call(
        points_kernel,
        out_shape=jax.ShapeDtypeStruct((BLOCK, LANES), BF16),
        in_specs=[vmem, vmem, hbm, hbm],
        out_specs=vmem,
        scratch_shapes=[pltpu.VMEM((2 * MOST + 1, nb, 2, LANES), BF16), dma((MOST, 2))],
        compiler_params=pltpu.CompilerParams(vmem_limit_bytes=58 << 20),
        name="points",
    )(owner, point_cell.reshape(1, npts), psi_val, psi_cond)
    weights, coef = pl.pallas_call(
        functools.partial(gather_kernel, nz),
        out_shape=[
            jax.ShapeDtypeStruct((2, 2 * npts, 2 * nb), BF16),
            jax.ShapeDtypeStruct((7, 8, plane), F32),
        ],
        in_specs=[vmem, vmem, vmem],
        out_specs=[vmem, vmem],
        scratch_shapes=[
            pltpu.VMEM((CORES, CHIPS_Y, nz, BLOCK, LANES), BF16),
            pltpu.VMEM((4 * npts, rows), BF16),
            pltpu.VMEM((2, nb, 2 * nb), BF16),
            pltpu.VMEM((5, 2, plane), F32),
            pltpu.VMEM((16, plane), F32),
            dma((nz,)), dma((nz,)),
            dma((CHIPS_Y, groups)), dma((CHIPS_Y, groups)),
            dma((groups,)), dma((groups,)),
            dma((4,)), dma((4,)),
        ],
        compiler_params=pltpu.CompilerParams(
            collective_id=0, has_side_effects=True, vmem_limit_bytes=24 << 20
        ),
        name="gather",
    )(owner, mine, dielectric)
    return pl.pallas_call(
        functools.partial(sums_kernel, nz, nx),
        out_shape=[jax.ShapeDtypeStruct((fields, 2, plane), F32)] * 2,
        in_specs=[vmem, vmem, hbm, hbm],
        out_specs=[hbm, hbm],
        scratch_shapes=[
            pltpu.VMEM((2, nb // 8, 16, plane), BF16),
            pltpu.VMEM((7, 8, 8, plane), F32),
            pltpu.VMEM((2, 2, npts, plane), F32),
            pltpu.VMEM((6, chunks, 16, plane + LANES), jnp.int16),
            pltpu.VMEM((6, chunks, 16, plane + LANES), jnp.int16),
            pltpu.VMEM((chunks, 8, 8, plane), F32),
            pltpu.VMEM((8, 8, plane), F32),
            pltpu.VMEM((8, 8, plane), F32),
            pltpu.VMEM((8, 8, plane), F32),
            pltpu.VMEM((chunks, 2, 8, plane), F32),
            dma((2, 8)),
            dma((6, chunks)), dma((6, chunks)),
            dma((chunks, 4)), dma((chunks, 4)),
            dma((chunks, 2, 2)),
        ],
        compiler_params=pltpu.CompilerParams(
            collective_id=1, has_side_effects=True, vmem_limit_bytes=40 << 20
        ),
        name="sums",
    )(
        weights, coef, psi_val.reshape(nb // 8, 8, 2, plane),
        psi_cond.reshape(nb // 8, 8, 2, plane),
    )


def solution(mesh):
    return jax.shard_map(
        functools.partial(local, mesh.shape["brick"], mesh.shape["band"]),
        mesh=mesh,
        in_specs=(P("band", "brick", None), P("band", "brick", None), P("brick", None), P(), P()),
        out_specs=(P("band", "brick", None), P("band", "brick", None)),
        check_vma=False,
    )
```

```python
import functools

import jax
import jax.numpy as jnp
from jax import lax
from jax.experimental import pallas as pl
from jax.experimental.pallas import tpu as pltpu
from jax.sharding import PartitionSpec as P

NZ = 64
FOURPI = 12.566370614359172
OMEGA = 0.8

CORES = 2
CHIPS_Y = 4
MOST = 4
BLOCK = 4 * MOST
GROUP = 512
LANES = 128
STEP = 32700.0
CODE = 128.0
MESH = pl.DeviceIdType.MESH
F32 = jnp.float32
BF16 = jnp.bfloat16


def iota(shape, dim):
    return lax.broadcasted_iota(jnp.int32, shape, dim)


def to(device):
    return dict(device_id=device, device_id_type=MESH)


def ranks(owners):
    npts = owners.shape[1]
    first_index = iota((npts, npts), 0)
    second_index = iota((npts, npts), 1)
    across = jnp.broadcast_to(owners.astype(F32), (npts, npts))
    down = jnp.sum(jnp.where(first_index == second_index, across, 0.0), axis=1, keepdims=True)
    same = across == down
    rank_down = jnp.sum(
        jnp.where(same & (second_index < first_index), 1.0, 0.0), axis=1, keepdims=True
    )
    rank_across = jnp.sum(
        jnp.where(same & (first_index < second_index), 1.0, 0.0), axis=0, keepdims=True
    )
    return down.astype(jnp.int32), rank_down.astype(jnp.int32), rank_across


def points_kernel(
    owner_ref, cell_ref, eps_ref, val_ref, cond_ref, table_ref, columns, sem
):
    nb, _, plane = val_ref.shape
    brick = lax.axis_index("brick")
    _, _, rank_across = ranks(owner_ref[...])
    own = owner_ref[...] == brick
    cells = [
        jnp.sum(
            jnp.where(own & (rank_across == j), cell_ref[...].astype(F32), 0.0)
        ).astype(jnp.int32)
        for j in range(MOST)
    ]
    copies = []
    for j in range(MOST):
        slot_plane = jnp.where(cells[j] >= plane, 1, 0)
        column = cells[j] - slot_plane * plane
        start = pl.multiple_of(column // LANES * LANES, LANES)
        for s, psi in enumerate((val_ref, cond_ref)):
            copy = pltpu.make_async_copy(
                psi.at[:, :, pl.ds(start, LANES)], columns.at[2 * j + s], sem.at[j, s]
            )
            copy.start()
            copies.append((copy, j, s, slot_plane, lax.rem(column, LANES)))

    table_ref[...] = jnp.zeros_like(table_ref)
    table_ref[0:2, :plane] = eps_ref[...]
    table_ref[2:3, : owner_ref.shape[1]] = owner_ref[...].astype(F32)

    fold = jnp.where(iota((2 * nb, nb), 0) // 2 == iota((2 * nb, nb), 1), 1.0, 0.0).astype(BF16)
    half = nb // 2
    row = iota((BLOCK, LANES), 0)
    lane = iota((BLOCK, LANES), 1)
    wide_row = iota((BLOCK, 2 * nb), 0)
    point_plane = jnp.zeros((BLOCK, 2 * nb), jnp.int32)
    taken = jnp.zeros((BLOCK, 2 * nb), F32)
    for copy, j, s, slot_plane, at in copies:
        copy.wait()
        if s == 0:
            point_plane = jnp.where(lax.rem(wide_row, MOST) == j, slot_plane, point_plane)
        pick = (lax.rem(row, MOST) == j) & (row // (2 * MOST) == s) & (lane == at)
        taken = taken + lax.dot_general(
            jnp.where(pick, 1.0, 0.0).astype(BF16), columns[2 * j + s].reshape(2 * nb, LANES),
            (((1,), (1,)), ((), ())), preferred_element_type=F32,
        )
    keep = lax.rem(iota((BLOCK, 2 * nb), 1), 2) == point_plane
    taken = jnp.dot(jnp.where(keep, taken, 0.0).astype(BF16), fold, preferred_element_type=F32)
    mine = jnp.where(lax.rem(row // MOST, 2) == 0, taken[:, :half], taken[:, half:])
    table_ref[:, plane : plane + LANES] = mine[:8, :]
    table_ref[:, plane + LANES :] = mine[8:, :]


def kernel(
    nz, nx,
    table_ref, val_ref, cond_ref,
    pair_ref, pot_ref,
    x_buf, g_buf, sel, found, spread, z_buf, part, out_q, in_q, eps_all, eps_rows, coef,
    field, first, second, third, result,
    load_sem, zs, zr, ys, yr, cs, cr, xs, xr, hs, hr, es, er, out_sem,
):
    brick = lax.axis_index("brick")
    band = lax.axis_index("band")
    bricks = nz * CHIPS_Y * CORES
    core = lax.rem(brick, CORES)
    y = lax.rem(brick // CORES, CHIPS_Y)
    z = brick // (CORES * CHIPS_Y)
    nb8, _, _, plane = val_ref.shape
    nb = nb8 * 8
    npts = part.shape[2]
    owners = table_ref[2:3, :npts]
    fields = npts // nx
    chunks = fields // 8
    groups = min(4, nz)
    per = nz // groups
    tiles = plane // LANES
    parts = plane // GROUP

    def brick_at(zz, yy, cc):
        return (zz * CHIPS_Y + yy) * CORES + cc

    def brick_off(o):
        return lax.rem(brick + o + bricks, bricks)

    def band_off(o):
        return lax.rem(band + o, nx)

    loads = []
    for s, psi in enumerate((val_ref, cond_ref)):
        for i in range(8):
            copy = pltpu.make_async_copy(
                psi.at[:, i], x_buf.at[s, :, 2 * i : 2 * i + 2, :], load_sem.at[s, i]
            )
            copy.start()
            loads.append(copy)

    barrier = pltpu.get_barrier_semaphore()

    @pl.loop(1, nz)
    def _(dz):
        pl.semaphore_signal(barrier, 1, **to({"brick": brick_at(lax.rem(z + dz, nz), y, core)}))

    for dy in (1, 3):
        pl.semaphore_signal(
            barrier, 1, **to({"brick": brick_at(z, lax.rem(y + dy, CHIPS_Y), core)})
        )
    pl.semaphore_signal(barrier, 1, **to({"brick": brick_at(z, y, 1 - core)}))
    for dx in (1, 3):
        pl.semaphore_signal(barrier, 1, **to({"band": band_off(dx)}))
    for o in (-2, -1, 1, 2):
        pl.semaphore_signal(barrier, 1, **to({"brick": brick_off(o)}))

    g_buf[core, y, z] = jnp.concatenate(
        [table_ref[:, plane : plane + LANES], table_ref[:, plane + LANES :]], axis=0
    ).astype(BF16)
    eps_all[2] = table_ref[0:2, :plane]
    pl.semaphore_wait(barrier, nz - 1 + 2 + 1 + 2 + 4)

    def z_copy(dz):
        return pltpu.make_async_remote_copy(
            src_ref=g_buf.at[core, y, z], dst_ref=g_buf.at[core, y, z],
            send_sem=zs.at[dz], recv_sem=zr.at[z],
            **to({"brick": brick_at(lax.rem(z + dz, nz), y, core)})
        )

    for dz in sorted(range(1, nz), key=lambda d: -min(d, nz - d)):
        z_copy(dz).start()

    eps_copies = []
    for n, o in enumerate((-2, -1, 1, 2)):
        copy = pltpu.make_async_remote_copy(
            src_ref=eps_all.at[2], dst_ref=eps_all.at[2 - o],
            send_sem=es.at[n], recv_sem=er.at[n], **to({"brick": brick_off(o)})
        )
        copy.start()
        eps_copies.append(copy)

    owner_down, rank_down, _ = ranks(owners)
    owner_z = owner_down >> 3
    group_down = jnp.zeros_like(owner_z)
    for g in range(1, groups):
        group_down = group_down + jnp.where(owner_z >= g * per, 1, 0)
    place = ((owner_down & 1) * groups + group_down) * CHIPS_Y + ((owner_down >> 1) & 3)
    place = (place * per + owner_z - group_down * per) * BLOCK + rank_down

    @pl.loop(0, sel.shape[1] // GROUP)
    def _(n):
        column = iota((npts, GROUP), 1) + n * GROUP
        for q in range(4):
            hit = column == place + q * MOST
            sel[pl.ds(q * npts, npts), pl.ds(pl.multiple_of(n * GROUP, GROUP), GROUP)] = (
                jnp.where(hit, 1.0, 0.0).astype(BF16)
            )

    for p in range(2):
        spread[:, 2 * nb * p : 2 * nb * (p + 1)] = jnp.where(
            iota((nb, 2 * nb), 1) == 2 * iota((nb, 2 * nb), 0) + p, 1.0, 0.0
        ).astype(BF16)

    y_up, y_down = lax.rem(y + 1, CHIPS_Y), lax.rem(y + 3, CHIPS_Y)

    def y_copy(g, way):
        odd = lax.rem(g, 2)
        source = y if way < 2 else jnp.where(odd == 1, y_up, y_down)
        target = (y_up, y_down, jnp.where(odd == 1, y_down, y_up))[way]
        part_of = g_buf.at[core, source, pl.ds(g * per, per)]
        return pltpu.make_async_remote_copy(
            src_ref=part_of, dst_ref=part_of, send_sem=ys.at[way, g], recv_sem=yr.at[source, g],
            **to({"brick": brick_at(z, target, core)})
        )

    def y_arrived(source, g):
        block = g_buf.at[core, source, pl.ds(g * per, per)]
        pltpu.make_async_remote_copy(
            src_ref=block, dst_ref=block, send_sem=ys.at[0, g], recv_sem=yr.at[source, g],
            **to({"brick": brick_at(z, source, core)})
        ).wait_recv()

    @pl.loop(0, groups)
    def _(g):
        @pl.loop(0, per)
        def _(i):
            source = g * per + i

            @pl.when(source != z)
            def _():
                block = g_buf.at[core, y, source]
                pltpu.make_async_remote_copy(
                    src_ref=block, dst_ref=block, send_sem=zs.at[0], recv_sem=zr.at[source],
                    **to({"brick": brick_at(source, y, core)})
                ).wait_recv()

        y_copy(g, 0).start()
        y_copy(g, 1).start()

    @pl.loop(0, groups)
    def _(g):
        y_arrived(jnp.where(lax.rem(g, 2) == 1, y_up, y_down), g)
        y_copy(g, 2).start()

    for copy in eps_copies:
        copy.wait()
    for o in range(5):
        eps_rows[2 * o : 2 * o + 2, :] = eps_all[o]
    here = eps_rows[1:9, :]
    xminus = 0.5 * (here + eps_rows[0:8, :])
    xplus = 0.5 * (here + eps_rows[2:10, :])
    depth = lax.rem(iota((8, plane), 1), NZ)
    above = depth < NZ - 1
    below = depth > 0
    yplus = 0.5 * (here + pltpu.roll(here, plane - NZ, 1))
    yminus = 0.5 * (here + pltpu.roll(here, NZ, 1))
    zplus = 0.5 * (here + jnp.where(above, pltpu.roll(here, plane - 1, 1), here))
    zminus = 0.5 * (here + jnp.where(below, pltpu.roll(here, 1, 1), here))
    scale = OMEGA / (xplus + xminus + yplus + yminus + zplus + zminus)
    faces = (
        xminus, xplus, yminus, yplus,
        jnp.where(below, zminus, 0.0), jnp.where(above, zplus, 0.0), FOURPI,
    )
    for n, face in enumerate(faces):
        scaled = scale * face
        for e in range(8):
            coef[n, e] = jnp.broadcast_to(scaled[e : e + 1, :], (8, plane))

    def core_copy(g):
        part_of = g_buf.at[core, :, pl.ds(g * per, per)]
        return pltpu.make_async_remote_copy(
            src_ref=part_of, dst_ref=part_of, send_sem=cs.at[g], recv_sem=cr.at[g],
            **to({"brick": brick_at(z, y, 1 - core)})
        )

    columns_of = CHIPS_Y * per * BLOCK

    def find(c, g):
        rows = g_buf[c, :, pl.ds(g * per, per)].reshape(columns_of, LANES)
        start = pl.multiple_of((c * groups + g) * columns_of, columns_of)
        return jnp.dot(sel[:, pl.ds(start, columns_of)], rows, preferred_element_type=F32)

    found[...] = jnp.zeros_like(found)

    @pl.loop(0, groups)
    def _(g):
        y_arrived(jnp.where(lax.rem(g, 2) == 1, y_down, y_up), g)
        y_arrived(lax.rem(y + 2, CHIPS_Y), g)
        core_copy(g).start()

    @pl.loop(0, groups)
    def _(g):
        found[...] += find(core, g)

    @pl.loop(0, groups)
    def _(g):
        block = g_buf.at[1 - core, :, pl.ds(g * per, per)]
        pltpu.make_async_remote_copy(
            src_ref=block, dst_ref=block, send_sem=cs.at[g], recv_sem=cr.at[g],
            **to({"brick": brick_at(z, y, 1 - core)})
        ).wait_recv()
        found[...] += find(1 - core, g)

    for copy in loads:
        copy.wait()

    for s in range(2):
        at_points = jnp.concatenate(
            [found[(2 * s + i) * npts : (2 * s + i + 1) * npts, :] for i in range(2)], axis=1
        ).astype(BF16)
        wide = jnp.dot(at_points, spread[...], preferred_element_type=F32).astype(BF16)
        for p in range(2):
            z_buf[s, p * npts : (p + 1) * npts, :] = wide[:, 2 * nb * p : 2 * nb * (p + 1)]

    @pl.loop(0, parts)
    def _(n):
        at = pl.ds(pl.multiple_of(n * GROUP, GROUP), GROUP)
        for s in range(2):
            got = jnp.dot(
                z_buf[s], x_buf[s, :, :, at].reshape(2 * nb, GROUP), preferred_element_type=F32
            )
            part[s, :, :, at] = got.reshape(2, npts, GROUP)

    code_lane = iota((16, LANES), 1)

    def pack(values_at, slot, k):
        codes = jnp.zeros((16, LANES), F32)
        for n in range(parts):
            at = slice(n * GROUP, (n + 1) * GROUP)
            values = values_at(n)
            most = jnp.max(jnp.abs(values), axis=1, keepdims=True)
            code = jnp.ceil(jnp.log2(jnp.maximum(most, 1e-30)) * CODE)
            codes = jnp.where(code_lane == n, code, codes)
            whole = jnp.round(values * (STEP * jnp.exp2(code * (-1.0 / CODE))))
            out_q[slot, k, :, at] = whole.astype(jnp.int32).astype(jnp.int16)
        out_q[slot, k, :, plane:] = codes.astype(jnp.int32).astype(jnp.int16)

    def unpacker(slot, k):
        scales = jnp.exp2(in_q[slot, k, :, plane:].astype(jnp.int32).astype(F32) * (1.0 / CODE))
        scales = scales * (1.0 / STEP)

        def values_at(n):
            got = in_q[slot, k, :, n * GROUP : (n + 1) * GROUP].astype(jnp.int32).astype(F32)
            return got * scales[:, n : n + 1]

        return values_at

    def held(target, p, k):
        start = pl.multiple_of(target * fields + k * 8, 8)

        def values_at(n):
            at = slice(n * GROUP, (n + 1) * GROUP)
            return jnp.concatenate(
                [part[0, p, pl.ds(start, 8), at], part[1, p, pl.ds(start, 8), at]], axis=0
            )

        return values_at

    up, down, across = band_off(1), band_off(3), band_off(2)
    heading = (up, down, up, down, up, down)

    def x_copy(k, slot):
        return pltpu.make_async_remote_copy(
            src_ref=out_q.at[slot, k], dst_ref=in_q.at[slot, k],
            send_sem=xs.at[slot, k], recv_sem=xr.at[slot, k], **to({"band": heading[slot]})
        )

    def join(k):
        for way in range(2):
            x_copy(k, way).wait_recv()
            mine_at, got_at = held(heading[way], way, k), unpacker(way, k)
            pack(lambda n: mine_at(n) + got_at(n), 4 + way, k)
            x_copy(k, 4 + way).start()

    def send(k):
        for way in range(2):
            pack(held(across, way, k), way, k)
            x_copy(k, way).start()
        for way in range(2):
            pack(held(heading[way], 1 - way, k), 2 + way, k)
            x_copy(k, 2 + way).start()

    sides = ((-2, 3, 1, 7), (-1, 3, 2, 5), (1, 3, 2, 1), (2, 4, 1, 0))

    def h_copy(k, n):
        o, source, count, target = sides[n]
        return pltpu.make_async_remote_copy(
            src_ref=field.at[k, source : source + count],
            dst_ref=field.at[k, target : target + count],
            send_sem=hs.at[k, n], recv_sem=hr.at[k, n], **to({"brick": brick_off(o)})
        )

    def out_copy(k, p, which):
        source = field.at[k, 3 + p] if which == 0 else result.at[k, p]
        target = (pair_ref, pot_ref)[which].at[pl.ds(pl.multiple_of(k * 8, 8), 8), p, :]
        return pltpu.make_async_copy(source, target, out_sem.at[k, p, which])

    def product(k):
        for p in range(2):
            x_copy(k, 3 - p).wait_recv()
            x_copy(k, 4 + p).wait_recv()
            parts_at = (held(band, p, k), unpacker(3 - p, k), unpacker(4 + p, k))
            for n in range(parts):
                total = sum(values_at(n) for values_at in parts_at)
                pair = total[:8, :] * total[8:, :]
                field[k, 3 + p, :, n * GROUP : (n + 1) * GROUP] = pair
            out_copy(k, p, 0).start()

    low_half = iota((8, LANES), 1) < NZ

    def sweep(k, source, target, e):
        tile_at = [pl.ds(t * LANES, LANES) for t in range(tiles)]
        swapped = [pltpu.roll(source[e, :, at], NZ, 1) for at in tile_at]
        for t, at in enumerate(tile_at):
            v = source[e, :, at]
            new = (1.0 - OMEGA) * v + first[e, :, at]
            new = new + coef[0, e, :, at] * source[e - 1, :, at]
            new = new + coef[1, e, :, at] * source[e + 1, :, at]
            before = swapped[(t - 1) % tiles]
            after = swapped[(t + 1) % tiles]
            new = new + coef[2, e, :, at] * jnp.where(low_half, before, swapped[t])
            new = new + coef[3, e, :, at] * jnp.where(low_half, swapped[t], after)
            new = new + coef[4, e, :, at] * pltpu.roll(v, 1, 1)
            new = new + coef[5, e, :, at] * pltpu.roll(v, LANES - 1, 1)
            target(e, at, new)

    def sweeps(k):
        for n in range(4):
            h_copy(k, n).wait_recv()

        @pl.loop(0, 8)
        def _(e):
            first[e] = coef[6, e] * field[k, e]

        def into(ref):
            def store(e, at, new):
                ref[e, :, at] = new
            return store

        def into_result(e, at, new):
            result[k, e - 3, :, at] = new

        pl.loop(1, 7)(lambda e: sweep(k, first, into(second), e))
        pl.loop(2, 6)(lambda e: sweep(k, second, into(third), e))
        pl.loop(3, 5)(lambda e: sweep(k, third, into_result, e))
        for p in range(2):
            out_copy(k, p, 1).start()

    @pl.loop(0, chunks + 3)
    def _(step):
        @pl.when(step < chunks)
        def _():
            send(step)

        @pl.when((step >= 1) & (step < chunks + 1))
        def _():
            join(step - 1)

        @pl.when((step >= 2) & (step < chunks + 2))
        def _():
            product(step - 2)
            for n in range(4):
                h_copy(step - 2, n).start()

        @pl.when(step >= 3)
        def _():
            sweeps(step - 3)

    @pl.loop(1, nz)
    def _(dz):
        z_copy(dz).wait_send()

    @pl.loop(0, groups)
    def _(g):
        for way in range(3):
            y_copy(g, way).wait_send()
        core_copy(g).wait_send()

    @pl.loop(0, chunks)
    def _(k):
        for slot in range(6):
            x_copy(k, slot).wait_send()
        for n in range(4):
            h_copy(k, n).wait_send()
        for p in range(2):
            for which in range(2):
                out_copy(k, p, which).wait()


def local(bricks, nx, psi_val, psi_cond, dielectric, point_owner, point_cell):
    nb, _, plane = psi_val.shape
    npts = point_owner.shape[0]
    nz = bricks // (CHIPS_Y * CORES)
    groups = min(4, nz)
    fields = npts // nx
    chunks = fields // 8
    rows = bricks * BLOCK

    vmem = pl.BlockSpec(memory_space=pltpu.VMEM)
    dma = pltpu.SemaphoreType.DMA
    hbm = pl.BlockSpec(memory_space=pl.ANY)
    table = pl.pallas_call(
        points_kernel,
        out_shape=jax.ShapeDtypeStruct((8, plane + 2 * LANES), F32),
        in_specs=[vmem, vmem, vmem, hbm, hbm],
        out_specs=vmem,
        scratch_shapes=[pltpu.VMEM((2 * MOST + 1, nb, 2, LANES), BF16), dma((MOST, 2))],
        compiler_params=pltpu.CompilerParams(vmem_limit_bytes=58 << 20),
        name="points",
    )(point_owner.reshape(1, npts), point_cell.reshape(1, npts), dielectric, psi_val, psi_cond)
    pair, potential = pl.pallas_call(
        functools.partial(kernel, nz, nx),
        out_shape=[jax.ShapeDtypeStruct((fields, 2, plane), F32)] * 2,
        in_specs=[
            vmem, hbm, hbm,
        ],
        out_specs=[pl.BlockSpec(memory_space=pl.ANY)] * 2,
        scratch_shapes=[
            pltpu.VMEM((2, nb // 8, 16, plane), BF16),
            pltpu.VMEM((CORES, CHIPS_Y, nz, BLOCK, LANES), BF16),
            pltpu.VMEM((4 * npts, rows), BF16),
            pltpu.VMEM((4 * npts, LANES), F32),
            pltpu.VMEM((nb, 4 * nb), BF16),
            pltpu.VMEM((2, 2 * npts, 2 * nb), BF16),
            pltpu.VMEM((2, 2, npts, plane), F32),
            pltpu.VMEM((6, chunks, 16, plane + LANES), jnp.int16),
            pltpu.VMEM((6, chunks, 16, plane + LANES), jnp.int16),
            pltpu.VMEM((5, 2, plane), F32),
            pltpu.VMEM((16, plane), F32),
            pltpu.VMEM((7, 8, 8, plane), F32),
            pltpu.VMEM((chunks, 8, 8, plane), F32),
            pltpu.VMEM((8, 8, plane), F32),
            pltpu.VMEM((8, 8, plane), F32),
            pltpu.VMEM((8, 8, plane), F32),
            pltpu.VMEM((chunks, 2, 8, plane), F32),
            dma((2, 8)),
            dma((nz,)), dma((nz,)),
            dma((CHIPS_Y, groups)), dma((CHIPS_Y, groups)),
            dma((groups,)), dma((groups,)),
            dma((6, chunks)), dma((6, chunks)),
            dma((chunks, 4)), dma((chunks, 4)),
            dma((4,)), dma((4,)),
            dma((chunks, 2, 2)),
        ],
        compiler_params=pltpu.CompilerParams(
            collective_id=0, has_side_effects=True, vmem_limit_bytes=52 << 20
        ),
        cost_estimate=pl.CostEstimate(
            flops=2 * 2 * 2 * npts * 2 * nb * plane,
            bytes_accessed=8 * nb * plane + 16 * fields * plane,
            transcendentals=0,
        ),
    )(
        table, psi_val.reshape(nb // 8, 8, 2, plane), psi_cond.reshape(nb // 8, 8, 2, plane),
    )
    return pair, potential


def solution(mesh):
    return jax.shard_map(
        functools.partial(local, mesh.shape["brick"], mesh.shape["band"]),
        mesh=mesh,
        in_specs=(P("band", "brick", None), P("band", "brick", None), P("brick", None), P(), P()),
        out_specs=(P("band", "brick", None), P("band", "brick", None)),
        check_vma=False,
    )
```

```python
import functools

import jax
import jax.numpy as jnp
from jax import lax
from jax.experimental import pallas as pl
from jax.experimental.pallas import tpu as pltpu
from jax.sharding import PartitionSpec as P

NZ = 64
FOURPI = 12.566370614359172
OMEGA = 0.8

CORES = 2
CHIPS_Y = 4
MOST = 4
BLOCK = 4 * MOST
GROUP = 512
LANES = 128
STEP = 32700.0
CODE = 128.0
MESH = pl.DeviceIdType.MESH
F32 = jnp.float32
BF16 = jnp.bfloat16


def iota(shape, dim):
    return lax.broadcasted_iota(jnp.int32, shape, dim)


def to(device):
    return dict(device_id=device, device_id_type=MESH)


def kernel(
    nz, nx,
    table_ref, val_ref, cond_ref,
    pair_ref, pot_ref,
    x_buf, g_buf, sel, found, spread, fold, z_buf, part, out_a, in_a, out_c, in_c,
    eps_all, eps_rows, coef, out_h, in_h, field, first, second, third, result,
    load_sem, zs, zr, ys, yr, cs, cr, xas, xar, xcs, xcr, hs, hr, es, er, out_sem,
):
    brick = lax.axis_index("brick")
    band = lax.axis_index("band")
    bricks = nz * CHIPS_Y * CORES
    core = lax.rem(brick, CORES)
    y = lax.rem(brick // CORES, CHIPS_Y)
    z = brick // (CORES * CHIPS_Y)
    nb8, _, _, plane = val_ref.shape
    nb = nb8 * 8
    npts = part.shape[2]
    owners, cells = table_ref[2:3, :npts], table_ref[3:4, :npts]
    fields = npts // nx
    chunks = fields // 8
    groups = min(4, nz)
    per = nz // groups
    tiles = plane // LANES
    parts = plane // GROUP

    def brick_at(zz, yy, cc):
        return (zz * CHIPS_Y + yy) * CORES + cc

    def brick_off(o):
        return lax.rem(brick + o + bricks, bricks)

    def band_off(o):
        return lax.rem(band + o, nx)

    barrier = pltpu.get_barrier_semaphore()

    @pl.loop(1, nz)
    def _(dz):
        pl.semaphore_signal(barrier, 1, **to({"brick": brick_at(lax.rem(z + dz, nz), y, core)}))

    for dy in (1, 3):
        pl.semaphore_signal(
            barrier, 1, **to({"brick": brick_at(z, lax.rem(y + dy, CHIPS_Y), core)})
        )
    pl.semaphore_signal(barrier, 1, **to({"brick": brick_at(z, y, 1 - core)}))
    for dx in (1, 3):
        pl.semaphore_signal(barrier, 1, **to({"band": band_off(dx)}))
    for o in (-2, -1, 1, 2):
        pl.semaphore_signal(barrier, 1, **to({"brick": brick_off(o)}))

    for s, psi in enumerate((val_ref, cond_ref)):
        for i in range(8):
            copy = pltpu.make_async_copy(
                psi.at[:, i], x_buf.at[s, :, 2 * i : 2 * i + 2, :], load_sem.at[s]
            )
            copy.start()

    first_index = iota((npts, npts), 0)
    second_index = iota((npts, npts), 1)
    owner_across = jnp.broadcast_to(owners, (npts, npts))
    owner_down = jnp.sum(
        jnp.where(first_index == second_index, owner_across, 0.0), axis=1, keepdims=True
    )
    same = owner_across == owner_down
    rank_down = jnp.sum(
        jnp.where(same & (second_index < first_index), 1.0, 0.0), axis=1, keepdims=True
    )
    rank_across = jnp.sum(
        jnp.where(same & (first_index < second_index), 1.0, 0.0), axis=0, keepdims=True
    )
    own = owners == brick.astype(F32)
    slot_of = lax.rem(iota((BLOCK, 1), 0), MOST)
    slot_cell = jnp.zeros((BLOCK, 1), F32)
    for j in range(MOST):
        cell = jnp.sum(
            jnp.where(own & (rank_across == j), cells, 0.0),
            axis=1, keepdims=True,
        )
        slot_cell = jnp.where(slot_of == j, cell, slot_cell)
    slot_cell = slot_cell.astype(jnp.int32)
    slot_plane = jnp.where(slot_cell >= plane, 1, 0)
    slot_column = slot_cell - slot_plane * plane
    owner_down = owner_down.astype(jnp.int32)
    away = lax.rem((owner_down >> 3) - z + nz, nz)
    position = jnp.where(away <= nz // 2, 2 * away - 1, 2 * (nz - away))
    position = jnp.where(away == 0, 0, position)
    group_down = jnp.zeros_like(position)
    for g in range(1, groups):
        group_down = group_down + jnp.where(position >= g * per, 1, 0)
    place = ((owner_down & 1) * groups + group_down) * CHIPS_Y + ((owner_down >> 1) & 3)
    place = (place * per + position - group_down * per) * BLOCK + rank_down.astype(jnp.int32)
    pl.semaphore_wait(barrier, nz - 1 + 2 + 1 + 2 + 4)

    for o in (-2, -1, 1, 2):
        copy = pltpu.make_async_remote_copy(
            src_ref=table_ref, dst_ref=eps_all.at[2 - o],
            send_sem=es, recv_sem=er, **to({"brick": brick_off(o)})
        )
        copy.start()

    fold[...] = jnp.where(iota((2 * nb, nb), 0) // 2 == iota((2 * nb, nb), 1), 1.0, 0.0).astype(BF16)

    half = nb // 2
    row = iota((BLOCK, LANES), 0)
    group_row = iota((BLOCK, GROUP), 0)

    taken = jnp.zeros((BLOCK, 2 * nb), F32)
    for s in range(2):
        pltpu.make_async_copy(x_buf.at[s], x_buf.at[s], load_sem.at[s]).wait()

        def take(n, taken):
            start = pl.multiple_of(n * GROUP, GROUP)
            pick = (iota((BLOCK, GROUP), 1) + start == slot_column) & (
                group_row // (2 * MOST) == s
            )
            return taken + lax.dot_general(
                jnp.where(pick, 1.0, 0.0).astype(BF16),
                x_buf[s, :, :, pl.ds(start, GROUP)].reshape(2 * nb, GROUP),
                (((1,), (1,)), ((), ())), preferred_element_type=F32,
            )

        taken = lax.fori_loop(0, parts, take, taken)
    keep = lax.rem(iota((BLOCK, 2 * nb), 1), 2) == slot_plane
    taken = jnp.dot(
        jnp.where(keep, taken, 0.0).astype(BF16), fold[...], preferred_element_type=F32
    )
    mine = jnp.where(lax.rem(row // MOST, 2) == 0, taken[:, :half], taken[:, half:])
    g_buf[core, y, 0] = mine.astype(BF16)

    def z_copy(i):
        away = (i + 1) // 2 if i % 2 else -(i // 2)
        return pltpu.make_async_remote_copy(
            src_ref=g_buf.at[core, y, 0], dst_ref=g_buf.at[core, y, i],
            send_sem=zs, recv_sem=zr.at[i // per],
            **to({"brick": brick_at(lax.rem(z - away + nz, nz), y, core)})
        )

    for i in range(1, nz):
        z_copy(i).start()

    @pl.loop(0, sel.shape[1] // GROUP)
    def _(n):
        column = iota((npts, GROUP), 1) + n * GROUP
        for q in range(4):
            hit = column == place + q * MOST
            sel[pl.ds(q * npts, npts), pl.ds(pl.multiple_of(n * GROUP, GROUP), GROUP)] = (
                jnp.where(hit, 1.0, 0.0).astype(BF16)
            )

    for p in range(2):
        spread[:, 2 * nb * p : 2 * nb * (p + 1)] = jnp.where(
            iota((nb, 2 * nb), 1) == 2 * iota((nb, 2 * nb), 0) + p, 1.0, 0.0
        ).astype(BF16)

    y_up, y_down = lax.rem(y + 1, CHIPS_Y), lax.rem(y + 3, CHIPS_Y)

    def y_copy(g, way):
        odd = g % 2
        source = y if way < 2 else (y_up if odd else y_down)
        target = (y_up, y_down, y_down if odd else y_up)[way]
        part_of = g_buf.at[core, source, pl.ds(g * per, per)]
        return pltpu.make_async_remote_copy(
            src_ref=part_of, dst_ref=part_of, send_sem=ys,
            recv_sem=yr.at[g, 0 if way == odd else 1],
            **to({"brick": brick_at(z, target, core)})
        )

    def y_arrived(g, n):
        block = g_buf.at[core, pl.ds(0, n + 1), pl.ds(g * per, per)]
        pltpu.make_async_remote_copy(
            src_ref=block, dst_ref=block, send_sem=ys, recv_sem=yr.at[g, n],
            **to({"brick": brick_at(z, y_up, core)})
        ).wait_recv()

    def core_copy(g):
        part_of = g_buf.at[core, :, pl.ds(g * per, per)]
        return pltpu.make_async_remote_copy(
            src_ref=part_of, dst_ref=part_of, send_sem=cs, recv_sem=cr.at[g],
            **to({"brick": brick_at(z, y, 1 - core)})
        )

    columns_of = CHIPS_Y * per * BLOCK

    def find(c, g):
        rows = g_buf[c, :, pl.ds(g * per, per)].reshape(columns_of, LANES)
        start = pl.multiple_of((c * groups + g) * columns_of, columns_of)
        return jnp.dot(sel[:, pl.ds(start, columns_of)], rows, preferred_element_type=F32)

    found[...] = jnp.zeros_like(found)
    for step in range(groups + 3):
        if step < groups:
            come = g_buf.at[core, y, pl.ds(max(1, step * per), per if step else per - 1)]
            pltpu.make_async_remote_copy(
                src_ref=come, dst_ref=come, send_sem=zs, recv_sem=zr.at[step],
                **to({"brick": brick_at(lax.rem(z + 1, nz), y, core)})
            ).wait_recv()
            y_copy(step, 0).start()
            y_copy(step, 1).start()
        if 1 <= step <= groups:
            g = step - 1
            y_arrived(g, 0)
            y_copy(g, 2).start()
        if 2 <= step <= groups + 1:
            g = step - 2
            y_arrived(g, 1)
            core_copy(g).start()
            found[...] += find(core, g)
        if step >= 3:
            g = step - 3
            block = g_buf.at[1 - core, :, pl.ds(g * per, per)]
            pltpu.make_async_remote_copy(
                src_ref=block, dst_ref=block, send_sem=cs, recv_sem=cr.at[g],
                **to({"brick": brick_at(z, y, 1 - core)})
            ).wait_recv()
            found[...] += find(1 - core, g)

    for s in range(2):
        at_points = jnp.concatenate(
            [found[(2 * s + i) * npts : (2 * s + i + 1) * npts, :] for i in range(2)], axis=1
        ).astype(BF16)
        wide = jnp.dot(at_points, spread[...], preferred_element_type=F32).astype(BF16)
        for p in range(2):
            z_buf[s, p * npts : (p + 1) * npts, :] = wide[:, 2 * nb * p : 2 * nb * (p + 1)]

    @pl.loop(0, parts)
    def _(n):
        at = pl.ds(pl.multiple_of(n * GROUP, GROUP), GROUP)
        for s in range(2):
            got = jnp.dot(
                z_buf[s], x_buf[s, :, :, at].reshape(2 * nb, GROUP), preferred_element_type=F32
            )
            part[s, :, :, at] = got.reshape(2, npts, GROUP)

    code_lane = iota((16, LANES), 1)

    def pack(values_at, target, count):
        codes = jnp.zeros((16, LANES), F32)
        for n in range(count):
            values = values_at(n)
            most = jnp.max(jnp.abs(values), axis=1, keepdims=True)
            code = jnp.ceil(jnp.log2(jnp.maximum(most, 1e-30)) * CODE)
            codes = jnp.where(code_lane == n, code, codes)
            whole = jnp.round(values * (STEP * jnp.exp2(code * (-1.0 / CODE))))
            target[:, n * GROUP : (n + 1) * GROUP] = whole.astype(jnp.int32).astype(jnp.int16)
        target[:, count * GROUP :] = codes.astype(jnp.int32).astype(jnp.int16)

    def unpacker(source, count):
        codes = source[:, count * GROUP :].astype(jnp.int32).astype(F32)
        scales = jnp.exp2(codes * (1.0 / CODE)) * (1.0 / STEP)

        def values_at(n):
            got = source[:, n * GROUP : (n + 1) * GROUP].astype(jnp.int32).astype(F32)
            return got * scales[:, n : n + 1]

        return values_at

    def held(target, p, k):
        start = pl.multiple_of(target * fields + k * 8, 8)

        def values_at(n):
            at = slice(n * GROUP, (n + 1) * GROUP)
            return jnp.concatenate(
                [part[0, p, pl.ds(start, 8), at], part[1, p, pl.ds(start, 8), at]], axis=0
            )

        return values_at

    up, down, across = band_off(1), band_off(3), band_off(2)
    heading = (up, down)

    def a_copy(k, way):
        return pltpu.make_async_remote_copy(
            src_ref=out_a.at[way, k], dst_ref=in_a.at[way, k],
            send_sem=xas, recv_sem=xar.at[k], **to({"band": heading[way]})
        )

    def c_copy(k, way):
        return pltpu.make_async_remote_copy(
            src_ref=out_c.at[way, k], dst_ref=in_c.at[way, k],
            send_sem=xcs, recv_sem=xcr.at[k], **to({"band": heading[way]})
        )

    def send(k):
        for way in range(2):
            passed, direct = held(across, way, k), held(heading[way], 1 - way, k)
            pack(
                lambda n: passed(n) if n < parts else direct(n - parts),
                out_a.at[way, k], 2 * parts,
            )
            a_copy(k, way).start()

    def join(k):
        both = in_a.at[:, k]
        pltpu.make_async_remote_copy(
            src_ref=both, dst_ref=both, send_sem=xas, recv_sem=xar.at[k], **to({"band": up})
        ).wait_recv()
        for way in range(2):
            mine_at, got_at = held(heading[way], way, k), unpacker(in_a.at[way, k], 2 * parts)
            pack(lambda n: mine_at(n) + got_at(n), out_c.at[way, k], parts)
            c_copy(k, way).start()

    sides = ((-2, 0, 1, 5), (-1, 0, 2, 3), (1, 0, 2, 1), (2, 1, 1, 0))

    def h_copy(k, n):
        o, source, count, target = sides[n]
        return pltpu.make_async_remote_copy(
            src_ref=out_h.at[k, source : source + count],
            dst_ref=in_h.at[k, target : target + count],
            send_sem=hs, recv_sem=hr.at[k], **to({"brick": brick_off(o)})
        )

    def out_copy(which, p, start, count):
        rows = pl.ds(start, count)
        return pltpu.make_async_copy(
            (field, result)[which].at[p, rows], (pair_ref, pot_ref)[which].at[rows, p, :],
            out_sem.at[which],
        )

    def product(k):
        both = in_c.at[:, k]
        pltpu.make_async_remote_copy(
            src_ref=both, dst_ref=both, send_sem=xcs, recv_sem=xcr.at[k], **to({"band": up})
        ).wait_recv()
        rows = pl.ds(pl.multiple_of(k * 8, 8), 8)
        for p in range(2):
            direct = unpacker(in_a.at[1 - p, k], 2 * parts)
            parts_at = (
                held(band, p, k), lambda n: direct(n + parts), unpacker(in_c.at[p, k], parts)
            )
            for n in range(parts):
                total = sum(values_at(n) for values_at in parts_at)
                pair = total[:8, :] * total[8:, :]
                field[p, rows, n * GROUP : (n + 1) * GROUP] = pair

            def halves(n):
                return jnp.concatenate(
                    [
                        field[p, rows, m * GROUP : (m + 1) * GROUP]
                        for m in (n, n + parts // 2)
                    ],
                    axis=0,
                )

            pack(halves, out_h.at[k, p], parts // 2)

        @pl.when(k == chunks - 1)
        def _():
            for p in range(2):
                out_copy(0, p, 0, fields).start()

    low_half = iota((8, LANES), 1) < NZ

    def sweep(k, source, target, e):
        tile_at = [pl.ds(t * LANES, LANES) for t in range(tiles)]
        swapped = [pltpu.roll(source[e, :, at], NZ, 1) for at in tile_at]
        for t, at in enumerate(tile_at):
            v = source[e, :, at]
            new = (1.0 - OMEGA) * v + first[e, :, at]
            new = new + coef[0, e, :, at] * source[e - 1, :, at]
            new = new + coef[1, e, :, at] * source[e + 1, :, at]
            before = swapped[(t - 1) % tiles]
            after = swapped[(t + 1) % tiles]
            new = new + coef[2, e, :, at] * jnp.where(low_half, before, swapped[t])
            new = new + coef[3, e, :, at] * jnp.where(low_half, swapped[t], after)
            new = new + coef[4, e, :, at] * pltpu.roll(v, 1, 1)
            new = new + coef[5, e, :, at] * pltpu.roll(v, LANES - 1, 1)
            target(e, at, new)

    def sweeps(k):
        come = in_h.at[k]
        pltpu.make_async_remote_copy(
            src_ref=come, dst_ref=come, send_sem=hs, recv_sem=hr.at[k],
            **to({"brick": brick_off(1)})
        ).wait_recv()
        rows = pl.ds(pl.multiple_of(k * 8, 8), 8)
        for p in range(2):
            first[3 + p] = coef[6, 3 + p] * field[p, rows, :]

        @pl.loop(0, 6)
        def _(i):
            e = i + 2 * (i // 3)
            halves = unpacker(in_h.at[k, i], parts // 2)
            for n in range(parts // 2):
                values = halves(n)
                for m in range(2):
                    at = slice((n + m * parts // 2) * GROUP, (n + m * parts // 2 + 1) * GROUP)
                    first[e, :, at] = coef[6, e, :, at] * values[8 * m : 8 * m + 8, :]

        def into(ref):
            def store(e, at, new):
                ref[e, :, at] = new
            return store

        def into_result(e, at, new):
            result[e - 3, rows, at] = new

        pl.loop(1, 7)(lambda e: sweep(k, first, into(second), e))
        pl.loop(2, 6)(lambda e: sweep(k, second, into(third), e))
        pl.loop(3, 5)(lambda e: sweep(k, third, into_result, e))
        last = 8 * (chunks - 1)

        @pl.when(k == chunks - 2)
        def _():
            for p in range(2):
                out_copy(1, p, 0, last).start()

        @pl.when(k == chunks - 1)
        def _():
            for p in range(2):
                out_copy(1, p, last, 8).start()

    def coefficients():
        pltpu.make_async_remote_copy(
            src_ref=eps_all.at[0:4], dst_ref=eps_all.at[0:4], send_sem=es, recv_sem=er,
            **to({"brick": brick_off(1)})
        ).wait()
        for o in range(5):
            eps_rows[2 * o : 2 * o + 2, :] = table_ref[:2, :] if o == 2 else eps_all[o, :2, :]
        here = eps_rows[1:9, :]
        xminus = 0.5 * (here + eps_rows[0:8, :])
        xplus = 0.5 * (here + eps_rows[2:10, :])
        depth = lax.rem(iota((8, plane), 1), NZ)
        above = depth < NZ - 1
        below = depth > 0
        yplus = 0.5 * (here + pltpu.roll(here, plane - NZ, 1))
        yminus = 0.5 * (here + pltpu.roll(here, NZ, 1))
        zplus = 0.5 * (here + jnp.where(above, pltpu.roll(here, plane - 1, 1), here))
        zminus = 0.5 * (here + jnp.where(below, pltpu.roll(here, 1, 1), here))
        scale = OMEGA / (xplus + xminus + yplus + yminus + zplus + zminus)
        faces = (
            xminus, xplus, yminus, yplus,
            jnp.where(below, zminus, 0.0), jnp.where(above, zplus, 0.0), FOURPI,
        )
        for n, face in enumerate(faces):
            scaled = scale * face
            for e in range(8):
                coef[n, e] = jnp.broadcast_to(scaled[e : e + 1, :], (8, plane))

    @pl.loop(0, chunks + 3)
    def _(step):
        @pl.when(step < chunks)
        def _():
            send(step)

        @pl.when((step >= 1) & (step < chunks + 1))
        def _():
            join(step - 1)

        @pl.when(step == 2)
        def _():
            coefficients()

        @pl.when((step >= 2) & (step < chunks + 2))
        def _():
            product(step - 2)
            for n in range(4):
                h_copy(step - 2, n).start()

        @pl.when(step >= 3)
        def _():
            sweeps(step - 3)

    def sent(ref, sem, recv_sem):
        pltpu.make_async_remote_copy(
            src_ref=ref, dst_ref=ref, send_sem=sem, recv_sem=recv_sem,
            **to({"brick": brick_off(1)})
        ).wait_send()

    sent(g_buf.at[core, y, pl.ds(1, nz - 1)], zs, zr.at[0])
    sent(g_buf.at[core, pl.ds(0, 3)], ys, yr.at[0, 0])
    sent(g_buf.at[core], cs, cr.at[0])
    sent(out_a, xas, xar.at[0])
    sent(out_c, xcs, xcr.at[0])
    sent(in_h, hs, hr.at[0])
    for which, ref in enumerate((field, result)):
        pltpu.make_async_copy(ref, ref, out_sem.at[which]).wait()


def local(bricks, nx, psi_val, psi_cond, dielectric, point_owner, point_cell):
    nb, _, plane = psi_val.shape
    npts = point_owner.shape[0]
    nz = bricks // (CHIPS_Y * CORES)
    groups = min(4, nz)
    fields = npts // nx
    chunks = fields // 8
    rows = bricks * BLOCK

    def row(values):
        return jnp.pad(values[None, :], ((0, 0), (0, plane - npts))).astype(F32)

    table = jnp.concatenate([dielectric, row(point_owner), row(point_cell)], axis=0)

    vmem = pl.BlockSpec(memory_space=pltpu.VMEM)
    dma = pltpu.SemaphoreType.DMA
    pair, potential = pl.pallas_call(
        functools.partial(kernel, nz, nx),
        out_shape=[jax.ShapeDtypeStruct((fields, 2, plane), F32)] * 2,
        in_specs=[
            vmem, pl.BlockSpec(memory_space=pl.ANY), pl.BlockSpec(memory_space=pl.ANY),
        ],
        out_specs=[pl.BlockSpec(memory_space=pl.ANY)] * 2,
        scratch_shapes=[
            pltpu.VMEM((2, nb // 8, 16, plane), BF16),
            pltpu.VMEM((CORES, CHIPS_Y, nz, BLOCK, LANES), BF16),
            pltpu.VMEM((4 * npts, rows), BF16),
            pltpu.VMEM((4 * npts, LANES), F32),
            pltpu.VMEM((nb, 4 * nb), BF16),
            pltpu.VMEM((2 * nb, nb), BF16),
            pltpu.VMEM((2, 2 * npts, 2 * nb), BF16),
            pltpu.VMEM((2, 2, npts, plane), F32),
            pltpu.VMEM((2, chunks, 16, 2 * plane + LANES), jnp.int16),
            pltpu.VMEM((2, chunks, 16, 2 * plane + LANES), jnp.int16),
            pltpu.VMEM((2, chunks, 16, plane + LANES), jnp.int16),
            pltpu.VMEM((2, chunks, 16, plane + LANES), jnp.int16),
            pltpu.VMEM((5, 4, plane), F32),
            pltpu.VMEM((16, plane), F32),
            pltpu.VMEM((7, 8, 8, plane), F32),
            pltpu.VMEM((chunks, 2, 16, plane // 2 + LANES), jnp.int16),
            pltpu.VMEM((chunks, 6, 16, plane // 2 + LANES), jnp.int16),
            pltpu.VMEM((2, fields, plane), F32),
            pltpu.VMEM((8, 8, plane), F32),
            pltpu.VMEM((8, 8, plane), F32),
            pltpu.VMEM((8, 8, plane), F32),
            pltpu.VMEM((2, fields, plane), F32),
            dma((2,)),
            dma, dma((groups,)),
            dma, dma((groups, 2)),
            dma, dma((groups,)),
            dma, dma((chunks,)),
            dma, dma((chunks,)),
            dma, dma((chunks,)),
            dma, dma,
            dma((2,)),
        ],
        compiler_params=pltpu.CompilerParams(
            collective_id=0, has_side_effects=True, vmem_limit_bytes=52 << 20
        ),
        cost_estimate=pl.CostEstimate(
            flops=2 * 2 * 2 * npts * 2 * nb * plane,
            bytes_accessed=8 * nb * plane + 16 * fields * plane,
            transcendentals=0,
        ),
    )(
        table, psi_val.reshape(nb // 8, 8, 2, plane), psi_cond.reshape(nb // 8, 8, 2, plane),
    )
    return pair, potential


def solution(mesh):
    return jax.shard_map(
        functools.partial(local, mesh.shape["brick"], mesh.shape["band"]),
        mesh=mesh,
        in_specs=(P("band", "brick", None), P("band", "brick", None), P("brick", None), P(), P()),
        out_specs=(P("band", "brick", None), P("band", "brick", None)),
        check_vma=False,
    )
```

```python
import functools

import jax
import jax.numpy as jnp
from jax import lax
from jax.experimental import pallas as pl
from jax.experimental.pallas import tpu as pltpu
from jax.sharding import PartitionSpec as P

NZ = 64
FOURPI = 12.566370614359172
OMEGA = 0.8

CORES = 2
CHIPS_Y = 4
MOST = 4
BLOCK = 4 * MOST
GROUP = 512
LANES = 128
STEP = 32700.0
CODE = 128.0
MESH = pl.DeviceIdType.MESH
F32 = jnp.float32
BF16 = jnp.bfloat16


def iota(shape, dim):
    return lax.broadcasted_iota(jnp.int32, shape, dim)


def to(device):
    return dict(device_id=device, device_id_type=MESH)


def kernel(
    nz, nx,
    table_ref, val_ref, cond_ref,
    pair_ref, pot_ref,
    x_buf, g_buf, sel, found, spread, fold, z_buf, part, out_a, in_a, out_c, in_c,
    eps_all, eps_rows, coef, out_h, in_h, field, first, second, third, result,
    load_sem, zs, zr, ys, yr, cs, cr, xas, xar, xcs, xcr, hs, hr, es, er, out_sem,
):
    brick = lax.axis_index("brick")
    band = lax.axis_index("band")
    bricks = nz * CHIPS_Y * CORES
    core = lax.rem(brick, CORES)
    y = lax.rem(brick // CORES, CHIPS_Y)
    z = brick // (CORES * CHIPS_Y)
    nb8, _, _, plane = val_ref.shape
    nb = nb8 * 8
    npts = part.shape[2]
    owners, cells = table_ref[2:3, :npts], table_ref[3:4, :npts]
    fields = npts // nx
    chunks = fields // 8
    groups = min(4, nz)
    per = nz // groups
    tiles = plane // LANES
    parts = plane // GROUP

    def brick_at(zz, yy, cc):
        return (zz * CHIPS_Y + yy) * CORES + cc

    def brick_off(o):
        return lax.rem(brick + o + bricks, bricks)

    def band_off(o):
        return lax.rem(band + o, nx)

    barrier = pltpu.get_barrier_semaphore()

    @pl.loop(1, nz)
    def _(dz):
        pl.semaphore_signal(barrier, 1, **to({"brick": brick_at(lax.rem(z + dz, nz), y, core)}))

    for dy in (1, 3):
        pl.semaphore_signal(
            barrier, 1, **to({"brick": brick_at(z, lax.rem(y + dy, CHIPS_Y), core)})
        )
    pl.semaphore_signal(barrier, 1, **to({"brick": brick_at(z, y, 1 - core)}))
    for dx in (1, 3):
        pl.semaphore_signal(barrier, 1, **to({"band": band_off(dx)}))
    for o in (-2, -1, 1, 2):
        pl.semaphore_signal(barrier, 1, **to({"brick": brick_off(o)}))

    for s, psi in enumerate((val_ref, cond_ref)):
        for i in range(8):
            copy = pltpu.make_async_copy(
                psi.at[:, i], x_buf.at[s, :, 2 * i : 2 * i + 2, :], load_sem.at[s]
            )
            copy.start()

    first_index = iota((npts, npts), 0)
    second_index = iota((npts, npts), 1)
    owner_across = jnp.broadcast_to(owners, (npts, npts))
    owner_down = jnp.sum(
        jnp.where(first_index == second_index, owner_across, 0.0), axis=1, keepdims=True
    )
    same = owner_across == owner_down
    rank_down = jnp.sum(
        jnp.where(same & (second_index < first_index), 1.0, 0.0), axis=1, keepdims=True
    )
    rank_across = jnp.sum(
        jnp.where(same & (first_index < second_index), 1.0, 0.0), axis=0, keepdims=True
    )
    own = owners == brick.astype(F32)
    slot_of = iota((BLOCK, 1), 0) & (MOST - 1)
    slot_cell = jnp.zeros((BLOCK, 1), F32)
    for j in range(MOST):
        cell = jnp.sum(
            jnp.where(own & (rank_across == j), cells, 0.0),
            axis=1, keepdims=True,
        )
        slot_cell = jnp.where(slot_of == j, cell, slot_cell)
    slot_cell = slot_cell.astype(jnp.int32)
    slot_plane = jnp.where(slot_cell >= plane, 1, 0)
    slot_column = slot_cell - slot_plane * plane
    owner_down = owner_down.astype(jnp.int32)
    away = (owner_down >> 3) - z
    away = jnp.where(away < 0, away + nz, away)
    position = jnp.where(away <= nz // 2, 2 * away - 1, 2 * (nz - away))
    position = jnp.where(away == 0, 0, position)
    group_down = jnp.zeros_like(position)
    for g in range(1, groups):
        group_down = group_down + jnp.where(position >= g * per, 1, 0)
    place = ((owner_down & 1) * groups + group_down) * CHIPS_Y + ((owner_down >> 1) & 3)
    place = (place * per + position - group_down * per) * BLOCK + rank_down.astype(jnp.int32)
    pl.semaphore_wait(barrier, nz - 1 + 2 + 1 + 2 + 4)

    for o in (-2, -1, 1, 2):
        copy = pltpu.make_async_remote_copy(
            src_ref=table_ref, dst_ref=eps_all.at[2 - o],
            send_sem=es, recv_sem=er, **to({"brick": brick_off(o)})
        )
        copy.start()

    fold[...] = jnp.where((iota((2 * nb, nb), 0) >> 1) == iota((2 * nb, nb), 1), 1.0, 0.0).astype(BF16)

    half = nb // 2
    row = iota((BLOCK, LANES), 0)
    group_row = iota((BLOCK, GROUP), 0)

    taken = jnp.zeros((BLOCK, 2 * nb), F32)
    for s in range(2):
        pltpu.make_async_copy(x_buf.at[s], x_buf.at[s], load_sem.at[s]).wait()

        def take(n, taken):
            start = pl.multiple_of(n * GROUP, GROUP)
            pick = (iota((BLOCK, GROUP), 1) + start == slot_column) & (
                (group_row >> 3) == s
            )
            return taken + lax.dot_general(
                jnp.where(pick, 1.0, 0.0).astype(BF16),
                x_buf[s, :, :, pl.ds(start, GROUP)].reshape(2 * nb, GROUP),
                (((1,), (1,)), ((), ())), preferred_element_type=F32,
            )

        taken = lax.fori_loop(0, parts, take, taken)
    keep = (iota((BLOCK, 2 * nb), 1) & 1) == slot_plane
    taken = jnp.dot(
        jnp.where(keep, taken, 0.0).astype(BF16), fold[...], preferred_element_type=F32
    )
    mine = jnp.where(((row >> 2) & 1) == 0, taken[:, :half], taken[:, half:])
    g_buf[core, y, 0] = mine.astype(BF16)

    def z_copy(i):
        away = (i + 1) // 2 if i % 2 else -(i // 2)
        return pltpu.make_async_remote_copy(
            src_ref=g_buf.at[core, y, 0], dst_ref=g_buf.at[core, y, i],
            send_sem=zs, recv_sem=zr.at[i // per],
            **to({"brick": brick_at(lax.rem(z - away + nz, nz), y, core)})
        )

    for i in range(1, nz):
        z_copy(i).start()

    @pl.loop(0, sel.shape[1] // GROUP)
    def _(n):
        column = iota((npts, GROUP), 1) + n * GROUP
        for q in range(4):
            hit = column == place + q * MOST
            sel[pl.ds(q * npts, npts), pl.ds(pl.multiple_of(n * GROUP, GROUP), GROUP)] = (
                jnp.where(hit, 1.0, 0.0).astype(BF16)
            )

    for p in range(2):
        spread[:, 2 * nb * p : 2 * nb * (p + 1)] = jnp.where(
            iota((nb, 2 * nb), 1) == 2 * iota((nb, 2 * nb), 0) + p, 1.0, 0.0
        ).astype(BF16)

    y_up, y_down = lax.rem(y + 1, CHIPS_Y), lax.rem(y + 3, CHIPS_Y)

    def y_copy(g, way):
        odd = g % 2
        source = y if way < 2 else (y_up if odd else y_down)
        target = (y_up, y_down, y_down if odd else y_up)[way]
        part_of = g_buf.at[core, source, pl.ds(g * per, per)]
        return pltpu.make_async_remote_copy(
            src_ref=part_of, dst_ref=part_of, send_sem=ys,
            recv_sem=yr.at[g, 0 if way == odd else 1],
            **to({"brick": brick_at(z, target, core)})
        )

    def y_arrived(g, n):
        block = g_buf.at[core, pl.ds(0, n + 1), pl.ds(g * per, per)]
        pltpu.make_async_remote_copy(
            src_ref=block, dst_ref=block, send_sem=ys, recv_sem=yr.at[g, n],
            **to({"brick": brick_at(z, y_up, core)})
        ).wait_recv()

    def core_copy(g):
        part_of = g_buf.at[core, :, pl.ds(g * per, per)]
        return pltpu.make_async_remote_copy(
            src_ref=part_of, dst_ref=part_of, send_sem=cs, recv_sem=cr.at[g],
            **to({"brick": brick_at(z, y, 1 - core)})
        )

    columns_of = CHIPS_Y * per * BLOCK

    def find(c, g):
        rows = g_buf[c, :, pl.ds(g * per, per)].reshape(columns_of, LANES)
        start = pl.multiple_of((c * groups + g) * columns_of, columns_of)
        return jnp.dot(sel[:, pl.ds(start, columns_of)], rows, preferred_element_type=F32)

    found[...] = jnp.zeros_like(found)
    for step in range(groups + 3):
        if step < groups:
            come = g_buf.at[core, y, pl.ds(max(1, step * per), per if step else per - 1)]
            pltpu.make_async_remote_copy(
                src_ref=come, dst_ref=come, send_sem=zs, recv_sem=zr.at[step],
                **to({"brick": brick_at(lax.rem(z + 1, nz), y, core)})
            ).wait_recv()
            y_copy(step, 0).start()
            y_copy(step, 1).start()
        if 1 <= step <= groups:
            g = step - 1
            y_arrived(g, 0)
            y_copy(g, 2).start()
        if 2 <= step <= groups + 1:
            g = step - 2
            y_arrived(g, 1)
            core_copy(g).start()
            found[...] += find(core, g)
        if step >= 3:
            g = step - 3
            block = g_buf.at[1 - core, :, pl.ds(g * per, per)]
            pltpu.make_async_remote_copy(
                src_ref=block, dst_ref=block, send_sem=cs, recv_sem=cr.at[g],
                **to({"brick": brick_at(z, y, 1 - core)})
            ).wait_recv()
            found[...] += find(1 - core, g)

    for s in range(2):
        at_points = jnp.concatenate(
            [found[(2 * s + i) * npts : (2 * s + i + 1) * npts, :] for i in range(2)], axis=1
        ).astype(BF16)
        wide = jnp.dot(at_points, spread[...], preferred_element_type=F32).astype(BF16)
        for p in range(2):
            z_buf[s, p * npts : (p + 1) * npts, :] = wide[:, 2 * nb * p : 2 * nb * (p + 1)]

    @pl.loop(0, parts)
    def _(n):
        at = pl.ds(pl.multiple_of(n * GROUP, GROUP), GROUP)
        for s in range(2):
            got = jnp.dot(
                z_buf[s], x_buf[s, :, :, at].reshape(2 * nb, GROUP), preferred_element_type=F32
            )
            part[s, :, :, at] = got.reshape(2, npts, GROUP)

    code_lane = iota((16, LANES), 1)

    def pack(*messages):
        scales = []
        for values_at, target, count in messages:
            most = jnp.zeros((16, LANES), F32)
            for n in range(count):
                peak = jnp.max(jnp.abs(values_at(n)), axis=1, keepdims=True)
                most = jnp.where(code_lane == n, peak, most)
            code = jnp.ceil(jnp.log2(jnp.maximum(most, 1e-30)) * CODE)
            scales.append((code, STEP * jnp.exp2(code * (-1.0 / CODE))))
        for (values_at, target, count), (code, scale) in zip(messages, scales):
            target[:, count * GROUP :] = code.astype(jnp.int32).astype(jnp.int16)
            for n in range(count):
                whole = jnp.round(values_at(n) * scale[:, n : n + 1])
                target[:, n * GROUP : (n + 1) * GROUP] = whole.astype(jnp.int32).astype(jnp.int16)

    def unpacker(source, count):
        codes = source[:, count * GROUP :].astype(jnp.int32).astype(F32)
        scales = jnp.exp2(codes * (1.0 / CODE)) * (1.0 / STEP)

        def values_at(n):
            got = source[:, n * GROUP : (n + 1) * GROUP].astype(jnp.int32).astype(F32)
            return got * scales[:, n : n + 1]

        return values_at

    def held(target, p, k):
        start = pl.multiple_of(target * fields + k * 8, 8)

        def values_at(n):
            at = slice(n * GROUP, (n + 1) * GROUP)
            return jnp.concatenate(
                [part[0, p, pl.ds(start, 8), at], part[1, p, pl.ds(start, 8), at]], axis=0
            )

        return values_at

    up, down, across = band_off(1), band_off(3), band_off(2)
    heading = (up, down)

    def a_copy(k, way):
        return pltpu.make_async_remote_copy(
            src_ref=out_a.at[way, k], dst_ref=in_a.at[way, k],
            send_sem=xas, recv_sem=xar.at[k], **to({"band": heading[way]})
        )

    def c_copy(k, way):
        return pltpu.make_async_remote_copy(
            src_ref=out_c.at[way, k], dst_ref=in_c.at[way, k],
            send_sem=xcs, recv_sem=xcr.at[k], **to({"band": heading[way]})
        )

    def send(k):
        def message(way):
            passed, direct = held(across, way, k), held(heading[way], 1 - way, k)
            return (
                lambda n: passed(n) if n < parts else direct(n - parts),
                out_a.at[way, k], 2 * parts,
            )

        pack(message(0), message(1))
        for way in range(2):
            a_copy(k, way).start()

    def join(k):
        both = in_a.at[:, k]
        pltpu.make_async_remote_copy(
            src_ref=both, dst_ref=both, send_sem=xas, recv_sem=xar.at[k], **to({"band": up})
        ).wait_recv()
        def message(way):
            mine_at, got_at = held(heading[way], way, k), unpacker(in_a.at[way, k], 2 * parts)
            return lambda n: mine_at(n) + got_at(n), out_c.at[way, k], parts

        pack(message(0), message(1))
        for way in range(2):
            c_copy(k, way).start()

    sides = ((-2, 0, 1, 5), (-1, 0, 2, 3), (1, 0, 2, 1), (2, 1, 1, 0))

    def h_copy(k, n):
        o, source, count, target = sides[n]
        return pltpu.make_async_remote_copy(
            src_ref=out_h.at[k, source : source + count],
            dst_ref=in_h.at[k, target : target + count],
            send_sem=hs, recv_sem=hr.at[k], **to({"brick": brick_off(o)})
        )

    def out_copy(which, p, start, count):
        rows = pl.ds(start, count)
        return pltpu.make_async_copy(
            (field, result)[which].at[p, rows], (pair_ref, pot_ref)[which].at[rows, p, :],
            out_sem.at[which],
        )

    def product(k):
        both = in_c.at[:, k]
        pltpu.make_async_remote_copy(
            src_ref=both, dst_ref=both, send_sem=xcs, recv_sem=xcr.at[k], **to({"band": up})
        ).wait_recv()
        rows = pl.ds(pl.multiple_of(k * 8, 8), 8)
        for p in range(2):
            direct = unpacker(in_a.at[1 - p, k], 2 * parts)
            parts_at = (
                held(band, p, k), lambda n: direct(n + parts), unpacker(in_c.at[p, k], parts)
            )
            pairs = []
            for n in range(parts):
                total = sum(values_at(n) for values_at in parts_at)
                pairs.append(total[:8, :] * total[8:, :])
            for n in range(parts):
                field[p, rows, n * GROUP : (n + 1) * GROUP] = pairs[n]

        def message(p):
            def halves(n):
                return jnp.concatenate(
                    [
                        field[p, rows, m * GROUP : (m + 1) * GROUP]
                        for m in (n, n + parts // 2)
                    ],
                    axis=0,
                )

            return halves, out_h.at[k, p], parts // 2

        pack(message(0), message(1))

        @pl.when(k == chunks - 1)
        def _():
            for p in range(2):
                out_copy(0, p, 0, fields).start()

    low_half = iota((8, LANES), 1) < NZ

    def sweep(source, e):
        tile_at = [pl.ds(t * LANES, LANES) for t in range(tiles)]
        swapped = [pltpu.roll(source[e, :, at], NZ, 1) for at in tile_at]
        news = []
        for t, at in enumerate(tile_at):
            v = source[e, :, at]
            before = swapped[(t - 1) % tiles]
            after = swapped[(t + 1) % tiles]
            alone = (1.0 - OMEGA) * v + first[e, :, at]
            along_x = coef[0, e, :, at] * source[e - 1, :, at]
            along_x = along_x + coef[1, e, :, at] * source[e + 1, :, at]
            along_y = coef[2, e, :, at] * jnp.where(low_half, before, swapped[t])
            along_y = along_y + coef[3, e, :, at] * jnp.where(low_half, swapped[t], after)
            along_z = coef[4, e, :, at] * pltpu.roll(v, 1, 1)
            along_z = along_z + coef[5, e, :, at] * pltpu.roll(v, LANES - 1, 1)
            news.append((alone + along_x) + (along_y + along_z))
        return zip(tile_at, news)

    def sweeps(k):
        come = in_h.at[k]
        pltpu.make_async_remote_copy(
            src_ref=come, dst_ref=come, send_sem=hs, recv_sem=hr.at[k],
            **to({"brick": brick_off(1)})
        ).wait_recv()
        rows = pl.ds(pl.multiple_of(k * 8, 8), 8)
        for p in range(2):
            first[3 + p] = coef[6, 3 + p] * field[p, rows, :]

        @pl.loop(0, 6)
        def _(i):
            e = i + 2 * (i // 3)
            halves = unpacker(in_h.at[k, i], parts // 2)
            values = [halves(n) for n in range(parts // 2)]
            for m in range(parts):
                at = slice(m * GROUP, (m + 1) * GROUP)
                half = values[m % (parts // 2)][8 * (m // (parts // 2)) :, :][:8, :]
                first[e, :, at] = coef[6, e, :, at] * half

        @pl.loop(1, 7)
        def _(e):
            for at, new in sweep(first, e):
                second[e, :, at] = new

        @pl.loop(2, 6)
        def _(e):
            for at, new in sweep(second, e):
                third[e, :, at] = new

        @pl.loop(3, 5)
        def _(e):
            for at, new in sweep(third, e):
                result[e - 3, rows, at] = new

        last = 8 * (chunks - 1)

        @pl.when(k == chunks - 2)
        def _():
            for p in range(2):
                out_copy(1, p, 0, last).start()

        @pl.when(k == chunks - 1)
        def _():
            for p in range(2):
                out_copy(1, p, last, 8).start()

    def coefficients():
        pltpu.make_async_remote_copy(
            src_ref=eps_all.at[0:4], dst_ref=eps_all.at[0:4], send_sem=es, recv_sem=er,
            **to({"brick": brick_off(1)})
        ).wait()
        for o in range(5):
            eps_rows[2 * o : 2 * o + 2, :] = table_ref[:2, :] if o == 2 else eps_all[o, :2, :]
        here = eps_rows[1:9, :]
        xminus = 0.5 * (here + eps_rows[0:8, :])
        xplus = 0.5 * (here + eps_rows[2:10, :])
        depth = iota((8, plane), 1) & (NZ - 1)
        above = depth < NZ - 1
        below = depth > 0
        yplus = 0.5 * (here + pltpu.roll(here, plane - NZ, 1))
        yminus = 0.5 * (here + pltpu.roll(here, NZ, 1))
        zplus = 0.5 * (here + jnp.where(above, pltpu.roll(here, plane - 1, 1), here))
        zminus = 0.5 * (here + jnp.where(below, pltpu.roll(here, 1, 1), here))
        scale = OMEGA / (xplus + xminus + yplus + yminus + zplus + zminus)
        faces = (
            xminus, xplus, yminus, yplus,
            jnp.where(below, zminus, 0.0), jnp.where(above, zplus, 0.0), FOURPI,
        )
        for n, face in enumerate(faces):
            scaled = scale * face
            for e in range(8):
                coef[n, e] = jnp.broadcast_to(scaled[e : e + 1, :], (8, plane))

    @pl.loop(0, chunks + 3)
    def _(step):
        @pl.when(step < chunks)
        def _():
            send(step)

        @pl.when((step >= 1) & (step < chunks + 1))
        def _():
            join(step - 1)

        @pl.when(step == 2)
        def _():
            coefficients()

        @pl.when((step >= 2) & (step < chunks + 2))
        def _():
            product(step - 2)
            for n in range(4):
                h_copy(step - 2, n).start()

        @pl.when(step >= 3)
        def _():
            sweeps(step - 3)

    def sent(ref, sem, recv_sem):
        pltpu.make_async_remote_copy(
            src_ref=ref, dst_ref=ref, send_sem=sem, recv_sem=recv_sem,
            **to({"brick": brick_off(1)})
        ).wait_send()

    sent(g_buf.at[core, y, pl.ds(1, nz - 1)], zs, zr.at[0])
    sent(g_buf.at[core, pl.ds(0, 3)], ys, yr.at[0, 0])
    sent(g_buf.at[core], cs, cr.at[0])
    sent(out_a, xas, xar.at[0])
    sent(out_c, xcs, xcr.at[0])
    sent(in_h, hs, hr.at[0])
    for which, ref in enumerate((field, result)):
        pltpu.make_async_copy(ref, ref, out_sem.at[which]).wait()


def local(bricks, nx, psi_val, psi_cond, dielectric, point_owner, point_cell):
    nb, _, plane = psi_val.shape
    npts = point_owner.shape[0]
    nz = bricks // (CHIPS_Y * CORES)
    groups = min(4, nz)
    fields = npts // nx
    chunks = fields // 8
    rows = bricks * BLOCK

    def row(values):
        return jnp.pad(values[None, :], ((0, 0), (0, plane - npts))).astype(F32)

    table = jnp.concatenate([dielectric, row(point_owner), row(point_cell)], axis=0)

    vmem = pl.BlockSpec(memory_space=pltpu.VMEM)
    dma = pltpu.SemaphoreType.DMA
    pair, potential = pl.pallas_call(
        functools.partial(kernel, nz, nx),
        out_shape=[jax.ShapeDtypeStruct((fields, 2, plane), F32)] * 2,
        in_specs=[
            vmem, pl.BlockSpec(memory_space=pl.ANY), pl.BlockSpec(memory_space=pl.ANY),
        ],
        out_specs=[pl.BlockSpec(memory_space=pl.ANY)] * 2,
        scratch_shapes=[
            pltpu.VMEM((2, nb // 8, 16, plane), BF16),
            pltpu.VMEM((CORES, CHIPS_Y, nz, BLOCK, LANES), BF16),
            pltpu.VMEM((4 * npts, rows), BF16),
            pltpu.VMEM((4 * npts, LANES), F32),
            pltpu.VMEM((nb, 4 * nb), BF16),
            pltpu.VMEM((2 * nb, nb), BF16),
            pltpu.VMEM((2, 2 * npts, 2 * nb), BF16),
            pltpu.VMEM((2, 2, npts, plane), F32),
            pltpu.VMEM((2, chunks, 16, 2 * plane + LANES), jnp.int16),
            pltpu.VMEM((2, chunks, 16, 2 * plane + LANES), jnp.int16),
            pltpu.VMEM((2, chunks, 16, plane + LANES), jnp.int16),
            pltpu.VMEM((2, chunks, 16, plane + LANES), jnp.int16),
            pltpu.VMEM((5, 4, plane), F32),
            pltpu.VMEM((16, plane), F32),
            pltpu.VMEM((7, 8, 8, plane), F32),
            pltpu.VMEM((chunks, 2, 16, plane // 2 + LANES), jnp.int16),
            pltpu.VMEM((chunks, 6, 16, plane // 2 + LANES), jnp.int16),
            pltpu.VMEM((2, fields, plane), F32),
            pltpu.VMEM((8, 8, plane), F32),
            pltpu.VMEM((8, 8, plane), F32),
            pltpu.VMEM((8, 8, plane), F32),
            pltpu.VMEM((2, fields, plane), F32),
            dma((2,)),
            dma, dma((groups,)),
            dma, dma((groups, 2)),
            dma, dma((groups,)),
            dma, dma((chunks,)),
            dma, dma((chunks,)),
            dma, dma((chunks,)),
            dma, dma,
            dma((2,)),
        ],
        compiler_params=pltpu.CompilerParams(
            collective_id=0, has_side_effects=True, vmem_limit_bytes=52 << 20
        ),
        cost_estimate=pl.CostEstimate(
            flops=2 * 2 * 2 * npts * 2 * nb * plane,
            bytes_accessed=8 * nb * plane + 16 * fields * plane,
            transcendentals=0,
        ),
    )(
        table, psi_val.reshape(nb // 8, 8, 2, plane), psi_cond.reshape(nb // 8, 8, 2, plane),
    )
    return pair, potential


def solution(mesh):
    return jax.shard_map(
        functools.partial(local, mesh.shape["brick"], mesh.shape["band"]),
        mesh=mesh,
        in_specs=(P("band", "brick", None), P("band", "brick", None), P("brick", None), P(), P()),
        out_specs=(P("band", "brick", None), P("band", "brick", None)),
        check_vma=False,
    )
```

```python
import functools

import jax
import jax.numpy as jnp
from jax import lax
from jax.experimental import pallas as pl
from jax.experimental.pallas import tpu as pltpu
from jax.sharding import PartitionSpec as P

NZ = 64
FOURPI = 12.566370614359172
OMEGA = 0.8

CORES = 2
CHIPS_Y = 4
MOST = 4
BLOCK = 4 * MOST
GROUP = 512
LANES = 128
STEP = 32700.0
CODE = 128.0
MESH = pl.DeviceIdType.MESH
F32 = jnp.float32
BF16 = jnp.bfloat16


def iota(shape, dim):
    return lax.broadcasted_iota(jnp.int32, shape, dim)


def to(device):
    return dict(device_id=device, device_id_type=MESH)


def kernel(
    nz, nx,
    table_ref, val_ref, cond_ref,
    pair_ref, pot_ref,
    x_buf, g_buf, sel, found, spread, fold, z_buf, part, out_a, in_a, out_c, in_c,
    eps_all, eps_rows, coef, out_h, in_h, field, first, second, third, result,
    load_sem, zs, zr, ys, yr, cs, cr, xas, xar, xcs, xcr, hs, hr, es, er, out_sem,
):
    brick = lax.axis_index("brick")
    band = lax.axis_index("band")
    bricks = nz * CHIPS_Y * CORES
    core = lax.rem(brick, CORES)
    y = lax.rem(brick // CORES, CHIPS_Y)
    z = brick // (CORES * CHIPS_Y)
    nb8, _, _, plane = val_ref.shape
    nb = nb8 * 8
    npts = part.shape[2]
    owners, cells = table_ref[2:3, :npts], table_ref[3:4, :npts]
    fields = npts // nx
    chunks = fields // 8
    groups = min(4, nz)
    per = nz // groups
    tiles = plane // LANES
    parts = plane // GROUP

    def brick_at(zz, yy, cc):
        return (zz * CHIPS_Y + yy) * CORES + cc

    def brick_off(o):
        return lax.rem(brick + o + bricks, bricks)

    def band_off(o):
        return lax.rem(band + o, nx)

    barrier = pltpu.get_barrier_semaphore()

    @pl.loop(1, nz)
    def _(dz):
        pl.semaphore_signal(barrier, 1, **to({"brick": brick_at(lax.rem(z + dz, nz), y, core)}))

    for dy in (1, 3):
        pl.semaphore_signal(
            barrier, 1, **to({"brick": brick_at(z, lax.rem(y + dy, CHIPS_Y), core)})
        )
    pl.semaphore_signal(barrier, 1, **to({"brick": brick_at(z, y, 1 - core)}))
    for dx in (1, 3):
        pl.semaphore_signal(barrier, 1, **to({"band": band_off(dx)}))
    for o in (-2, -1, 1, 2):
        pl.semaphore_signal(barrier, 1, **to({"brick": brick_off(o)}))

    for s, psi in enumerate((val_ref, cond_ref)):
        for i in range(8):
            copy = pltpu.make_async_copy(
                psi.at[:, i], x_buf.at[s, :, 2 * i : 2 * i + 2, :], load_sem.at[s]
            )
            copy.start()

    first_index = iota((npts, npts), 0)
    second_index = iota((npts, npts), 1)
    owner_across = jnp.broadcast_to(owners, (npts, npts))
    owner_down = jnp.sum(
        jnp.where(first_index == second_index, owner_across, 0.0), axis=1, keepdims=True
    )
    same = owner_across == owner_down
    rank_down = jnp.sum(
        jnp.where(same & (second_index < first_index), 1.0, 0.0), axis=1, keepdims=True
    )
    rank_across = jnp.sum(
        jnp.where(same & (first_index < second_index), 1.0, 0.0), axis=0, keepdims=True
    )
    own = owners == brick.astype(F32)
    slot_of = iota((BLOCK, 1), 0) & (MOST - 1)
    slot_cell = jnp.zeros((BLOCK, 1), F32)
    for j in range(MOST):
        cell = jnp.sum(
            jnp.where(own & (rank_across == j), cells, 0.0),
            axis=1, keepdims=True,
        )
        slot_cell = jnp.where(slot_of == j, cell, slot_cell)
    slot_cell = slot_cell.astype(jnp.int32)
    slot_plane = jnp.where(slot_cell >= plane, 1, 0)
    slot_column = slot_cell - slot_plane * plane
    owner_down = owner_down.astype(jnp.int32)
    away = (owner_down >> 3) - z
    away = jnp.where(away < 0, away + nz, away)
    position = jnp.where(away <= nz // 2, 2 * away - 1, 2 * (nz - away))
    position = jnp.where(away == 0, 0, position)
    group_down = jnp.zeros_like(position)
    for g in range(1, groups):
        group_down = group_down + jnp.where(position >= g * per, 1, 0)
    place = ((owner_down & 1) * groups + group_down) * CHIPS_Y + ((owner_down >> 1) & 3)
    place = (place * per + position - group_down * per) * BLOCK + rank_down.astype(jnp.int32)
    pl.semaphore_wait(barrier, nz - 1 + 2 + 1 + 2 + 4)

    for o in (-2, -1, 1, 2):
        copy = pltpu.make_async_remote_copy(
            src_ref=table_ref, dst_ref=eps_all.at[2 - o],
            send_sem=es, recv_sem=er, **to({"brick": brick_off(o)})
        )
        copy.start()

    fold[...] = jnp.where((iota((2 * nb, nb), 0) >> 1) == iota((2 * nb, nb), 1), 1.0, 0.0).astype(BF16)

    half = nb // 2
    row = iota((BLOCK, LANES), 0)
    group_row = iota((BLOCK, GROUP), 0)

    taken = jnp.zeros((BLOCK, 2 * nb), F32)
    for s in range(2):
        pltpu.make_async_copy(x_buf.at[s], x_buf.at[s], load_sem.at[s]).wait()

        def take(n, taken):
            start = pl.multiple_of(n * GROUP, GROUP)
            pick = (iota((BLOCK, GROUP), 1) + start == slot_column) & (
                (group_row >> 3) == s
            )
            return taken + lax.dot_general(
                jnp.where(pick, 1.0, 0.0).astype(BF16),
                x_buf[s, :, :, pl.ds(start, GROUP)].reshape(2 * nb, GROUP),
                (((1,), (1,)), ((), ())), preferred_element_type=F32,
            )

        taken = lax.fori_loop(0, parts, take, taken)
    keep = (iota((BLOCK, 2 * nb), 1) & 1) == slot_plane
    taken = jnp.dot(
        jnp.where(keep, taken, 0.0).astype(BF16), fold[...], preferred_element_type=F32
    )
    mine = jnp.where(((row >> 2) & 1) == 0, taken[:, :half], taken[:, half:])
    g_buf[core, y, 0] = mine.astype(BF16)

    def z_copy(i):
        away = (i + 1) // 2 if i % 2 else -(i // 2)
        return pltpu.make_async_remote_copy(
            src_ref=g_buf.at[core, y, 0], dst_ref=g_buf.at[core, y, i],
            send_sem=zs, recv_sem=zr.at[i // per],
            **to({"brick": brick_at(lax.rem(z - away + nz, nz), y, core)})
        )

    for i in range(1, nz):
        z_copy(i).start()

    @pl.loop(0, sel.shape[1] // GROUP)
    def _(n):
        column = iota((npts, GROUP), 1) + n * GROUP
        for q in range(4):
            hit = column == place + q * MOST
            sel[pl.ds(q * npts, npts), pl.ds(pl.multiple_of(n * GROUP, GROUP), GROUP)] = (
                jnp.where(hit, 1.0, 0.0).astype(BF16)
            )

    for p in range(2):
        spread[:, 2 * nb * p : 2 * nb * (p + 1)] = jnp.where(
            iota((nb, 2 * nb), 1) == 2 * iota((nb, 2 * nb), 0) + p, 1.0, 0.0
        ).astype(BF16)

    y_up, y_down = lax.rem(y + 1, CHIPS_Y), lax.rem(y + 3, CHIPS_Y)

    def y_copy(g, way):
        odd = g % 2
        source = y if way < 2 else (y_up if odd else y_down)
        target = (y_up, y_down, y_down if odd else y_up)[way]
        part_of = g_buf.at[core, source, pl.ds(g * per, per)]
        return pltpu.make_async_remote_copy(
            src_ref=part_of, dst_ref=part_of, send_sem=ys,
            recv_sem=yr.at[g, 0 if way == odd else 1],
            **to({"brick": brick_at(z, target, core)})
        )

    def y_arrived(g, n):
        block = g_buf.at[core, pl.ds(0, n + 1), pl.ds(g * per, per)]
        pltpu.make_async_remote_copy(
            src_ref=block, dst_ref=block, send_sem=ys, recv_sem=yr.at[g, n],
            **to({"brick": brick_at(z, y_up, core)})
        ).wait_recv()

    def core_copy(g):
        part_of = g_buf.at[core, :, pl.ds(g * per, per)]
        return pltpu.make_async_remote_copy(
            src_ref=part_of, dst_ref=part_of, send_sem=cs, recv_sem=cr.at[g],
            **to({"brick": brick_at(z, y, 1 - core)})
        )

    columns_of = CHIPS_Y * per * BLOCK

    def find(c, g):
        rows = g_buf[c, :, pl.ds(g * per, per)].reshape(columns_of, LANES)
        start = pl.multiple_of((c * groups + g) * columns_of, columns_of)
        return jnp.dot(sel[:, pl.ds(start, columns_of)], rows, preferred_element_type=F32)

    found[...] = jnp.zeros_like(found)
    for step in range(groups + 3):
        if step < groups:
            come = g_buf.at[core, y, pl.ds(max(1, step * per), per if step else per - 1)]
            pltpu.make_async_remote_copy(
                src_ref=come, dst_ref=come, send_sem=zs, recv_sem=zr.at[step],
                **to({"brick": brick_at(lax.rem(z + 1, nz), y, core)})
            ).wait_recv()
            y_copy(step, 0).start()
            y_copy(step, 1).start()
        if 1 <= step <= groups:
            g = step - 1
            y_arrived(g, 0)
            y_copy(g, 2).start()
        if 2 <= step <= groups + 1:
            g = step - 2
            y_arrived(g, 1)
            core_copy(g).start()
            found[...] += find(core, g)
        if step >= 3:
            g = step - 3
            block = g_buf.at[1 - core, :, pl.ds(g * per, per)]
            pltpu.make_async_remote_copy(
                src_ref=block, dst_ref=block, send_sem=cs, recv_sem=cr.at[g],
                **to({"brick": brick_at(z, y, 1 - core)})
            ).wait_recv()
            found[...] += find(1 - core, g)

    for s in range(2):
        at_points = jnp.concatenate(
            [found[(2 * s + i) * npts : (2 * s + i + 1) * npts, :] for i in range(2)], axis=1
        ).astype(BF16)
        wide = jnp.dot(at_points, spread[...], preferred_element_type=F32).astype(BF16)
        for p in range(2):
            z_buf[s, p * npts : (p + 1) * npts, :] = wide[:, 2 * nb * p : 2 * nb * (p + 1)]

    @pl.loop(0, parts)
    def _(n):
        at = pl.ds(pl.multiple_of(n * GROUP, GROUP), GROUP)
        for s in range(2):
            got = jnp.dot(
                z_buf[s], x_buf[s, :, :, at].reshape(2 * nb, GROUP), preferred_element_type=F32
            )
            part[s, :, :, at] = got.reshape(2, npts, GROUP)

    code_lane = iota((16, LANES), 1)

    def lanes_of(n):
        return slice(n * GROUP + LANES * (n >= parts), (n + 1) * GROUP + LANES * (n >= parts))

    def pack(*messages):
        scales = []
        for values_at, target, count in messages:
            most = jnp.zeros((16, LANES), F32)
            for n in range(count):
                peak = jnp.max(jnp.abs(values_at(n)), axis=1, keepdims=True)
                most = jnp.where(code_lane == n, peak, most)
            code = jnp.ceil(jnp.log2(jnp.maximum(most, 1e-30)) * CODE)
            scales.append((code, STEP * jnp.exp2(code * (-1.0 / CODE))))
        for (values_at, target, count), (code, scale) in zip(messages, scales):
            first_of = min(count, parts) * GROUP
            target[:, first_of : first_of + LANES] = code.astype(jnp.int32).astype(jnp.int16)
            for n in range(count):
                whole = jnp.round(values_at(n) * scale[:, n : n + 1])
                target[:, lanes_of(n)] = whole.astype(jnp.int32).astype(jnp.int16)

    def unpacker(source, count):
        first_of = min(count, parts) * GROUP
        codes = source[:, first_of : first_of + LANES].astype(jnp.int32).astype(F32)
        scales = jnp.exp2(codes * (1.0 / CODE)) * (1.0 / STEP)

        def values_at(n):
            got = source[:, lanes_of(n)].astype(jnp.int32).astype(F32)
            return got * scales[:, n : n + 1]

        return values_at

    def held(target, p, k):
        start = pl.multiple_of(target * fields + k * 8, 8)

        def values_at(n):
            at = slice(n * GROUP, (n + 1) * GROUP)
            return jnp.concatenate(
                [part[0, p, pl.ds(start, 8), at], part[1, p, pl.ds(start, 8), at]], axis=0
            )

        return values_at

    up, down, across = band_off(1), band_off(3), band_off(2)
    heading = (up, down)

    pieces = ((0, plane + LANES), (plane + LANES, plane))

    def a_copy(k, way, piece):
        at = pl.ds(*pieces[piece])
        return pltpu.make_async_remote_copy(
            src_ref=out_a.at[way, k, :, at], dst_ref=in_a.at[way, k, :, at],
            send_sem=xas, recv_sem=xar.at[piece, k], **to({"band": heading[way]})
        )

    def c_copy(k, way):
        return pltpu.make_async_remote_copy(
            src_ref=out_c.at[way, k], dst_ref=in_c.at[way, k],
            send_sem=xcs, recv_sem=xcr.at[k], **to({"band": heading[way]})
        )

    def send(k):
        def message(way):
            passed, direct = held(across, way, k), held(heading[way], 1 - way, k)
            return (
                lambda n: passed(n) if n < parts else direct(n - parts),
                out_a.at[way, k], 2 * parts,
            )

        pack(message(0), message(1))
        for piece in range(2):
            for way in range(2):
                a_copy(k, way, piece).start()

    def arrived(k, piece):
        both = in_a.at[:, k, :, pl.ds(*pieces[piece])]
        pltpu.make_async_remote_copy(
            src_ref=both, dst_ref=both, send_sem=xas, recv_sem=xar.at[piece, k],
            **to({"band": up})
        ).wait_recv()

    def join(k):
        arrived(k, 0)
        def message(way):
            mine_at, got_at = held(heading[way], way, k), unpacker(in_a.at[way, k], 2 * parts)
            return lambda n: mine_at(n) + got_at(n), out_c.at[way, k], parts

        pack(message(0), message(1))
        for way in range(2):
            c_copy(k, way).start()

    sides = ((-2, 0, 1, 5), (-1, 0, 2, 3), (1, 0, 2, 1), (2, 1, 1, 0))

    def h_copy(k, n):
        o, source, count, target = sides[n]
        return pltpu.make_async_remote_copy(
            src_ref=out_h.at[k, source : source + count],
            dst_ref=in_h.at[k, target : target + count],
            send_sem=hs, recv_sem=hr.at[k], **to({"brick": brick_off(o)})
        )

    def out_copy(which, p, start, count):
        rows = pl.ds(start, count)
        return pltpu.make_async_copy(
            (field, result)[which].at[p, rows], (pair_ref, pot_ref)[which].at[rows, p, :],
            out_sem.at[which],
        )

    def product(k):
        arrived(k, 1)
        both = in_c.at[:, k]
        pltpu.make_async_remote_copy(
            src_ref=both, dst_ref=both, send_sem=xcs, recv_sem=xcr.at[k], **to({"band": up})
        ).wait_recv()
        rows = pl.ds(pl.multiple_of(k * 8, 8), 8)
        for p in range(2):
            direct = unpacker(in_a.at[1 - p, k], 2 * parts)
            parts_at = (
                held(band, p, k), lambda n: direct(n + parts), unpacker(in_c.at[p, k], parts)
            )
            pairs = []
            for n in range(parts):
                total = sum(values_at(n) for values_at in parts_at)
                pairs.append(total[:8, :] * total[8:, :])
            for n in range(parts):
                field[p, rows, n * GROUP : (n + 1) * GROUP] = pairs[n]

        def message(p):
            def halves(n):
                return jnp.concatenate(
                    [
                        field[p, rows, m * GROUP : (m + 1) * GROUP]
                        for m in (n, n + parts // 2)
                    ],
                    axis=0,
                )

            return halves, out_h.at[k, p], parts // 2

        pack(message(0), message(1))

        @pl.when(k == chunks - 1)
        def _():
            for p in range(2):
                out_copy(0, p, 0, fields).start()

    low_half = iota((8, LANES), 1) < NZ

    def sweep(source, e):
        tile_at = [pl.ds(t * LANES, LANES) for t in range(tiles)]
        swapped = [pltpu.roll(source[e, :, at], NZ, 1) for at in tile_at]
        news = []
        for t, at in enumerate(tile_at):
            v = source[e, :, at]
            before = swapped[(t - 1) % tiles]
            after = swapped[(t + 1) % tiles]
            alone = (1.0 - OMEGA) * v + first[e, :, at]
            along_x = coef[0, e, :, at] * source[e - 1, :, at]
            along_x = along_x + coef[1, e, :, at] * source[e + 1, :, at]
            along_y = coef[2, e, :, at] * jnp.where(low_half, before, swapped[t])
            along_y = along_y + coef[3, e, :, at] * jnp.where(low_half, swapped[t], after)
            along_z = coef[4, e, :, at] * pltpu.roll(v, 1, 1)
            along_z = along_z + coef[5, e, :, at] * pltpu.roll(v, LANES - 1, 1)
            news.append((alone + along_x) + (along_y + along_z))
        return zip(tile_at, news)

    def sweeps(k):
        come = in_h.at[k]
        pltpu.make_async_remote_copy(
            src_ref=come, dst_ref=come, send_sem=hs, recv_sem=hr.at[k],
            **to({"brick": brick_off(1)})
        ).wait_recv()
        rows = pl.ds(pl.multiple_of(k * 8, 8), 8)
        for p in range(2):
            first[3 + p] = coef[6, 3 + p] * field[p, rows, :]

        @pl.loop(0, 6)
        def _(i):
            e = i + 2 * (i // 3)
            halves = unpacker(in_h.at[k, i], parts // 2)
            values = [halves(n) for n in range(parts // 2)]
            for m in range(parts):
                at = slice(m * GROUP, (m + 1) * GROUP)
                half = values[m % (parts // 2)][8 * (m // (parts // 2)) :, :][:8, :]
                first[e, :, at] = coef[6, e, :, at] * half

        @pl.loop(1, 7)
        def _(e):
            for at, new in sweep(first, e):
                second[e, :, at] = new

        @pl.loop(2, 6)
        def _(e):
            for at, new in sweep(second, e):
                third[e, :, at] = new

        @pl.loop(3, 5)
        def _(e):
            for at, new in sweep(third, e):
                result[e - 3, rows, at] = new

        last = 8 * (chunks - 1)

        @pl.when(k == chunks - 2)
        def _():
            for p in range(2):
                out_copy(1, p, 0, last).start()

        @pl.when(k == chunks - 1)
        def _():
            for p in range(2):
                out_copy(1, p, last, 8).start()

    def coefficients():
        pltpu.make_async_remote_copy(
            src_ref=eps_all.at[0:4], dst_ref=eps_all.at[0:4], send_sem=es, recv_sem=er,
            **to({"brick": brick_off(1)})
        ).wait()
        for o in range(5):
            eps_rows[2 * o : 2 * o + 2, :] = table_ref[:2, :] if o == 2 else eps_all[o, :2, :]
        here = eps_rows[1:9, :]
        xminus = 0.5 * (here + eps_rows[0:8, :])
        xplus = 0.5 * (here + eps_rows[2:10, :])
        depth = iota((8, plane), 1) & (NZ - 1)
        above = depth < NZ - 1
        below = depth > 0
        yplus = 0.5 * (here + pltpu.roll(here, plane - NZ, 1))
        yminus = 0.5 * (here + pltpu.roll(here, NZ, 1))
        zplus = 0.5 * (here + jnp.where(above, pltpu.roll(here, plane - 1, 1), here))
        zminus = 0.5 * (here + jnp.where(below, pltpu.roll(here, 1, 1), here))
        scale = OMEGA / (xplus + xminus + yplus + yminus + zplus + zminus)
        faces = (
            xminus, xplus, yminus, yplus,
            jnp.where(below, zminus, 0.0), jnp.where(above, zplus, 0.0), FOURPI,
        )
        for n, face in enumerate(faces):
            scaled = scale * face
            for e in range(8):
                coef[n, e] = jnp.broadcast_to(scaled[e : e + 1, :], (8, plane))

    @pl.loop(0, chunks + 6)
    def _(step):
        @pl.when(step < chunks)
        def _():
            send(step)

        @pl.when((step >= 2) & (step < chunks + 2))
        def _():
            join(step - 2)

        @pl.when(step == 3)
        def _():
            coefficients()

        @pl.when((step >= 4) & (step < chunks + 4))
        def _():
            product(step - 4)
            for n in range(4):
                h_copy(step - 4, n).start()

        @pl.when(step >= 6)
        def _():
            sweeps(step - 6)

    def sent(ref, sem, recv_sem):
        pltpu.make_async_remote_copy(
            src_ref=ref, dst_ref=ref, send_sem=sem, recv_sem=recv_sem,
            **to({"brick": brick_off(1)})
        ).wait_send()

    sent(g_buf.at[core, y, pl.ds(1, nz - 1)], zs, zr.at[0])
    sent(g_buf.at[core, pl.ds(0, 3)], ys, yr.at[0, 0])
    sent(g_buf.at[core], cs, cr.at[0])
    sent(out_a, xas, xar.at[0, 0])
    sent(out_c, xcs, xcr.at[0])
    sent(in_h, hs, hr.at[0])
    for which, ref in enumerate((field, result)):
        pltpu.make_async_copy(ref, ref, out_sem.at[which]).wait()


def local(bricks, nx, psi_val, psi_cond, dielectric, point_owner, point_cell):
    nb, _, plane = psi_val.shape
    npts = point_owner.shape[0]
    nz = bricks // (CHIPS_Y * CORES)
    groups = min(4, nz)
    fields = npts // nx
    chunks = fields // 8
    rows = bricks * BLOCK

    def row(values):
        return jnp.pad(values[None, :], ((0, 0), (0, plane - npts))).astype(F32)

    table = jnp.concatenate([dielectric, row(point_owner), row(point_cell)], axis=0)

    vmem = pl.BlockSpec(memory_space=pltpu.VMEM)
    dma = pltpu.SemaphoreType.DMA
    pair, potential = pl.pallas_call(
        functools.partial(kernel, nz, nx),
        out_shape=[jax.ShapeDtypeStruct((fields, 2, plane), F32)] * 2,
        in_specs=[
            vmem, pl.BlockSpec(memory_space=pl.ANY), pl.BlockSpec(memory_space=pl.ANY),
        ],
        out_specs=[pl.BlockSpec(memory_space=pl.ANY)] * 2,
        scratch_shapes=[
            pltpu.VMEM((2, nb // 8, 16, plane), BF16),
            pltpu.VMEM((CORES, CHIPS_Y, nz, BLOCK, LANES), BF16),
            pltpu.VMEM((4 * npts, rows), BF16),
            pltpu.VMEM((4 * npts, LANES), F32),
            pltpu.VMEM((nb, 4 * nb), BF16),
            pltpu.VMEM((2 * nb, nb), BF16),
            pltpu.VMEM((2, 2 * npts, 2 * nb), BF16),
            pltpu.VMEM((2, 2, npts, plane), F32),
            pltpu.VMEM((2, chunks, 16, 2 * plane + LANES), jnp.int16),
            pltpu.VMEM((2, chunks, 16, 2 * plane + LANES), jnp.int16),
            pltpu.VMEM((2, chunks, 16, plane + LANES), jnp.int16),
            pltpu.VMEM((2, chunks, 16, plane + LANES), jnp.int16),
            pltpu.VMEM((5, 4, plane), F32),
            pltpu.VMEM((16, plane), F32),
            pltpu.VMEM((7, 8, 8, plane), F32),
            pltpu.VMEM((chunks, 2, 16, plane // 2 + LANES), jnp.int16),
            pltpu.VMEM((chunks, 6, 16, plane // 2 + LANES), jnp.int16),
            pltpu.VMEM((2, fields, plane), F32),
            pltpu.VMEM((8, 8, plane), F32),
            pltpu.VMEM((8, 8, plane), F32),
            pltpu.VMEM((8, 8, plane), F32),
            pltpu.VMEM((2, fields, plane), F32),
            dma((2,)),
            dma, dma((groups,)),
            dma, dma((groups, 2)),
            dma, dma((groups,)),
            dma, dma((2, chunks)),
            dma, dma((chunks,)),
            dma, dma((chunks,)),
            dma, dma,
            dma((2,)),
        ],
        compiler_params=pltpu.CompilerParams(
            collective_id=0, has_side_effects=True, vmem_limit_bytes=52 << 20
        ),
        cost_estimate=pl.CostEstimate(
            flops=2 * 2 * 2 * npts * 2 * nb * plane,
            bytes_accessed=8 * nb * plane + 16 * fields * plane,
            transcendentals=0,
        ),
    )(
        table, psi_val.reshape(nb // 8, 8, 2, plane), psi_cond.reshape(nb // 8, 8, 2, plane),
    )
    return pair, potential


def solution(mesh):
    return jax.shard_map(
        functools.partial(local, mesh.shape["brick"], mesh.shape["band"]),
        mesh=mesh,
        in_specs=(P("band", "brick", None), P("band", "brick", None), P("brick", None), P(), P()),
        out_specs=(P("band", "brick", None), P("band", "brick", None)),
        check_vma=False,
    )
```

```python
import functools

import jax
import jax.numpy as jnp
from jax import lax
from jax.experimental import pallas as pl
from jax.experimental.pallas import tpu as pltpu
from jax.sharding import PartitionSpec as P

NZ = 64
FOURPI = 12.566370614359172
OMEGA = 0.8

CORES = 2
CHIPS_Y = 4
MOST = 4
BLOCK = 4 * MOST
GROUP = 512
LANES = 128
STEP = 32700.0
CODE = 128.0
MESH = pl.DeviceIdType.MESH
F32 = jnp.float32
BF16 = jnp.bfloat16


def iota(shape, dim):
    return lax.broadcasted_iota(jnp.int32, shape, dim)


def to(device):
    return dict(device_id=device, device_id_type=MESH)


def kernel(
    nz, nx,
    table_ref, val_ref, cond_ref,
    pair_ref, pot_ref,
    x_buf, g_buf, sel, found, spread, fold, pick, taken, z_buf, part, out_a, in_a, out_c, in_c,
    eps_all, eps_rows, coef, out_h, in_h, field, first, second, third, result,
    load_sem, zs, zr, ys, yr, cs, cr, xas, xar, xcs, xcr, hs, hr, es, er, out_sem,
):
    brick = lax.axis_index("brick")
    band = lax.axis_index("band")
    bricks = nz * CHIPS_Y * CORES
    core = lax.rem(brick, CORES)
    y = lax.rem(brick // CORES, CHIPS_Y)
    z = brick // (CORES * CHIPS_Y)
    nb8, _, _, plane = val_ref.shape
    nb = nb8 * 8
    npts = part.shape[2]
    owners, cells = table_ref[2:3, :npts], table_ref[3:4, :npts]
    fields = npts // nx
    chunks = fields // 8
    groups = min(4, nz)
    per = nz // groups
    tiles = plane // LANES
    parts = plane // GROUP

    def brick_at(zz, yy, cc):
        return (zz * CHIPS_Y + yy) * CORES + cc

    def brick_off(o):
        return lax.rem(brick + o + bricks, bricks)

    def band_off(o):
        return lax.rem(band + o, nx)

    barrier = pltpu.get_barrier_semaphore()

    @pl.loop(1, nz)
    def _(dz):
        pl.semaphore_signal(barrier, 1, **to({"brick": brick_at(lax.rem(z + dz, nz), y, core)}))

    for dy in (1, 3):
        pl.semaphore_signal(
            barrier, 1, **to({"brick": brick_at(z, lax.rem(y + dy, CHIPS_Y), core)})
        )
    pl.semaphore_signal(barrier, 1, **to({"brick": brick_at(z, y, 1 - core)}))
    for dx in (1, 3):
        pl.semaphore_signal(barrier, 1, **to({"band": band_off(dx)}))
    for o in (-2, -1, 1, 2):
        pl.semaphore_signal(barrier, 1, **to({"brick": brick_off(o)}))

    for s, psi in enumerate((val_ref, cond_ref)):
        for i in range(8):
            copy = pltpu.make_async_copy(
                psi.at[:, i], x_buf.at[s, :, 2 * i : 2 * i + 2, :], load_sem.at[s]
            )
            copy.start()

    first_index = iota((npts, npts), 0)
    second_index = iota((npts, npts), 1)
    owner_across = jnp.broadcast_to(owners, (npts, npts))
    owner_down = jnp.sum(
        jnp.where(first_index == second_index, owner_across, 0.0), axis=1, keepdims=True
    )
    same = owner_across == owner_down
    rank_down = jnp.sum(
        jnp.where(same & (second_index < first_index), 1.0, 0.0), axis=1, keepdims=True
    )
    rank_across = jnp.sum(
        jnp.where(same & (first_index < second_index), 1.0, 0.0), axis=0, keepdims=True
    )
    own = owners == brick.astype(F32)
    slot_of = iota((1, LANES), 1) & (MOST - 1)
    slot_cell = jnp.zeros((1, LANES), F32)
    for j in range(MOST):
        cell = jnp.sum(
            jnp.where(own & (rank_across == j), cells, 0.0),
            axis=1, keepdims=True,
        )
        slot_cell = jnp.where(slot_of == j, cell, slot_cell)
    slot_cell = slot_cell.astype(jnp.int32)
    slot_plane = jnp.where(slot_cell >= plane, 1, 0)
    slot_column = slot_cell - slot_plane * plane
    owner_down = owner_down.astype(jnp.int32)
    away = (owner_down >> 3) - z
    away = jnp.where(away < 0, away + nz, away)
    position = jnp.where(away <= nz // 2, 2 * away - 1, 2 * (nz - away))
    position = jnp.where(away == 0, 0, position)
    group_down = jnp.zeros_like(position)
    for g in range(1, groups):
        group_down = group_down + jnp.where(position >= g * per, 1, 0)
    place = ((owner_down & 1) * groups + group_down) * CHIPS_Y + ((owner_down >> 1) & 3)
    place = (place * per + position - group_down * per) * BLOCK + rank_down.astype(jnp.int32)

    fold[...] = jnp.where(iota((nb, 2 * nb), 0) == (iota((nb, 2 * nb), 1) >> 1), 1.0, 0.0).astype(
        BF16
    )
    for s in range(2):
        for n in range(parts):
            hit = (iota((GROUP, LANES), 0) + n * GROUP == slot_column) & (
                (iota((GROUP, LANES), 1) >> 3) == s
            )
            pick[s, n * GROUP : (n + 1) * GROUP, :] = jnp.where(hit, 1.0, 0.0).astype(BF16)

    half = nb // 2
    taken[...] = jnp.zeros_like(taken)
    for s in range(2):
        pltpu.make_async_copy(x_buf.at[s], x_buf.at[s], load_sem.at[s]).wait()
        taken[...] += jnp.dot(
            x_buf[s].reshape(2 * nb, plane), pick[s], preferred_element_type=F32
        )
    keep = (iota((2 * nb, LANES), 0) & 1) == slot_plane
    folded = jnp.dot(
        fold[...], jnp.where(keep, taken[...], 0.0).astype(BF16), preferred_element_type=F32
    )
    halves = [folded[half * i : half * (i + 1), :].T[:BLOCK, :] for i in range(2)]
    mine = jnp.where(((iota((BLOCK, half), 0) >> 2) & 1) == 0, halves[0], halves[1])
    g_buf[core, y, 0] = mine.astype(BF16)

    pl.semaphore_wait(barrier, nz - 1 + 2 + 1 + 2 + 4)

    def z_copy(i):
        away = (i + 1) // 2 if i % 2 else -(i // 2)
        return pltpu.make_async_remote_copy(
            src_ref=g_buf.at[core, y, 0], dst_ref=g_buf.at[core, y, i],
            send_sem=zs, recv_sem=zr.at[i // per],
            **to({"brick": brick_at(lax.rem(z - away + nz, nz), y, core)})
        )

    for i in range(1, nz):
        z_copy(i).start()

    for o in (-2, -1, 1, 2):
        copy = pltpu.make_async_remote_copy(
            src_ref=table_ref, dst_ref=eps_all.at[2 - o],
            send_sem=es, recv_sem=er, **to({"brick": brick_off(o)})
        )
        copy.start()

    @pl.loop(0, sel.shape[1] // GROUP)
    def _(n):
        column = iota((npts, GROUP), 1) + n * GROUP
        for q in range(4):
            hit = column == place + q * MOST
            sel[pl.ds(q * npts, npts), pl.ds(pl.multiple_of(n * GROUP, GROUP), GROUP)] = (
                jnp.where(hit, 1.0, 0.0).astype(BF16)
            )

    for p in range(2):
        spread[:, 2 * nb * p : 2 * nb * (p + 1)] = jnp.where(
            iota((nb, 2 * nb), 1) == 2 * iota((nb, 2 * nb), 0) + p, 1.0, 0.0
        ).astype(BF16)

    y_up, y_down = lax.rem(y + 1, CHIPS_Y), lax.rem(y + 3, CHIPS_Y)

    def y_copy(g, way):
        odd = g % 2
        source = y if way < 2 else (y_up if odd else y_down)
        target = (y_up, y_down, y_down if odd else y_up)[way]
        part_of = g_buf.at[core, source, pl.ds(g * per, per)]
        return pltpu.make_async_remote_copy(
            src_ref=part_of, dst_ref=part_of, send_sem=ys,
            recv_sem=yr.at[g, 0 if way == odd else 1],
            **to({"brick": brick_at(z, target, core)})
        )

    def y_arrived(g, n):
        block = g_buf.at[core, pl.ds(0, n + 1), pl.ds(g * per, per)]
        pltpu.make_async_remote_copy(
            src_ref=block, dst_ref=block, send_sem=ys, recv_sem=yr.at[g, n],
            **to({"brick": brick_at(z, y_up, core)})
        ).wait_recv()

    def core_copy(g):
        part_of = g_buf.at[core, :, pl.ds(g * per, per)]
        return pltpu.make_async_remote_copy(
            src_ref=part_of, dst_ref=part_of, send_sem=cs, recv_sem=cr.at[g],
            **to({"brick": brick_at(z, y, 1 - core)})
        )

    columns_of = CHIPS_Y * per * BLOCK

    def find(c, g):
        rows = g_buf[c, :, pl.ds(g * per, per)].reshape(columns_of, LANES)
        start = pl.multiple_of((c * groups + g) * columns_of, columns_of)
        return jnp.dot(sel[:, pl.ds(start, columns_of)], rows, preferred_element_type=F32)

    found[...] = jnp.zeros_like(found)
    for step in range(groups + 3):
        if step < groups:
            come = g_buf.at[core, y, pl.ds(max(1, step * per), per if step else per - 1)]
            pltpu.make_async_remote_copy(
                src_ref=come, dst_ref=come, send_sem=zs, recv_sem=zr.at[step],
                **to({"brick": brick_at(lax.rem(z + 1, nz), y, core)})
            ).wait_recv()
            y_copy(step, 0).start()
            y_copy(step, 1).start()
        if 1 <= step <= groups:
            g = step - 1
            y_arrived(g, 0)
            y_copy(g, 2).start()
        if 2 <= step <= groups + 1:
            g = step - 2
            y_arrived(g, 1)
            core_copy(g).start()
            found[...] += find(core, g)
        if step >= 3:
            g = step - 3
            block = g_buf.at[1 - core, :, pl.ds(g * per, per)]
            pltpu.make_async_remote_copy(
                src_ref=block, dst_ref=block, send_sem=cs, recv_sem=cr.at[g],
                **to({"brick": brick_at(z, y, 1 - core)})
            ).wait_recv()
            found[...] += find(1 - core, g)

    for s in range(2):
        at_points = jnp.concatenate(
            [found[(2 * s + i) * npts : (2 * s + i + 1) * npts, :] for i in range(2)], axis=1
        ).astype(BF16)
        wide = jnp.dot(at_points, spread[...], preferred_element_type=F32).astype(BF16)
        for p in range(2):
            z_buf[s, p * npts : (p + 1) * npts, :] = wide[:, 2 * nb * p : 2 * nb * (p + 1)]

    @pl.loop(0, parts)
    def _(n):
        at = pl.ds(pl.multiple_of(n * GROUP, GROUP), GROUP)
        for s in range(2):
            got = jnp.dot(
                z_buf[s], x_buf[s, :, :, at].reshape(2 * nb, GROUP), preferred_element_type=F32
            )
            part[s, :, :, at] = got.reshape(2, npts, GROUP)

    code_lane = iota((16, LANES), 1)

    def lanes_of(n):
        return slice(n * GROUP + LANES * (n >= parts), (n + 1) * GROUP + LANES * (n >= parts))

    def pack(*messages):
        scales = []
        for values_at, target, count in messages:
            most = jnp.zeros((16, LANES), F32)
            for n in range(count):
                peak = jnp.max(jnp.abs(values_at(n)), axis=1, keepdims=True)
                most = jnp.where(code_lane == n, peak, most)
            code = jnp.ceil(jnp.log2(jnp.maximum(most, 1e-30)) * CODE)
            scales.append((code, STEP * jnp.exp2(code * (-1.0 / CODE))))
        for (values_at, target, count), (code, scale) in zip(messages, scales):
            first_of = min(count, parts) * GROUP
            target[:, first_of : first_of + LANES] = code.astype(jnp.int32).astype(jnp.int16)
            for n in range(count):
                whole = jnp.round(values_at(n) * scale[:, n : n + 1])
                target[:, lanes_of(n)] = whole.astype(jnp.int32).astype(jnp.int16)

    def unpacker(source, count):
        first_of = min(count, parts) * GROUP
        codes = source[:, first_of : first_of + LANES].astype(jnp.int32).astype(F32)
        scales = jnp.exp2(codes * (1.0 / CODE)) * (1.0 / STEP)

        def values_at(n):
            got = source[:, lanes_of(n)].astype(jnp.int32).astype(F32)
            return got * scales[:, n : n + 1]

        return values_at

    def held(target, p, k):
        start = pl.multiple_of(target * fields + k * 8, 8)

        def values_at(n):
            at = slice(n * GROUP, (n + 1) * GROUP)
            return jnp.concatenate(
                [part[0, p, pl.ds(start, 8), at], part[1, p, pl.ds(start, 8), at]], axis=0
            )

        return values_at

    up, down, across = band_off(1), band_off(3), band_off(2)
    heading = (up, down)

    pieces = ((0, plane + LANES), (plane + LANES, plane))

    def a_copy(k, way, piece):
        at = pl.ds(*pieces[piece])
        return pltpu.make_async_remote_copy(
            src_ref=out_a.at[way, k, :, at], dst_ref=in_a.at[way, k, :, at],
            send_sem=xas, recv_sem=xar.at[piece, k], **to({"band": heading[way]})
        )

    def c_copy(k, way):
        return pltpu.make_async_remote_copy(
            src_ref=out_c.at[way, k], dst_ref=in_c.at[way, k],
            send_sem=xcs, recv_sem=xcr.at[k], **to({"band": heading[way]})
        )

    def send(k):
        def message(way):
            passed, direct = held(across, way, k), held(heading[way], 1 - way, k)
            return (
                lambda n: passed(n) if n < parts else direct(n - parts),
                out_a.at[way, k], 2 * parts,
            )

        pack(message(0), message(1))
        for piece in range(2):
            for way in range(2):
                a_copy(k, way, piece).start()

    def arrived(k, piece):
        both = in_a.at[:, k, :, pl.ds(*pieces[piece])]
        pltpu.make_async_remote_copy(
            src_ref=both, dst_ref=both, send_sem=xas, recv_sem=xar.at[piece, k],
            **to({"band": up})
        ).wait_recv()

    def join(k):
        arrived(k, 0)
        def message(way):
            mine_at, got_at = held(heading[way], way, k), unpacker(in_a.at[way, k], 2 * parts)
            return lambda n: mine_at(n) + got_at(n), out_c.at[way, k], parts

        pack(message(0), message(1))
        for way in range(2):
            c_copy(k, way).start()

    sides = ((-2, 0, 1, 5), (-1, 0, 2, 3), (1, 0, 2, 1), (2, 1, 1, 0))

    def h_copy(k, n):
        o, source, count, target = sides[n]
        return pltpu.make_async_remote_copy(
            src_ref=out_h.at[k, source : source + count],
            dst_ref=in_h.at[k, target : target + count],
            send_sem=hs, recv_sem=hr.at[k], **to({"brick": brick_off(o)})
        )

    def out_copy(which, p, start, count):
        rows = pl.ds(start, count)
        return pltpu.make_async_copy(
            (field, result)[which].at[p, rows], (pair_ref, pot_ref)[which].at[rows, p, :],
            out_sem.at[which],
        )

    def product(k):
        arrived(k, 1)
        both = in_c.at[:, k]
        pltpu.make_async_remote_copy(
            src_ref=both, dst_ref=both, send_sem=xcs, recv_sem=xcr.at[k], **to({"band": up})
        ).wait_recv()
        rows = pl.ds(pl.multiple_of(k * 8, 8), 8)
        for p in range(2):
            direct = unpacker(in_a.at[1 - p, k], 2 * parts)
            parts_at = (
                held(band, p, k), lambda n: direct(n + parts), unpacker(in_c.at[p, k], parts)
            )
            pairs = []
            for n in range(parts):
                total = sum(values_at(n) for values_at in parts_at)
                pairs.append(total[:8, :] * total[8:, :])
            for n in range(parts):
                field[p, rows, n * GROUP : (n + 1) * GROUP] = pairs[n]

        def message(p):
            def halves(n):
                return jnp.concatenate(
                    [
                        field[p, rows, m * GROUP : (m + 1) * GROUP]
                        for m in (n, n + parts // 2)
                    ],
                    axis=0,
                )

            return halves, out_h.at[k, p], parts // 2

        pack(message(0), message(1))

        @pl.when(k == chunks - 1)
        def _():
            for p in range(2):
                out_copy(0, p, 0, fields).start()

    low_half = iota((8, LANES), 1) < NZ

    def sweep(source, e):
        tile_at = [pl.ds(t * LANES, LANES) for t in range(tiles)]
        swapped = [pltpu.roll(source[e, :, at], NZ, 1) for at in tile_at]
        news = []
        for t, at in enumerate(tile_at):
            v = source[e, :, at]
            before = swapped[(t - 1) % tiles]
            after = swapped[(t + 1) % tiles]
            alone = (1.0 - OMEGA) * v + first[e, :, at]
            along_x = coef[0, e, :, at] * source[e - 1, :, at]
            along_x = along_x + coef[1, e, :, at] * source[e + 1, :, at]
            along_y = coef[2, e, :, at] * jnp.where(low_half, before, swapped[t])
            along_y = along_y + coef[3, e, :, at] * jnp.where(low_half, swapped[t], after)
            along_z = coef[4, e, :, at] * pltpu.roll(v, 1, 1)
            along_z = along_z + coef[5, e, :, at] * pltpu.roll(v, LANES - 1, 1)
            news.append((alone + along_x) + (along_y + along_z))
        return zip(tile_at, news)

    def sweeps(k):
        come = in_h.at[k]
        pltpu.make_async_remote_copy(
            src_ref=come, dst_ref=come, send_sem=hs, recv_sem=hr.at[k],
            **to({"brick": brick_off(1)})
        ).wait_recv()
        rows = pl.ds(pl.multiple_of(k * 8, 8), 8)
        for p in range(2):
            first[3 + p] = coef[6, 3 + p] * field[p, rows, :]

        @pl.loop(0, 6)
        def _(i):
            e = i + 2 * (i // 3)
            halves = unpacker(in_h.at[k, i], parts // 2)
            values = [halves(n) for n in range(parts // 2)]
            for m in range(parts):
                at = slice(m * GROUP, (m + 1) * GROUP)
                half = values[m % (parts // 2)][8 * (m // (parts // 2)) :, :][:8, :]
                first[e, :, at] = coef[6, e, :, at] * half

        @pl.loop(1, 7)
        def _(e):
            for at, new in sweep(first, e):
                second[e, :, at] = new

        @pl.loop(2, 6)
        def _(e):
            for at, new in sweep(second, e):
                third[e, :, at] = new

        @pl.loop(3, 5)
        def _(e):
            for at, new in sweep(third, e):
                result[e - 3, rows, at] = new

        last = 8 * (chunks - 1)

        @pl.when(k == chunks - 2)
        def _():
            for p in range(2):
                out_copy(1, p, 0, last).start()

        @pl.when(k == chunks - 1)
        def _():
            for p in range(2):
                out_copy(1, p, last, 8).start()

    def coefficients():
        pltpu.make_async_remote_copy(
            src_ref=eps_all.at[0:4], dst_ref=eps_all.at[0:4], send_sem=es, recv_sem=er,
            **to({"brick": brick_off(1)})
        ).wait()
        for o in range(5):
            eps_rows[2 * o : 2 * o + 2, :] = table_ref[:2, :] if o == 2 else eps_all[o, :2, :]
        here = eps_rows[1:9, :]
        xminus = 0.5 * (here + eps_rows[0:8, :])
        xplus = 0.5 * (here + eps_rows[2:10, :])
        depth = iota((8, plane), 1) & (NZ - 1)
        above = depth < NZ - 1
        below = depth > 0
        yplus = 0.5 * (here + pltpu.roll(here, plane - NZ, 1))
        yminus = 0.5 * (here + pltpu.roll(here, NZ, 1))
        zplus = 0.5 * (here + jnp.where(above, pltpu.roll(here, plane - 1, 1), here))
        zminus = 0.5 * (here + jnp.where(below, pltpu.roll(here, 1, 1), here))
        scale = OMEGA / (xplus + xminus + yplus + yminus + zplus + zminus)
        faces = (
            xminus, xplus, yminus, yplus,
            jnp.where(below, zminus, 0.0), jnp.where(above, zplus, 0.0), FOURPI,
        )
        for n, face in enumerate(faces):
            scaled = scale * face
            for e in range(8):
                coef[n, e] = jnp.broadcast_to(scaled[e : e + 1, :], (8, plane))

    @pl.loop(0, chunks + 6)
    def _(step):
        @pl.when(step < chunks)
        def _():
            send(step)

        @pl.when((step >= 2) & (step < chunks + 2))
        def _():
            join(step - 2)

        @pl.when(step == 3)
        def _():
            coefficients()

        @pl.when((step >= 4) & (step < chunks + 4))
        def _():
            product(step - 4)
            for n in range(4):
                h_copy(step - 4, n).start()

        @pl.when(step >= 6)
        def _():
            sweeps(step - 6)

    def sent(ref, sem, recv_sem):
        pltpu.make_async_remote_copy(
            src_ref=ref, dst_ref=ref, send_sem=sem, recv_sem=recv_sem,
            **to({"brick": brick_off(1)})
        ).wait_send()

    sent(g_buf.at[core, y, pl.ds(1, nz - 1)], zs, zr.at[0])
    sent(g_buf.at[core, pl.ds(0, 3)], ys, yr.at[0, 0])
    sent(g_buf.at[core], cs, cr.at[0])
    sent(out_a, xas, xar.at[0, 0])
    sent(out_c, xcs, xcr.at[0])
    sent(in_h, hs, hr.at[0])
    for which, ref in enumerate((field, result)):
        pltpu.make_async_copy(ref, ref, out_sem.at[which]).wait()


def local(bricks, nx, psi_val, psi_cond, dielectric, point_owner, point_cell):
    nb, _, plane = psi_val.shape
    npts = point_owner.shape[0]
    nz = bricks // (CHIPS_Y * CORES)
    groups = min(4, nz)
    fields = npts // nx
    chunks = fields // 8
    rows = bricks * BLOCK

    def row(values):
        return jnp.pad(values[None, :], ((0, 0), (0, plane - npts))).astype(F32)

    table = jnp.concatenate([dielectric, row(point_owner), row(point_cell)], axis=0)

    vmem = pl.BlockSpec(memory_space=pltpu.VMEM)
    dma = pltpu.SemaphoreType.DMA
    pair, potential = pl.pallas_call(
        functools.partial(kernel, nz, nx),
        out_shape=[jax.ShapeDtypeStruct((fields, 2, plane), F32)] * 2,
        in_specs=[
            vmem, pl.BlockSpec(memory_space=pl.ANY), pl.BlockSpec(memory_space=pl.ANY),
        ],
        out_specs=[pl.BlockSpec(memory_space=pl.ANY)] * 2,
        scratch_shapes=[
            pltpu.VMEM((2, nb // 8, 16, plane), BF16),
            pltpu.VMEM((CORES, CHIPS_Y, nz, BLOCK, LANES), BF16),
            pltpu.VMEM((4 * npts, rows), BF16),
            pltpu.VMEM((4 * npts, LANES), F32),
            pltpu.VMEM((nb, 4 * nb), BF16),
            pltpu.VMEM((nb, 2 * nb), BF16),
            pltpu.VMEM((2, plane, LANES), BF16),
            pltpu.VMEM((2 * nb, LANES), F32),
            pltpu.VMEM((2, 2 * npts, 2 * nb), BF16),
            pltpu.VMEM((2, 2, npts, plane), F32),
            pltpu.VMEM((2, chunks, 16, 2 * plane + LANES), jnp.int16),
            pltpu.VMEM((2, chunks, 16, 2 * plane + LANES), jnp.int16),
            pltpu.VMEM((2, chunks, 16, plane + LANES), jnp.int16),
            pltpu.VMEM((2, chunks, 16, plane + LANES), jnp.int16),
            pltpu.VMEM((5, 4, plane), F32),
            pltpu.VMEM((16, plane), F32),
            pltpu.VMEM((7, 8, 8, plane), F32),
            pltpu.VMEM((chunks, 2, 16, plane // 2 + LANES), jnp.int16),
            pltpu.VMEM((chunks, 6, 16, plane // 2 + LANES), jnp.int16),
            pltpu.VMEM((2, fields, plane), F32),
            pltpu.VMEM((8, 8, plane), F32),
            pltpu.VMEM((8, 8, plane), F32),
            pltpu.VMEM((8, 8, plane), F32),
            pltpu.VMEM((2, fields, plane), F32),
            dma((2,)),
            dma, dma((groups,)),
            dma, dma((groups, 2)),
            dma, dma((groups,)),
            dma, dma((2, chunks)),
            dma, dma((chunks,)),
            dma, dma((chunks,)),
            dma, dma,
            dma((2,)),
        ],
        compiler_params=pltpu.CompilerParams(
            collective_id=0, has_side_effects=True, vmem_limit_bytes=52 << 20
        ),
        cost_estimate=pl.CostEstimate(
            flops=2 * 2 * 2 * npts * 2 * nb * plane,
            bytes_accessed=8 * nb * plane + 16 * fields * plane,
            transcendentals=0,
        ),
    )(
        table, psi_val.reshape(nb // 8, 8, 2, plane), psi_cond.reshape(nb // 8, 8, 2, plane),
    )
    return pair, potential


def solution(mesh):
    return jax.shard_map(
        functools.partial(local, mesh.shape["brick"], mesh.shape["band"]),
        mesh=mesh,
        in_specs=(P("band", "brick", None), P("band", "brick", None), P("brick", None), P(), P()),
        out_specs=(P("band", "brick", None), P("band", "brick", None)),
        check_vma=False,
    )
```

```python
import functools

import jax
import jax.numpy as jnp
from jax import lax
from jax.experimental import pallas as pl
from jax.experimental.pallas import tpu as pltpu
from jax.sharding import PartitionSpec as P

NZ = 64
FOURPI = 12.566370614359172
OMEGA = 0.8

CORES = 2
CHIPS_Y = 4
MOST = 4
BLOCK = 4 * MOST
GROUP = 512
LANES = 128
STEP = 32700.0
CODE = 128.0
MESH = pl.DeviceIdType.MESH
F32 = jnp.float32
BF16 = jnp.bfloat16


def iota(shape, dim):
    return lax.broadcasted_iota(jnp.int32, shape, dim)


def to(device):
    return dict(device_id=device, device_id_type=MESH)


def kernel(
    nz, nx,
    table_ref, val_ref, cond_ref,
    pair_ref, pot_ref,
    x_buf, g_buf, sel, found, spread, fold, pick, taken, z_buf, part, out_a, in_a, out_c, in_c,
    eps_all, eps_rows, coef, out_h, in_h, field, first, second, third, result,
    load_sem, zs, zr, ys, yr, cs, cr, fs, fr, xas, xar, xcs, xcr, hs, hr, es, er, out_sem,
):
    brick = lax.axis_index("brick")
    band = lax.axis_index("band")
    bricks = nz * CHIPS_Y * CORES
    core = lax.rem(brick, CORES)
    y = lax.rem(brick // CORES, CHIPS_Y)
    z = brick // (CORES * CHIPS_Y)
    nb8, _, _, plane = val_ref.shape
    nb = nb8 * 8
    npts = part.shape[2]
    owners, cells = table_ref[2:3, :npts], table_ref[3:4, :npts]
    fields = npts // nx
    chunks = fields // 8
    groups = min(4, nz)
    per = nz // groups
    tiles = plane // LANES
    parts = plane // GROUP

    def brick_at(zz, yy, cc):
        return (zz * CHIPS_Y + yy) * CORES + cc

    def brick_off(o):
        return lax.rem(brick + o + bricks, bricks)

    def band_off(o):
        return lax.rem(band + o, nx)

    barrier = pltpu.get_barrier_semaphore()

    @pl.loop(1, nz)
    def _(dz):
        pl.semaphore_signal(barrier, 1, **to({"brick": brick_at(lax.rem(z + dz, nz), y, core)}))

    same_z = [(dy, dc) for dy in (2, 1, 3, 0) for dc in range(CORES) if (dy, dc) != (0, 0)]

    def at_z(dy, dc):
        return to({"brick": brick_at(z, lax.rem(y + dy, CHIPS_Y), 1 - core if dc else core)})

    for dy, dc in same_z:
        pl.semaphore_signal(barrier, 1, **at_z(dy, dc))
    for dx in (1, 3):
        pl.semaphore_signal(barrier, 1, **to({"band": band_off(dx)}))
    for o in (-2, -1, 1, 2):
        pl.semaphore_signal(barrier, 1, **to({"brick": brick_off(o)}))

    for s, psi in enumerate((val_ref, cond_ref)):
        for i in range(8):
            copy = pltpu.make_async_copy(
                psi.at[:, i], x_buf.at[s, :, 2 * i : 2 * i + 2, :], load_sem.at[s]
            )
            copy.start()

    first_index = iota((npts, npts), 0)
    second_index = iota((npts, npts), 1)
    owner_across = jnp.broadcast_to(owners, (npts, npts))
    owner_down = jnp.sum(
        jnp.where(first_index == second_index, owner_across, 0.0), axis=1, keepdims=True
    )
    same = owner_across == owner_down
    rank_down = jnp.sum(
        jnp.where(same & (second_index < first_index), 1.0, 0.0), axis=1, keepdims=True
    )
    rank_across = jnp.sum(
        jnp.where(same & (first_index < second_index), 1.0, 0.0), axis=0, keepdims=True
    )
    own = owners == brick.astype(F32)
    slot_of = iota((1, LANES), 1) & (MOST - 1)
    slot_cell = jnp.zeros((1, LANES), F32)
    for j in range(MOST):
        cell = jnp.sum(
            jnp.where(own & (rank_across == j), cells, 0.0),
            axis=1, keepdims=True,
        )
        slot_cell = jnp.where(slot_of == j, cell, slot_cell)
    slot_cell = slot_cell.astype(jnp.int32)
    slot_plane = jnp.where(slot_cell >= plane, 1, 0)
    slot_column = slot_cell - slot_plane * plane
    owner_down = owner_down.astype(jnp.int32)
    away = (owner_down >> 3) - z
    away = jnp.where(away < 0, away + nz, away)
    position = jnp.where(away <= nz // 2, 2 * away - 1, 2 * (nz - away))
    position = jnp.where(away == 0, 0, position)
    group_down = jnp.zeros_like(position)
    for g in range(1, groups):
        group_down = group_down + jnp.where(position >= g * per, 1, 0)
    place = ((owner_down & 1) * groups + group_down) * CHIPS_Y + ((owner_down >> 1) & 3)
    place = (place * per + position - group_down * per) * BLOCK + rank_down.astype(jnp.int32)

    fold[...] = jnp.where(iota((nb, 2 * nb), 0) == (iota((nb, 2 * nb), 1) >> 1), 1.0, 0.0).astype(
        BF16
    )
    for s in range(2):
        for n in range(parts):
            hit = (iota((GROUP, LANES), 0) + n * GROUP == slot_column) & (
                (iota((GROUP, LANES), 1) >> 3) == s
            )
            pick[s, n * GROUP : (n + 1) * GROUP, :] = jnp.where(hit, 1.0, 0.0).astype(BF16)

    half = nb // 2
    taken[...] = jnp.zeros_like(taken)
    for s in range(2):
        pltpu.make_async_copy(x_buf.at[s], x_buf.at[s], load_sem.at[s]).wait()
        taken[...] += jnp.dot(
            x_buf[s].reshape(2 * nb, plane), pick[s], preferred_element_type=F32
        )
    keep = (iota((2 * nb, LANES), 0) & 1) == slot_plane
    folded = jnp.dot(
        fold[...], jnp.where(keep, taken[...], 0.0).astype(BF16), preferred_element_type=F32
    )
    halves = [folded[half * i : half * (i + 1), :].T[:BLOCK, :] for i in range(2)]
    mine = jnp.where(((iota((BLOCK, half), 0) >> 2) & 1) == 0, halves[0], halves[1])
    g_buf[core, y, 0] = mine.astype(BF16)

    pl.semaphore_wait(barrier, nz - 1 + len(same_z) + 2 + 4)

    def z_copy(i):
        away = (i + 1) // 2 if i % 2 else -(i // 2)
        return pltpu.make_async_remote_copy(
            src_ref=g_buf.at[core, y, 0], dst_ref=g_buf.at[core, y, i],
            send_sem=zs, recv_sem=zr.at[i // per],
            **to({"brick": brick_at(lax.rem(z - away + nz, nz), y, core)})
        )

    for i in range(1, nz):
        z_copy(i).start()

    for o in (-2, -1, 1, 2):
        copy = pltpu.make_async_remote_copy(
            src_ref=table_ref, dst_ref=eps_all.at[2 - o],
            send_sem=es, recv_sem=er, **to({"brick": brick_off(o)})
        )
        copy.start()

    @pl.loop(0, sel.shape[1] // GROUP)
    def _(n):
        column = iota((npts, GROUP), 1) + n * GROUP
        for q in range(4):
            hit = column == place + q * MOST
            sel[pl.ds(q * npts, npts), pl.ds(pl.multiple_of(n * GROUP, GROUP), GROUP)] = (
                jnp.where(hit, 1.0, 0.0).astype(BF16)
            )

    for p in range(2):
        spread[:, 2 * nb * p : 2 * nb * (p + 1)] = jnp.where(
            iota((nb, 2 * nb), 1) == 2 * iota((nb, 2 * nb), 0) + p, 1.0, 0.0
        ).astype(BF16)

    y_up, y_down = lax.rem(y + 1, CHIPS_Y), lax.rem(y + 3, CHIPS_Y)

    def y_copy(g, way):
        odd = g % 2
        source = y if way < 2 else (y_up if odd else y_down)
        target = (y_up, y_down, y_down if odd else y_up)[way]
        part_of = g_buf.at[core, source, pl.ds(g * per, per)]
        return pltpu.make_async_remote_copy(
            src_ref=part_of, dst_ref=part_of, send_sem=ys,
            recv_sem=yr.at[g, 0 if way == odd else 1],
            **to({"brick": brick_at(z, target, core)})
        )

    def y_arrived(g, n):
        block = g_buf.at[core, pl.ds(0, n + 1), pl.ds(g * per, per)]
        pltpu.make_async_remote_copy(
            src_ref=block, dst_ref=block, send_sem=ys, recv_sem=yr.at[g, n],
            **to({"brick": brick_at(z, y_up, core)})
        ).wait_recv()

    def core_copy(g):
        part_of = g_buf.at[core, :, pl.ds(g * per, per)]
        return pltpu.make_async_remote_copy(
            src_ref=part_of, dst_ref=part_of, send_sem=cs, recv_sem=cr.at[g],
            **to({"brick": brick_at(z, y, 1 - core)})
        )

    columns_of = CHIPS_Y * per * BLOCK

    def find(c, g):
        rows = g_buf[c, :, pl.ds(g * per, per)].reshape(columns_of, LANES)
        start = pl.multiple_of((c * groups + g) * columns_of, columns_of)
        return jnp.dot(sel[:, pl.ds(start, columns_of)], rows, preferred_element_type=F32)

    found[...] = jnp.zeros_like(found)
    far = groups - 1

    def far_copy(dy, dc):
        block = g_buf.at[core, y, pl.ds(far * per, per)]
        return pltpu.make_async_remote_copy(
            src_ref=block, dst_ref=block, send_sem=fs.at[dc], recv_sem=fr.at[dc], **at_z(dy, dc)
        )

    for step in range(groups + 2):
        if step < groups:
            come = g_buf.at[core, y, pl.ds(max(1, step * per), per if step else per - 1)]
            pltpu.make_async_remote_copy(
                src_ref=come, dst_ref=come, send_sem=zs, recv_sem=zr.at[step],
                **to({"brick": brick_at(lax.rem(z + 1, nz), y, core)})
            ).wait_recv()
        if step < far:
            y_copy(step, 0).start()
            y_copy(step, 1).start()
        if step == far:
            for dy, dc in same_z:
                far_copy(dy, dc).start()
        if 1 <= step <= far:
            g = step - 1
            y_arrived(g, 0)
            y_copy(g, 2).start()
        if 2 <= step <= far + 1:
            g = step - 2
            y_arrived(g, 1)
            core_copy(g).start()
            found[...] += find(core, g)
        if 3 <= step <= far + 2:
            g = step - 3
            block = g_buf.at[1 - core, :, pl.ds(g * per, per)]
            pltpu.make_async_remote_copy(
                src_ref=block, dst_ref=block, send_sem=cs, recv_sem=cr.at[g],
                **to({"brick": brick_at(z, y, 1 - core)})
            ).wait_recv()
            found[...] += find(1 - core, g)
    for dc in range(CORES):
        c = 1 - core if dc else core
        block = g_buf.at[c, pl.ds(0, CHIPS_Y - 1 + dc), pl.ds(far * per, per)]
        pltpu.make_async_remote_copy(
            src_ref=block, dst_ref=block, send_sem=fs.at[dc], recv_sem=fr.at[dc], **at_z(1, 0)
        ).wait_recv()
        found[...] += find(c, far)

    for s in range(2):
        at_points = jnp.concatenate(
            [found[(2 * s + i) * npts : (2 * s + i + 1) * npts, :] for i in range(2)], axis=1
        ).astype(BF16)
        wide = jnp.dot(at_points, spread[...], preferred_element_type=F32).astype(BF16)
        for p in range(2):
            z_buf[s, p * npts : (p + 1) * npts, :] = wide[:, 2 * nb * p : 2 * nb * (p + 1)]

    @pl.loop(0, parts)
    def _(n):
        at = pl.ds(pl.multiple_of(n * GROUP, GROUP), GROUP)
        for s in range(2):
            got = jnp.dot(
                z_buf[s], x_buf[s, :, :, at].reshape(2 * nb, GROUP), preferred_element_type=F32
            )
            part[s, :, :, at] = got.reshape(2, npts, GROUP)

    code_lane = iota((16, LANES), 1)

    def lanes_of(n):
        return slice(n * GROUP + LANES * (n >= parts), (n + 1) * GROUP + LANES * (n >= parts))

    def pack(*messages):
        scales = []
        for values_at, target, count in messages:
            most = jnp.zeros((16, LANES), F32)
            for n in range(count):
                peak = jnp.max(jnp.abs(values_at(n)), axis=1, keepdims=True)
                most = jnp.where(code_lane == n, peak, most)
            code = jnp.ceil(jnp.log2(jnp.maximum(most, 1e-30)) * CODE)
            scales.append((code, STEP * jnp.exp2(code * (-1.0 / CODE))))
        for (values_at, target, count), (code, scale) in zip(messages, scales):
            first_of = min(count, parts) * GROUP
            target[:, first_of : first_of + LANES] = code.astype(jnp.int32).astype(jnp.int16)
            for n in range(count):
                whole = jnp.round(values_at(n) * scale[:, n : n + 1])
                target[:, lanes_of(n)] = whole.astype(jnp.int32).astype(jnp.int16)

    def unpacker(source, count):
        first_of = min(count, parts) * GROUP
        codes = source[:, first_of : first_of + LANES].astype(jnp.int32).astype(F32)
        scales = jnp.exp2(codes * (1.0 / CODE)) * (1.0 / STEP)

        def values_at(n):
            got = source[:, lanes_of(n)].astype(jnp.int32).astype(F32)
            return got * scales[:, n : n + 1]

        return values_at

    def held(target, p, k):
        start = pl.multiple_of(target * fields + k * 8, 8)

        def values_at(n):
            at = slice(n * GROUP, (n + 1) * GROUP)
            return jnp.concatenate(
                [part[0, p, pl.ds(start, 8), at], part[1, p, pl.ds(start, 8), at]], axis=0
            )

        return values_at

    up, down, across = band_off(1), band_off(3), band_off(2)
    heading = (up, down)

    pieces = ((0, plane + LANES), (plane + LANES, plane))

    def a_copy(k, way, piece):
        at = pl.ds(*pieces[piece])
        return pltpu.make_async_remote_copy(
            src_ref=out_a.at[way, k, :, at], dst_ref=in_a.at[way, k, :, at],
            send_sem=xas, recv_sem=xar.at[piece, k], **to({"band": heading[way]})
        )

    def c_copy(k, way):
        return pltpu.make_async_remote_copy(
            src_ref=out_c.at[way, k], dst_ref=in_c.at[way, k],
            send_sem=xcs, recv_sem=xcr.at[k], **to({"band": heading[way]})
        )

    def send(k):
        def message(way):
            passed, direct = held(across, way, k), held(heading[way], 1 - way, k)
            return (
                lambda n: passed(n) if n < parts else direct(n - parts),
                out_a.at[way, k], 2 * parts,
            )

        pack(message(0), message(1))
        for piece in range(2):
            for way in range(2):
                a_copy(k, way, piece).start()

    def arrived(k, piece):
        both = in_a.at[:, k, :, pl.ds(*pieces[piece])]
        pltpu.make_async_remote_copy(
            src_ref=both, dst_ref=both, send_sem=xas, recv_sem=xar.at[piece, k],
            **to({"band": up})
        ).wait_recv()

    def join(k):
        arrived(k, 0)
        def message(way):
            mine_at, got_at = held(heading[way], way, k), unpacker(in_a.at[way, k], 2 * parts)
            return lambda n: mine_at(n) + got_at(n), out_c.at[way, k], parts

        pack(message(0), message(1))
        for way in range(2):
            c_copy(k, way).start()

    sides = ((-2, 0, 1, 5), (-1, 0, 2, 3), (1, 0, 2, 1), (2, 1, 1, 0))

    def h_copy(k, n):
        o, source, count, target = sides[n]
        return pltpu.make_async_remote_copy(
            src_ref=out_h.at[k, source : source + count],
            dst_ref=in_h.at[k, target : target + count],
            send_sem=hs, recv_sem=hr.at[k], **to({"brick": brick_off(o)})
        )

    def out_copy(which, p, start, count):
        rows = pl.ds(start, count)
        return pltpu.make_async_copy(
            (field, result)[which].at[p, rows], (pair_ref, pot_ref)[which].at[rows, p, :],
            out_sem.at[which],
        )

    def product(k):
        arrived(k, 1)
        both = in_c.at[:, k]
        pltpu.make_async_remote_copy(
            src_ref=both, dst_ref=both, send_sem=xcs, recv_sem=xcr.at[k], **to({"band": up})
        ).wait_recv()
        rows = pl.ds(pl.multiple_of(k * 8, 8), 8)
        for p in range(2):
            direct = unpacker(in_a.at[1 - p, k], 2 * parts)
            parts_at = (
                held(band, p, k), lambda n: direct(n + parts), unpacker(in_c.at[p, k], parts)
            )
            pairs = []
            for n in range(parts):
                total = sum(values_at(n) for values_at in parts_at)
                pairs.append(total[:8, :] * total[8:, :])
            for n in range(parts):
                field[p, rows, n * GROUP : (n + 1) * GROUP] = pairs[n]

        def message(p):
            def halves(n):
                return jnp.concatenate(
                    [
                        field[p, rows, m * GROUP : (m + 1) * GROUP]
                        for m in (n, n + parts // 2)
                    ],
                    axis=0,
                )

            return halves, out_h.at[k, p], parts // 2

        pack(message(0), message(1))

        @pl.when(k == chunks - 1)
        def _():
            for p in range(2):
                out_copy(0, p, 0, fields).start()

    low_half = iota((8, LANES), 1) < NZ

    def sweep(source, e):
        tile_at = [pl.ds(t * LANES, LANES) for t in range(tiles)]
        swapped = [pltpu.roll(source[e, :, at], NZ, 1) for at in tile_at]
        news = []
        for t, at in enumerate(tile_at):
            v = source[e, :, at]
            before = swapped[(t - 1) % tiles]
            after = swapped[(t + 1) % tiles]
            alone = (1.0 - OMEGA) * v + first[e, :, at]
            along_x = coef[0, e, :, at] * source[e - 1, :, at]
            along_x = along_x + coef[1, e, :, at] * source[e + 1, :, at]
            along_y = coef[2, e, :, at] * jnp.where(low_half, before, swapped[t])
            along_y = along_y + coef[3, e, :, at] * jnp.where(low_half, swapped[t], after)
            along_z = coef[4, e, :, at] * pltpu.roll(v, 1, 1)
            along_z = along_z + coef[5, e, :, at] * pltpu.roll(v, LANES - 1, 1)
            news.append((alone + along_x) + (along_y + along_z))
        return zip(tile_at, news)

    def sweeps(k):
        come = in_h.at[k]
        pltpu.make_async_remote_copy(
            src_ref=come, dst_ref=come, send_sem=hs, recv_sem=hr.at[k],
            **to({"brick": brick_off(1)})
        ).wait_recv()
        rows = pl.ds(pl.multiple_of(k * 8, 8), 8)
        for p in range(2):
            first[3 + p] = coef[6, 3 + p] * field[p, rows, :]

        @pl.loop(0, 6)
        def _(i):
            e = i + 2 * (i // 3)
            halves = unpacker(in_h.at[k, i], parts // 2)
            values = [halves(n) for n in range(parts // 2)]
            for m in range(parts):
                at = slice(m * GROUP, (m + 1) * GROUP)
                half = values[m % (parts // 2)][8 * (m // (parts // 2)) :, :][:8, :]
                first[e, :, at] = coef[6, e, :, at] * half

        @pl.loop(1, 7)
        def _(e):
            for at, new in sweep(first, e):
                second[e, :, at] = new

        @pl.loop(2, 6)
        def _(e):
            for at, new in sweep(second, e):
                third[e, :, at] = new

        @pl.loop(3, 5)
        def _(e):
            for at, new in sweep(third, e):
                result[e - 3, rows, at] = new

        last = 8 * (chunks - 1)

        @pl.when(k == chunks - 2)
        def _():
            for p in range(2):
                out_copy(1, p, 0, last).start()

        @pl.when(k == chunks - 1)
        def _():
            for p in range(2):
                out_copy(1, p, last, 8).start()

    def coefficients():
        pltpu.make_async_remote_copy(
            src_ref=eps_all.at[0:4], dst_ref=eps_all.at[0:4], send_sem=es, recv_sem=er,
            **to({"brick": brick_off(1)})
        ).wait()
        for o in range(5):
            eps_rows[2 * o : 2 * o + 2, :] = table_ref[:2, :] if o == 2 else eps_all[o, :2, :]
        here = eps_rows[1:9, :]
        xminus = 0.5 * (here + eps_rows[0:8, :])
        xplus = 0.5 * (here + eps_rows[2:10, :])
        depth = iota((8, plane), 1) & (NZ - 1)
        above = depth < NZ - 1
        below = depth > 0
        yplus = 0.5 * (here + pltpu.roll(here, plane - NZ, 1))
        yminus = 0.5 * (here + pltpu.roll(here, NZ, 1))
        zplus = 0.5 * (here + jnp.where(above, pltpu.roll(here, plane - 1, 1), here))
        zminus = 0.5 * (here + jnp.where(below, pltpu.roll(here, 1, 1), here))
        scale = OMEGA / (xplus + xminus + yplus + yminus + zplus + zminus)
        faces = (
            xminus, xplus, yminus, yplus,
            jnp.where(below, zminus, 0.0), jnp.where(above, zplus, 0.0), FOURPI,
        )
        for n, face in enumerate(faces):
            scaled = scale * face
            for e in range(8):
                coef[n, e] = jnp.broadcast_to(scaled[e : e + 1, :], (8, plane))

    @pl.loop(0, chunks + 6)
    def _(step):
        @pl.when(step < chunks)
        def _():
            send(step)

        @pl.when((step >= 2) & (step < chunks + 2))
        def _():
            join(step - 2)

        @pl.when(step == 3)
        def _():
            coefficients()

        @pl.when((step >= 4) & (step < chunks + 4))
        def _():
            product(step - 4)
            for n in range(4):
                h_copy(step - 4, n).start()

        @pl.when(step >= 6)
        def _():
            sweeps(step - 6)

    def sent(ref, sem, recv_sem):
        pltpu.make_async_remote_copy(
            src_ref=ref, dst_ref=ref, send_sem=sem, recv_sem=recv_sem,
            **to({"brick": brick_off(1)})
        ).wait_send()

    sent(g_buf.at[core, y, pl.ds(1, nz - 1)], zs, zr.at[0])
    near = pl.ds(0, far * per)
    sent(g_buf.at[core, pl.ds(0, 3), near], ys, yr.at[0, 0])
    sent(g_buf.at[core, :, near], cs, cr.at[0])
    for dc in range(CORES):
        sent(g_buf.at[core, pl.ds(0, 3 + dc), pl.ds(far * per, per)], fs.at[dc], fr.at[dc])
    sent(out_a, xas, xar.at[0, 0])
    sent(out_c, xcs, xcr.at[0])
    sent(in_h, hs, hr.at[0])
    for which, ref in enumerate((field, result)):
        pltpu.make_async_copy(ref, ref, out_sem.at[which]).wait()


def local(bricks, nx, psi_val, psi_cond, dielectric, point_owner, point_cell):
    nb, _, plane = psi_val.shape
    npts = point_owner.shape[0]
    nz = bricks // (CHIPS_Y * CORES)
    groups = min(4, nz)
    fields = npts // nx
    chunks = fields // 8
    rows = bricks * BLOCK

    def row(values):
        return jnp.pad(values[None, :], ((0, 0), (0, plane - npts))).astype(F32)

    table = jnp.concatenate([dielectric, row(point_owner), row(point_cell)], axis=0)

    vmem = pl.BlockSpec(memory_space=pltpu.VMEM)
    dma = pltpu.SemaphoreType.DMA
    pair, potential = pl.pallas_call(
        functools.partial(kernel, nz, nx),
        out_shape=[jax.ShapeDtypeStruct((fields, 2, plane), F32)] * 2,
        in_specs=[
            vmem, pl.BlockSpec(memory_space=pl.ANY), pl.BlockSpec(memory_space=pl.ANY),
        ],
        out_specs=[pl.BlockSpec(memory_space=pl.ANY)] * 2,
        scratch_shapes=[
            pltpu.VMEM((2, nb // 8, 16, plane), BF16),
            pltpu.VMEM((CORES, CHIPS_Y, nz, BLOCK, LANES), BF16),
            pltpu.VMEM((4 * npts, rows), BF16),
            pltpu.VMEM((4 * npts, LANES), F32),
            pltpu.VMEM((nb, 4 * nb), BF16),
            pltpu.VMEM((nb, 2 * nb), BF16),
            pltpu.VMEM((2, plane, LANES), BF16),
            pltpu.VMEM((2 * nb, LANES), F32),
            pltpu.VMEM((2, 2 * npts, 2 * nb), BF16),
            pltpu.VMEM((2, 2, npts, plane), F32),
            pltpu.VMEM((2, chunks, 16, 2 * plane + LANES), jnp.int16),
            pltpu.VMEM((2, chunks, 16, 2 * plane + LANES), jnp.int16),
            pltpu.VMEM((2, chunks, 16, plane + LANES), jnp.int16),
            pltpu.VMEM((2, chunks, 16, plane + LANES), jnp.int16),
            pltpu.VMEM((5, 4, plane), F32),
            pltpu.VMEM((16, plane), F32),
            pltpu.VMEM((7, 8, 8, plane), F32),
            pltpu.VMEM((chunks, 2, 16, plane // 2 + LANES), jnp.int16),
            pltpu.VMEM((chunks, 6, 16, plane // 2 + LANES), jnp.int16),
            pltpu.VMEM((2, fields, plane), F32),
            pltpu.VMEM((8, 8, plane), F32),
            pltpu.VMEM((8, 8, plane), F32),
            pltpu.VMEM((8, 8, plane), F32),
            pltpu.VMEM((2, fields, plane), F32),
            dma((2,)),
            dma, dma((groups,)),
            dma, dma((groups, 2)),
            dma, dma((groups,)),
            dma((CORES,)), dma((CORES,)),
            dma, dma((2, chunks)),
            dma, dma((chunks,)),
            dma, dma((chunks,)),
            dma, dma,
            dma((2,)),
        ],
        compiler_params=pltpu.CompilerParams(
            collective_id=0, has_side_effects=True, vmem_limit_bytes=52 << 20
        ),
        cost_estimate=pl.CostEstimate(
            flops=2 * 2 * 2 * npts * 2 * nb * plane,
            bytes_accessed=8 * nb * plane + 16 * fields * plane,
            transcendentals=0,
        ),
    )(
        table, psi_val.reshape(nb // 8, 8, 2, plane), psi_cond.reshape(nb // 8, 8, 2, plane),
    )
    return pair, potential


def solution(mesh):
    return jax.shard_map(
        functools.partial(local, mesh.shape["brick"], mesh.shape["band"]),
        mesh=mesh,
        in_specs=(P("band", "brick", None), P("band", "brick", None), P("brick", None), P(), P()),
        out_specs=(P("band", "brick", None), P("band", "brick", None)),
        check_vma=False,
    )
```

```python
import functools

import jax
import jax.numpy as jnp
from jax import lax
from jax.experimental import pallas as pl
from jax.experimental.pallas import tpu as pltpu
from jax.sharding import PartitionSpec as P

NZ = 64
FOURPI = 12.566370614359172
OMEGA = 0.8

CORES = 2
CHIPS_Y = 4
MOST = 4
BLOCK = 4 * MOST
GROUP = 512
LANES = 128
STEP = 32700.0
CODE = 128.0
MESH = pl.DeviceIdType.MESH
F32 = jnp.float32
BF16 = jnp.bfloat16


def iota(shape, dim):
    return lax.broadcasted_iota(jnp.int32, shape, dim)


def to(device):
    return dict(device_id=device, device_id_type=MESH)


def kernel(
    nz, nx,
    table_ref, val_ref, cond_ref,
    pair_ref, pot_ref,
    x_buf, g_buf, sel, found, spread, fold, pick, taken, z_buf, part, out_a, in_a, out_c, in_c,
    eps_all, eps_rows, coef, out_h, in_h, field, first, second, third, result,
    load_sem, zs, zr, ys, yr, cs, cr, fs, fr, xas, xar, xcs, xcr, hs, hr, es, er, out_sem,
):
    brick = lax.axis_index("brick")
    band = lax.axis_index("band")
    bricks = nz * CHIPS_Y * CORES
    core = lax.rem(brick, CORES)
    y = lax.rem(brick // CORES, CHIPS_Y)
    z = brick // (CORES * CHIPS_Y)
    nb8, _, _, plane = val_ref.shape
    nb = nb8 * 8
    npts = part.shape[2]
    owners, cells = table_ref[2:3, :npts], table_ref[3:4, :npts]
    fields = npts // nx
    chunks = fields // 8
    groups = min(4, nz)
    per = nz // groups
    tiles = plane // LANES
    parts = plane // GROUP

    def brick_at(zz, yy, cc):
        return (zz * CHIPS_Y + yy) * CORES + cc

    def brick_off(o):
        return lax.rem(brick + o + bricks, bricks)

    def band_off(o):
        return lax.rem(band + o, nx)

    barrier = pltpu.get_barrier_semaphore()

    @pl.loop(1, nz)
    def _(dz):
        pl.semaphore_signal(barrier, 1, **to({"brick": brick_at(lax.rem(z + dz, nz), y, core)}))

    same_z = [(dy, dc) for dy in (2, 1, 3, 0) for dc in range(CORES) if (dy, dc) != (0, 0)]

    def at_z(dy, dc):
        return to({"brick": brick_at(z, lax.rem(y + dy, CHIPS_Y), 1 - core if dc else core)})

    for dy, dc in same_z:
        pl.semaphore_signal(barrier, 1, **at_z(dy, dc))
    for dx in (1, 3):
        pl.semaphore_signal(barrier, 1, **to({"band": band_off(dx)}))
    for o in (-2, -1, 1, 2):
        pl.semaphore_signal(barrier, 1, **to({"brick": brick_off(o)}))

    for s, psi in enumerate((val_ref, cond_ref)):
        for i in range(8):
            copy = pltpu.make_async_copy(
                psi.at[:, i], x_buf.at[s, :, 2 * i : 2 * i + 2, :], load_sem.at[s]
            )
            copy.start()

    first_index = iota((npts, npts), 0)
    second_index = iota((npts, npts), 1)
    owner_across = jnp.broadcast_to(owners, (npts, npts))
    owner_down = jnp.sum(
        jnp.where(first_index == second_index, owner_across, 0.0), axis=1, keepdims=True
    )
    same = owner_across == owner_down
    rank_down = jnp.sum(
        jnp.where(same & (second_index < first_index), 1.0, 0.0), axis=1, keepdims=True
    )
    rank_across = jnp.sum(
        jnp.where(same & (first_index < second_index), 1.0, 0.0), axis=0, keepdims=True
    )
    own = owners == brick.astype(F32)
    slot_of = iota((1, LANES), 1) & (MOST - 1)
    slot_cell = jnp.zeros((1, LANES), F32)
    for j in range(MOST):
        cell = jnp.sum(
            jnp.where(own & (rank_across == j), cells, 0.0),
            axis=1, keepdims=True,
        )
        slot_cell = jnp.where(slot_of == j, cell, slot_cell)
    slot_cell = slot_cell.astype(jnp.int32)
    slot_plane = jnp.where(slot_cell >= plane, 1, 0)
    slot_column = slot_cell - slot_plane * plane
    owner_down = owner_down.astype(jnp.int32)
    away = (owner_down >> 3) - z
    away = jnp.where(away < 0, away + nz, away)
    position = jnp.where(away <= nz // 2, 2 * away - 1, 2 * (nz - away))
    position = jnp.where(away == 0, 0, position)
    group_down = jnp.zeros_like(position)
    for g in range(1, groups):
        group_down = group_down + jnp.where(position >= g * per, 1, 0)
    place = ((owner_down & 1) * groups + group_down) * CHIPS_Y + ((owner_down >> 1) & 3)
    place = (place * per + position - group_down * per) * BLOCK + rank_down.astype(jnp.int32)

    fold[...] = jnp.where(iota((nb, 2 * nb), 0) == (iota((nb, 2 * nb), 1) >> 1), 1.0, 0.0).astype(
        BF16
    )
    for s in range(2):
        for n in range(parts):
            hit = (iota((GROUP, LANES), 0) + n * GROUP == slot_column) & (
                (iota((GROUP, LANES), 1) >> 3) == s
            )
            pick[s, n * GROUP : (n + 1) * GROUP, :] = jnp.where(hit, 1.0, 0.0).astype(BF16)

    half = nb // 2
    taken[...] = jnp.zeros_like(taken)
    for s in range(2):
        pltpu.make_async_copy(x_buf.at[s], x_buf.at[s], load_sem.at[s]).wait()
        taken[...] += jnp.dot(
            x_buf[s].reshape(2 * nb, plane), pick[s], preferred_element_type=F32
        )
    keep = (iota((2 * nb, LANES), 0) & 1) == slot_plane
    folded = jnp.dot(
        fold[...], jnp.where(keep, taken[...], 0.0).astype(BF16), preferred_element_type=F32
    )
    halves = [folded[half * i : half * (i + 1), :].T[:BLOCK, :] for i in range(2)]
    mine = jnp.where(((iota((BLOCK, half), 0) >> 2) & 1) == 0, halves[0], halves[1])
    g_buf[core, y, 0] = mine.astype(BF16)

    pl.semaphore_wait(barrier, nz - 1 + len(same_z) + 2 + 4)

    def z_copy(i):
        away = (i + 1) // 2 if i % 2 else -(i // 2)
        return pltpu.make_async_remote_copy(
            src_ref=g_buf.at[core, y, 0], dst_ref=g_buf.at[core, y, i],
            send_sem=zs, recv_sem=zr.at[i // per],
            **to({"brick": brick_at(lax.rem(z - away + nz, nz), y, core)})
        )

    for i in range(1, nz):
        z_copy(i).start()

    for o in (-2, -1, 1, 2):
        copy = pltpu.make_async_remote_copy(
            src_ref=table_ref, dst_ref=eps_all.at[2 - o],
            send_sem=es, recv_sem=er, **to({"brick": brick_off(o)})
        )
        copy.start()

    @pl.loop(0, sel.shape[1] // GROUP)
    def _(n):
        column = iota((npts, GROUP), 1) + n * GROUP
        for q in range(4):
            hit = column == place + q * MOST
            sel[pl.ds(q * npts, npts), pl.ds(pl.multiple_of(n * GROUP, GROUP), GROUP)] = (
                jnp.where(hit, 1.0, 0.0).astype(BF16)
            )

    for p in range(2):
        spread[:, 2 * nb * p : 2 * nb * (p + 1)] = jnp.where(
            iota((nb, 2 * nb), 1) == 2 * iota((nb, 2 * nb), 0) + p, 1.0, 0.0
        ).astype(BF16)

    y_up, y_down = lax.rem(y + 1, CHIPS_Y), lax.rem(y + 3, CHIPS_Y)

    def y_copy(g, way):
        on = way == 2 and g == 0
        source = y_down if on else y
        target = (y_up, y_down, y_up if on else lax.rem(y + 2, CHIPS_Y))[way]
        part_of = g_buf.at[core, source, pl.ds(g * per, per)]
        return pltpu.make_async_remote_copy(
            src_ref=part_of, dst_ref=part_of, send_sem=ys,
            recv_sem=yr.at[g, 0 if (g, way) == (0, 0) else 1],
            **to({"brick": brick_at(z, target, core)})
        )

    def y_arrived(g, n):
        block = g_buf.at[core, pl.ds(0, 1 if n == 0 else 2 if g == 0 else 3), pl.ds(g * per, per)]
        pltpu.make_async_remote_copy(
            src_ref=block, dst_ref=block, send_sem=ys, recv_sem=yr.at[g, n],
            **to({"brick": brick_at(z, y_up, core)})
        ).wait_recv()

    def core_copy(g):
        part_of = g_buf.at[core, :, pl.ds(g * per, per)]
        return pltpu.make_async_remote_copy(
            src_ref=part_of, dst_ref=part_of, send_sem=cs, recv_sem=cr.at[g],
            **to({"brick": brick_at(z, y, 1 - core)})
        )

    columns_of = CHIPS_Y * per * BLOCK

    def find(c, g):
        rows = g_buf[c, :, pl.ds(g * per, per)].reshape(columns_of, LANES)
        start = pl.multiple_of((c * groups + g) * columns_of, columns_of)
        return jnp.dot(sel[:, pl.ds(start, columns_of)], rows, preferred_element_type=F32)

    found[...] = jnp.zeros_like(found)
    far = groups - 1

    def far_copy(dy, dc):
        block = g_buf.at[core, y, pl.ds(far * per, per)]
        return pltpu.make_async_remote_copy(
            src_ref=block, dst_ref=block, send_sem=fs.at[dc], recv_sem=fr.at[dc], **at_z(dy, dc)
        )

    for step in range(groups + 2):
        if step < groups:
            come = g_buf.at[core, y, pl.ds(max(1, step * per), per if step else per - 1)]
            pltpu.make_async_remote_copy(
                src_ref=come, dst_ref=come, send_sem=zs, recv_sem=zr.at[step],
                **to({"brick": brick_at(lax.rem(z + 1, nz), y, core)})
            ).wait_recv()
        if step < far:
            for way in (0, 1) if step == 0 else (2, 0, 1):
                y_copy(step, way).start()
        if step == far:
            for dy, dc in same_z:
                far_copy(dy, dc).start()
        if step == 1:
            y_arrived(0, 0)
            y_copy(0, 2).start()
        if 2 <= step <= far + 1:
            g = step - 2
            y_arrived(g, 1)
            core_copy(g).start()
            found[...] += find(core, g)
        if 3 <= step <= far + 2:
            g = step - 3
            block = g_buf.at[1 - core, :, pl.ds(g * per, per)]
            pltpu.make_async_remote_copy(
                src_ref=block, dst_ref=block, send_sem=cs, recv_sem=cr.at[g],
                **to({"brick": brick_at(z, y, 1 - core)})
            ).wait_recv()
            found[...] += find(1 - core, g)
    for dc in range(CORES):
        c = 1 - core if dc else core
        block = g_buf.at[c, pl.ds(0, CHIPS_Y - 1 + dc), pl.ds(far * per, per)]
        pltpu.make_async_remote_copy(
            src_ref=block, dst_ref=block, send_sem=fs.at[dc], recv_sem=fr.at[dc], **at_z(1, 0)
        ).wait_recv()
        found[...] += find(c, far)

    for s in range(2):
        at_points = jnp.concatenate(
            [found[(2 * s + i) * npts : (2 * s + i + 1) * npts, :] for i in range(2)], axis=1
        ).astype(BF16)
        wide = jnp.dot(at_points, spread[...], preferred_element_type=F32).astype(BF16)
        for p in range(2):
            z_buf[s, p * npts : (p + 1) * npts, :] = wide[:, 2 * nb * p : 2 * nb * (p + 1)]

    @pl.loop(0, parts)
    def _(n):
        at = pl.ds(pl.multiple_of(n * GROUP, GROUP), GROUP)
        for s in range(2):
            got = jnp.dot(
                z_buf[s], x_buf[s, :, :, at].reshape(2 * nb, GROUP), preferred_element_type=F32
            )
            part[s, :, :, at] = got.reshape(2, npts, GROUP)

    code_lane = iota((16, LANES), 1)

    def lanes_of(n):
        return slice(n * GROUP + LANES * (n >= parts), (n + 1) * GROUP + LANES * (n >= parts))

    def pack(*messages):
        scales = []
        for values_at, target, count in messages:
            most = jnp.zeros((16, LANES), F32)
            for n in range(count):
                peak = jnp.max(jnp.abs(values_at(n)), axis=1, keepdims=True)
                most = jnp.where(code_lane == n, peak, most)
            code = jnp.ceil(jnp.log2(jnp.maximum(most, 1e-30)) * CODE)
            scales.append((code, STEP * jnp.exp2(code * (-1.0 / CODE))))
        for (values_at, target, count), (code, scale) in zip(messages, scales):
            first_of = min(count, parts) * GROUP
            target[:, first_of : first_of + LANES] = code.astype(jnp.int32).astype(jnp.int16)
            for n in range(count):
                whole = jnp.round(values_at(n) * scale[:, n : n + 1])
                target[:, lanes_of(n)] = whole.astype(jnp.int32).astype(jnp.int16)

    def unpacker(source, count):
        first_of = min(count, parts) * GROUP
        codes = source[:, first_of : first_of + LANES].astype(jnp.int32).astype(F32)
        scales = jnp.exp2(codes * (1.0 / CODE)) * (1.0 / STEP)

        def values_at(n):
            got = source[:, lanes_of(n)].astype(jnp.int32).astype(F32)
            return got * scales[:, n : n + 1]

        return values_at

    def held(target, p, k):
        start = pl.multiple_of(target * fields + k * 8, 8)

        def values_at(n):
            at = slice(n * GROUP, (n + 1) * GROUP)
            return jnp.concatenate(
                [part[0, p, pl.ds(start, 8), at], part[1, p, pl.ds(start, 8), at]], axis=0
            )

        return values_at

    up, down, across = band_off(1), band_off(3), band_off(2)
    heading = (up, down)

    pieces = ((0, plane + LANES), (plane + LANES, plane))

    def a_copy(k, way, piece):
        at = pl.ds(*pieces[piece])
        return pltpu.make_async_remote_copy(
            src_ref=out_a.at[way, k, :, at], dst_ref=in_a.at[way, k, :, at],
            send_sem=xas, recv_sem=xar.at[piece, k], **to({"band": heading[way]})
        )

    def c_copy(k, way):
        return pltpu.make_async_remote_copy(
            src_ref=out_c.at[way, k], dst_ref=in_c.at[way, k],
            send_sem=xcs, recv_sem=xcr.at[k], **to({"band": heading[way]})
        )

    def send(k):
        def message(way):
            passed, direct = held(across, way, k), held(heading[way], 1 - way, k)
            return (
                lambda n: passed(n) if n < parts else direct(n - parts),
                out_a.at[way, k], 2 * parts,
            )

        pack(message(0), message(1))
        for piece in range(2):
            for way in range(2):
                a_copy(k, way, piece).start()

    def arrived(k, piece):
        both = in_a.at[:, k, :, pl.ds(*pieces[piece])]
        pltpu.make_async_remote_copy(
            src_ref=both, dst_ref=both, send_sem=xas, recv_sem=xar.at[piece, k],
            **to({"band": up})
        ).wait_recv()

    def join(k):
        arrived(k, 0)
        def message(way):
            mine_at, got_at = held(heading[way], way, k), unpacker(in_a.at[way, k], 2 * parts)
            return lambda n: mine_at(n) + got_at(n), out_c.at[way, k], parts

        pack(message(0), message(1))
        for way in range(2):
            c_copy(k, way).start()

    sides = ((-2, 0, 1, 5), (-1, 0, 2, 3), (1, 0, 2, 1), (2, 1, 1, 0))

    def h_copy(k, n):
        o, source, count, target = sides[n]
        return pltpu.make_async_remote_copy(
            src_ref=out_h.at[k, source : source + count],
            dst_ref=in_h.at[k, target : target + count],
            send_sem=hs, recv_sem=hr.at[k], **to({"brick": brick_off(o)})
        )

    def out_copy(which, p, start, count):
        rows = pl.ds(start, count)
        return pltpu.make_async_copy(
            (field, result)[which].at[p, rows], (pair_ref, pot_ref)[which].at[rows, p, :],
            out_sem.at[which],
        )

    def product(k):
        arrived(k, 1)
        both = in_c.at[:, k]
        pltpu.make_async_remote_copy(
            src_ref=both, dst_ref=both, send_sem=xcs, recv_sem=xcr.at[k], **to({"band": up})
        ).wait_recv()
        rows = pl.ds(pl.multiple_of(k * 8, 8), 8)
        for p in range(2):
            direct = unpacker(in_a.at[1 - p, k], 2 * parts)
            parts_at = (
                held(band, p, k), lambda n: direct(n + parts), unpacker(in_c.at[p, k], parts)
            )
            pairs = []
            for n in range(parts):
                total = sum(values_at(n) for values_at in parts_at)
                pairs.append(total[:8, :] * total[8:, :])
            for n in range(parts):
                field[p, rows, n * GROUP : (n + 1) * GROUP] = pairs[n]

        def message(p):
            def halves(n):
                return jnp.concatenate(
                    [
                        field[p, rows, m * GROUP : (m + 1) * GROUP]
                        for m in (n, n + parts // 2)
                    ],
                    axis=0,
                )

            return halves, out_h.at[k, p], parts // 2

        pack(message(0), message(1))

        @pl.when(k == chunks - 1)
        def _():
            for p in range(2):
                out_copy(0, p, 0, fields).start()

    low_half = iota((8, LANES), 1) < NZ

    def sweep(source, e):
        tile_at = [pl.ds(t * LANES, LANES) for t in range(tiles)]
        swapped = [pltpu.roll(source[e, :, at], NZ, 1) for at in tile_at]
        news = []
        for t, at in enumerate(tile_at):
            v = source[e, :, at]
            before = swapped[(t - 1) % tiles]
            after = swapped[(t + 1) % tiles]
            alone = (1.0 - OMEGA) * v + first[e, :, at]
            along_x = coef[0, e, :, at] * source[e - 1, :, at]
            along_x = along_x + coef[1, e, :, at] * source[e + 1, :, at]
            along_y = coef[2, e, :, at] * jnp.where(low_half, before, swapped[t])
            along_y = along_y + coef[3, e, :, at] * jnp.where(low_half, swapped[t], after)
            along_z = coef[4, e, :, at] * pltpu.roll(v, 1, 1)
            along_z = along_z + coef[5, e, :, at] * pltpu.roll(v, LANES - 1, 1)
            news.append((alone + along_x) + (along_y + along_z))
        return zip(tile_at, news)

    def sweeps(k):
        come = in_h.at[k]
        pltpu.make_async_remote_copy(
            src_ref=come, dst_ref=come, send_sem=hs, recv_sem=hr.at[k],
            **to({"brick": brick_off(1)})
        ).wait_recv()
        rows = pl.ds(pl.multiple_of(k * 8, 8), 8)
        for p in range(2):
            first[3 + p] = coef[6, 3 + p] * field[p, rows, :]

        @pl.loop(0, 6)
        def _(i):
            e = i + 2 * (i // 3)
            halves = unpacker(in_h.at[k, i], parts // 2)
            values = [halves(n) for n in range(parts // 2)]
            for m in range(parts):
                at = slice(m * GROUP, (m + 1) * GROUP)
                half = values[m % (parts // 2)][8 * (m // (parts // 2)) :, :][:8, :]
                first[e, :, at] = coef[6, e, :, at] * half

        @pl.loop(1, 7)
        def _(e):
            for at, new in sweep(first, e):
                second[e, :, at] = new

        @pl.loop(2, 6)
        def _(e):
            for at, new in sweep(second, e):
                third[e, :, at] = new

        @pl.loop(3, 5)
        def _(e):
            for at, new in sweep(third, e):
                result[e - 3, rows, at] = new

        last = 8 * (chunks - 1)

        @pl.when(k == chunks - 2)
        def _():
            for p in range(2):
                out_copy(1, p, 0, last).start()

        @pl.when(k == chunks - 1)
        def _():
            for p in range(2):
                out_copy(1, p, last, 8).start()

    def coefficients():
        pltpu.make_async_remote_copy(
            src_ref=eps_all.at[0:4], dst_ref=eps_all.at[0:4], send_sem=es, recv_sem=er,
            **to({"brick": brick_off(1)})
        ).wait()
        for o in range(5):
            eps_rows[2 * o : 2 * o + 2, :] = table_ref[:2, :] if o == 2 else eps_all[o, :2, :]
        here = eps_rows[1:9, :]
        xminus = 0.5 * (here + eps_rows[0:8, :])
        xplus = 0.5 * (here + eps_rows[2:10, :])
        depth = iota((8, plane), 1) & (NZ - 1)
        above = depth < NZ - 1
        below = depth > 0
        yplus = 0.5 * (here + pltpu.roll(here, plane - NZ, 1))
        yminus = 0.5 * (here + pltpu.roll(here, NZ, 1))
        zplus = 0.5 * (here + jnp.where(above, pltpu.roll(here, plane - 1, 1), here))
        zminus = 0.5 * (here + jnp.where(below, pltpu.roll(here, 1, 1), here))
        scale = OMEGA / (xplus + xminus + yplus + yminus + zplus + zminus)
        faces = (
            xminus, xplus, yminus, yplus,
            jnp.where(below, zminus, 0.0), jnp.where(above, zplus, 0.0), FOURPI,
        )
        for n, face in enumerate(faces):
            scaled = scale * face
            for e in range(8):
                coef[n, e] = jnp.broadcast_to(scaled[e : e + 1, :], (8, plane))

    @pl.loop(0, chunks + 6)
    def _(step):
        @pl.when(step < chunks)
        def _():
            send(step)

        @pl.when((step >= 2) & (step < chunks + 2))
        def _():
            join(step - 2)

        @pl.when(step == 3)
        def _():
            coefficients()

        @pl.when((step >= 4) & (step < chunks + 4))
        def _():
            product(step - 4)
            for n in range(4):
                h_copy(step - 4, n).start()

        @pl.when(step >= 6)
        def _():
            sweeps(step - 6)

    def sent(ref, sem, recv_sem):
        pltpu.make_async_remote_copy(
            src_ref=ref, dst_ref=ref, send_sem=sem, recv_sem=recv_sem,
            **to({"brick": brick_off(1)})
        ).wait_send()

    sent(g_buf.at[core, y, pl.ds(1, nz - 1)], zs, zr.at[0])
    near = pl.ds(0, far * per)
    sent(g_buf.at[core, pl.ds(0, 3), near], ys, yr.at[0, 0])
    sent(g_buf.at[core, :, near], cs, cr.at[0])
    for dc in range(CORES):
        sent(g_buf.at[core, pl.ds(0, 3 + dc), pl.ds(far * per, per)], fs.at[dc], fr.at[dc])
    sent(out_a, xas, xar.at[0, 0])
    sent(out_c, xcs, xcr.at[0])
    sent(in_h, hs, hr.at[0])
    for which, ref in enumerate((field, result)):
        pltpu.make_async_copy(ref, ref, out_sem.at[which]).wait()


def local(bricks, nx, psi_val, psi_cond, dielectric, point_owner, point_cell):
    nb, _, plane = psi_val.shape
    npts = point_owner.shape[0]
    nz = bricks // (CHIPS_Y * CORES)
    groups = min(4, nz)
    fields = npts // nx
    chunks = fields // 8
    rows = bricks * BLOCK

    def row(values):
        return jnp.pad(values[None, :], ((0, 0), (0, plane - npts))).astype(F32)

    table = jnp.concatenate([dielectric, row(point_owner), row(point_cell)], axis=0)

    vmem = pl.BlockSpec(memory_space=pltpu.VMEM)
    dma = pltpu.SemaphoreType.DMA
    pair, potential = pl.pallas_call(
        functools.partial(kernel, nz, nx),
        out_shape=[jax.ShapeDtypeStruct((fields, 2, plane), F32)] * 2,
        in_specs=[
            vmem, pl.BlockSpec(memory_space=pl.ANY), pl.BlockSpec(memory_space=pl.ANY),
        ],
        out_specs=[pl.BlockSpec(memory_space=pl.ANY)] * 2,
        scratch_shapes=[
            pltpu.VMEM((2, nb // 8, 16, plane), BF16),
            pltpu.VMEM((CORES, CHIPS_Y, nz, BLOCK, LANES), BF16),
            pltpu.VMEM((4 * npts, rows), BF16),
            pltpu.VMEM((4 * npts, LANES), F32),
            pltpu.VMEM((nb, 4 * nb), BF16),
            pltpu.VMEM((nb, 2 * nb), BF16),
            pltpu.VMEM((2, plane, LANES), BF16),
            pltpu.VMEM((2 * nb, LANES), F32),
            pltpu.VMEM((2, 2 * npts, 2 * nb), BF16),
            pltpu.VMEM((2, 2, npts, plane), F32),
            pltpu.VMEM((2, chunks, 16, 2 * plane + LANES), jnp.int16),
            pltpu.VMEM((2, chunks, 16, 2 * plane + LANES), jnp.int16),
            pltpu.VMEM((2, chunks, 16, plane + LANES), jnp.int16),
            pltpu.VMEM((2, chunks, 16, plane + LANES), jnp.int16),
            pltpu.VMEM((5, 4, plane), F32),
            pltpu.VMEM((16, plane), F32),
            pltpu.VMEM((7, 8, 8, plane), F32),
            pltpu.VMEM((chunks, 2, 16, plane // 2 + LANES), jnp.int16),
            pltpu.VMEM((chunks, 6, 16, plane // 2 + LANES), jnp.int16),
            pltpu.VMEM((2, fields, plane), F32),
            pltpu.VMEM((8, 8, plane), F32),
            pltpu.VMEM((8, 8, plane), F32),
            pltpu.VMEM((8, 8, plane), F32),
            pltpu.VMEM((2, fields, plane), F32),
            dma((2,)),
            dma, dma((groups,)),
            dma, dma((groups, 2)),
            dma, dma((groups,)),
            dma((CORES,)), dma((CORES,)),
            dma, dma((2, chunks)),
            dma, dma((chunks,)),
            dma, dma((chunks,)),
            dma, dma,
            dma((2,)),
        ],
        compiler_params=pltpu.CompilerParams(
            collective_id=0, has_side_effects=True, vmem_limit_bytes=52 << 20
        ),
        cost_estimate=pl.CostEstimate(
            flops=2 * 2 * 2 * npts * 2 * nb * plane,
            bytes_accessed=8 * nb * plane + 16 * fields * plane,
            transcendentals=0,
        ),
    )(
        table, psi_val.reshape(nb // 8, 8, 2, plane), psi_cond.reshape(nb // 8, 8, 2, plane),
    )
    return pair, potential


def solution(mesh):
    return jax.shard_map(
        functools.partial(local, mesh.shape["brick"], mesh.shape["band"]),
        mesh=mesh,
        in_specs=(P("band", "brick", None), P("band", "brick", None), P("brick", None), P(), P()),
        out_specs=(P("band", "brick", None), P("band", "brick", None)),
        check_vma=False,
    )
```

```python
import functools

import jax
import jax.numpy as jnp
from jax import lax
from jax.experimental import pallas as pl
from jax.experimental.pallas import tpu as pltpu
from jax.sharding import PartitionSpec as P

NZ = 64
FOURPI = 12.566370614359172
OMEGA = 0.8

CORES = 2
CHIPS_Y = 4
MOST = 4
BLOCK = 4 * MOST
GROUP = 512
LANES = 128
STEP = 32700.0
CODE = 128.0
MESH = pl.DeviceIdType.MESH
F32 = jnp.float32
BF16 = jnp.bfloat16


def iota(shape, dim):
    return lax.broadcasted_iota(jnp.int32, shape, dim)


def to(device):
    return dict(device_id=device, device_id_type=MESH)


def kernel(
    nz, nx,
    table_ref, val_ref, cond_ref,
    pair_ref, pot_ref,
    x_buf, g_buf, sel, found, spread, fold, pick, taken, z_buf, part, out_a, in_a, out_c, in_c,
    eps_all, eps_rows, coef, out_h, in_h, field, first, second, third, result,
    load_sem, zs, zr, ys, yr, cs, cr, fs, fr, xas, xar, xcs, xcr, hs, hr, es, er, out_sem,
):
    brick = lax.axis_index("brick")
    band = lax.axis_index("band")
    bricks = nz * CHIPS_Y * CORES
    core = lax.rem(brick, CORES)
    y = lax.rem(brick // CORES, CHIPS_Y)
    z = brick // (CORES * CHIPS_Y)
    nb8, _, _, plane = val_ref.shape
    nb = nb8 * 8
    npts = part.shape[2]
    owners, cells = table_ref[2:3, :npts], table_ref[3:4, :npts]
    fields = npts // nx
    chunks = fields // 8
    groups = min(4, nz)
    per = nz // groups
    tiles = plane // LANES
    parts = plane // GROUP

    def brick_at(zz, yy, cc):
        return (zz * CHIPS_Y + yy) * CORES + cc

    def brick_off(o):
        return lax.rem(brick + o + bricks, bricks)

    def band_off(o):
        return lax.rem(band + o, nx)

    barrier = pltpu.get_barrier_semaphore()

    @pl.loop(1, nz)
    def _(dz):
        pl.semaphore_signal(barrier, 1, **to({"brick": brick_at(lax.rem(z + dz, nz), y, core)}))

    same_z = [(dy, dc) for dy in (2, 1, 3, 0) for dc in range(CORES) if (dy, dc) != (0, 0)]

    def at_z(dy, dc):
        return to({"brick": brick_at(z, lax.rem(y + dy, CHIPS_Y), 1 - core if dc else core)})

    for dy, dc in same_z:
        pl.semaphore_signal(barrier, 1, **at_z(dy, dc))
    for dx in (1, 3):
        pl.semaphore_signal(barrier, 1, **to({"band": band_off(dx)}))
    for o in (-2, -1, 1, 2):
        pl.semaphore_signal(barrier, 1, **to({"brick": brick_off(o)}))

    for s, psi in enumerate((val_ref, cond_ref)):
        for i in range(8):
            copy = pltpu.make_async_copy(
                psi.at[:, i], x_buf.at[s, :, 2 * i : 2 * i + 2, :], load_sem.at[s]
            )
            copy.start()

    first_index = iota((npts, npts), 0)
    second_index = iota((npts, npts), 1)
    owner_across = jnp.broadcast_to(owners, (npts, npts))
    owner_down = jnp.sum(
        jnp.where(first_index == second_index, owner_across, 0.0), axis=1, keepdims=True
    )
    same = owner_across == owner_down
    rank_down = jnp.sum(
        jnp.where(same & (second_index < first_index), 1.0, 0.0), axis=1, keepdims=True
    )
    rank_across = jnp.sum(
        jnp.where(same & (first_index < second_index), 1.0, 0.0), axis=0, keepdims=True
    )
    own = owners == brick.astype(F32)
    slot_of = iota((1, LANES), 1) & (MOST - 1)
    slot_cell = jnp.zeros((1, LANES), F32)
    for j in range(MOST):
        cell = jnp.sum(
            jnp.where(own & (rank_across == j), cells, 0.0),
            axis=1, keepdims=True,
        )
        slot_cell = jnp.where(slot_of == j, cell, slot_cell)
    slot_cell = slot_cell.astype(jnp.int32)
    slot_plane = jnp.where(slot_cell >= plane, 1, 0)
    slot_column = slot_cell - slot_plane * plane
    owner_down = owner_down.astype(jnp.int32)
    away = (owner_down >> 3) - z
    away = jnp.where(away < 0, away + nz, away)
    position = jnp.where(away <= nz // 2, 2 * away - 1, 2 * (nz - away))
    position = jnp.where(away == 0, 0, position)
    group_down = jnp.zeros_like(position)
    for g in range(1, groups):
        group_down = group_down + jnp.where(position >= g * per, 1, 0)
    place = ((owner_down & 1) * groups + group_down) * CHIPS_Y + ((owner_down >> 1) & 3)
    place = (place * per + position - group_down * per) * BLOCK + rank_down.astype(jnp.int32)

    fold[...] = jnp.where(iota((nb, 2 * nb), 0) == (iota((nb, 2 * nb), 1) >> 1), 1.0, 0.0).astype(
        BF16
    )
    for s in range(2):
        for n in range(parts):
            hit = (iota((GROUP, LANES), 0) + n * GROUP == slot_column) & (
                (iota((GROUP, LANES), 1) >> 3) == s
            )
            pick[s, n * GROUP : (n + 1) * GROUP, :] = jnp.where(hit, 1.0, 0.0).astype(BF16)

    half = nb // 2
    taken[...] = jnp.zeros_like(taken)
    for s in range(2):
        pltpu.make_async_copy(x_buf.at[s], x_buf.at[s], load_sem.at[s]).wait()
        taken[...] += jnp.dot(
            x_buf[s].reshape(2 * nb, plane), pick[s], preferred_element_type=F32
        )
    keep = (iota((2 * nb, LANES), 0) & 1) == slot_plane
    folded = jnp.dot(
        fold[...], jnp.where(keep, taken[...], 0.0).astype(BF16), preferred_element_type=F32
    )
    halves = [folded[half * i : half * (i + 1), :].T[:BLOCK, :] for i in range(2)]
    mine = jnp.where(((iota((BLOCK, half), 0) >> 2) & 1) == 0, halves[0], halves[1])
    g_buf[core, y, 0] = mine.astype(BF16)

    pl.semaphore_wait(barrier, nz - 1 + len(same_z) + 2 + 4)

    def z_copy(i):
        away = (i + 1) // 2 if i % 2 else -(i // 2)
        return pltpu.make_async_remote_copy(
            src_ref=g_buf.at[core, y, 0], dst_ref=g_buf.at[core, y, i],
            send_sem=zs, recv_sem=zr.at[i // per],
            **to({"brick": brick_at(lax.rem(z - away + nz, nz), y, core)})
        )

    for i in range(1, nz):
        z_copy(i).start()

    for o in (-2, -1, 1, 2):
        copy = pltpu.make_async_remote_copy(
            src_ref=table_ref, dst_ref=eps_all.at[2 - o],
            send_sem=es, recv_sem=er, **to({"brick": brick_off(o)})
        )
        copy.start()

    @pl.loop(0, sel.shape[1] // GROUP)
    def _(n):
        column = iota((npts, GROUP), 1) + n * GROUP
        for q in range(4):
            hit = column == place + q * MOST
            sel[pl.ds(q * npts, npts), pl.ds(pl.multiple_of(n * GROUP, GROUP), GROUP)] = (
                jnp.where(hit, 1.0, 0.0).astype(BF16)
            )

    for p in range(2):
        spread[:, 2 * nb * p : 2 * nb * (p + 1)] = jnp.where(
            iota((nb, 2 * nb), 1) == 2 * iota((nb, 2 * nb), 0) + p, 1.0, 0.0
        ).astype(BF16)

    y_up, y_down = lax.rem(y + 1, CHIPS_Y), lax.rem(y + 3, CHIPS_Y)

    def y_copy(g, way):
        on = way == 2 and g == 0
        source = y_down if on else y
        target = (y_up, y_down, y_up if on else lax.rem(y + 2, CHIPS_Y))[way]
        part_of = g_buf.at[core, source, pl.ds(g * per, per)]
        return pltpu.make_async_remote_copy(
            src_ref=part_of, dst_ref=part_of, send_sem=ys,
            recv_sem=yr.at[g, 0 if (g, way) == (0, 0) else 1],
            **to({"brick": brick_at(z, target, core)})
        )

    def y_arrived(g, n):
        block = g_buf.at[core, pl.ds(0, 1 if n == 0 else 2 if g == 0 else 3), pl.ds(g * per, per)]
        pltpu.make_async_remote_copy(
            src_ref=block, dst_ref=block, send_sem=ys, recv_sem=yr.at[g, n],
            **to({"brick": brick_at(z, y_up, core)})
        ).wait_recv()

    def core_copy(g):
        part_of = g_buf.at[core, :, pl.ds(g * per, per)]
        return pltpu.make_async_remote_copy(
            src_ref=part_of, dst_ref=part_of, send_sem=cs, recv_sem=cr.at[g],
            **to({"brick": brick_at(z, y, 1 - core)})
        )

    columns_of = CHIPS_Y * per * BLOCK

    def find(c, g):
        rows = g_buf[c, :, pl.ds(g * per, per)].reshape(columns_of, LANES)
        start = pl.multiple_of((c * groups + g) * columns_of, columns_of)
        return jnp.dot(sel[:, pl.ds(start, columns_of)], rows, preferred_element_type=F32)

    found[...] = jnp.zeros_like(found)
    far = groups - 1

    def far_copy(dy, dc):
        block = g_buf.at[core, y, pl.ds(far * per, per)]
        return pltpu.make_async_remote_copy(
            src_ref=block, dst_ref=block, send_sem=fs.at[dc], recv_sem=fr.at[dc], **at_z(dy, dc)
        )

    for step in range(groups + 2):
        if step < groups:
            come = g_buf.at[core, y, pl.ds(max(1, step * per), per if step else per - 1)]
            pltpu.make_async_remote_copy(
                src_ref=come, dst_ref=come, send_sem=zs, recv_sem=zr.at[step],
                **to({"brick": brick_at(lax.rem(z + 1, nz), y, core)})
            ).wait_recv()
        if step < far:
            for way in (0, 1) if step == 0 else (2, 0, 1):
                y_copy(step, way).start()
        if step == far:
            for dy, dc in same_z:
                far_copy(dy, dc).start()
        if step == 1:
            y_arrived(0, 0)
            y_copy(0, 2).start()
        if 2 <= step <= far + 1:
            g = step - 2
            y_arrived(g, 1)
            core_copy(g).start()
    for g in range(far):
        found[...] += find(core, g)
    for g in range(far):
        block = g_buf.at[1 - core, :, pl.ds(g * per, per)]
        pltpu.make_async_remote_copy(
            src_ref=block, dst_ref=block, send_sem=cs, recv_sem=cr.at[g],
            **to({"brick": brick_at(z, y, 1 - core)})
        ).wait_recv()
        found[...] += find(1 - core, g)
    for dc in range(CORES):
        c = 1 - core if dc else core
        block = g_buf.at[c, pl.ds(0, CHIPS_Y - 1 + dc), pl.ds(far * per, per)]
        pltpu.make_async_remote_copy(
            src_ref=block, dst_ref=block, send_sem=fs.at[dc], recv_sem=fr.at[dc], **at_z(1, 0)
        ).wait_recv()
        found[...] += find(c, far)

    for s in range(2):
        at_points = jnp.concatenate(
            [found[(2 * s + i) * npts : (2 * s + i + 1) * npts, :] for i in range(2)], axis=1
        ).astype(BF16)
        wide = jnp.dot(at_points, spread[...], preferred_element_type=F32).astype(BF16)
        for p in range(2):
            z_buf[s, p * npts : (p + 1) * npts, :] = wide[:, 2 * nb * p : 2 * nb * (p + 1)]

    @pl.loop(0, parts)
    def _(n):
        at = pl.ds(pl.multiple_of(n * GROUP, GROUP), GROUP)
        for s in range(2):
            got = jnp.dot(
                z_buf[s], x_buf[s, :, :, at].reshape(2 * nb, GROUP), preferred_element_type=F32
            )
            part[s, :, :, at] = got.reshape(2, npts, GROUP)

    code_lane = iota((16, LANES), 1)

    def lanes_of(n):
        return slice(n * GROUP + LANES * (n >= parts), (n + 1) * GROUP + LANES * (n >= parts))

    def pack(*messages):
        scales = []
        for values_at, target, count in messages:
            most = jnp.zeros((16, LANES), F32)
            for n in range(count):
                peak = jnp.max(jnp.abs(values_at(n)), axis=1, keepdims=True)
                most = jnp.where(code_lane == n, peak, most)
            code = jnp.ceil(jnp.log2(jnp.maximum(most, 1e-30)) * CODE)
            scales.append((code, STEP * jnp.exp2(code * (-1.0 / CODE))))
        for (values_at, target, count), (code, scale) in zip(messages, scales):
            first_of = min(count, parts) * GROUP
            target[:, first_of : first_of + LANES] = code.astype(jnp.int32).astype(jnp.int16)
            for n in range(count):
                whole = jnp.round(values_at(n) * scale[:, n : n + 1])
                target[:, lanes_of(n)] = whole.astype(jnp.int32).astype(jnp.int16)

    def unpacker(source, count):
        first_of = min(count, parts) * GROUP
        codes = source[:, first_of : first_of + LANES].astype(jnp.int32).astype(F32)
        scales = jnp.exp2(codes * (1.0 / CODE)) * (1.0 / STEP)

        def values_at(n):
            got = source[:, lanes_of(n)].astype(jnp.int32).astype(F32)
            return got * scales[:, n : n + 1]

        return values_at

    def held(target, p, k):
        start = pl.multiple_of(target * fields + k * 8, 8)

        def values_at(n):
            at = slice(n * GROUP, (n + 1) * GROUP)
            return jnp.concatenate(
                [part[0, p, pl.ds(start, 8), at], part[1, p, pl.ds(start, 8), at]], axis=0
            )

        return values_at

    up, down, across = band_off(1), band_off(3), band_off(2)
    heading = (up, down)

    pieces = ((0, plane + LANES), (plane + LANES, plane))

    def a_copy(k, way, piece):
        at = pl.ds(*pieces[piece])
        return pltpu.make_async_remote_copy(
            src_ref=out_a.at[way, k, :, at], dst_ref=in_a.at[way, k, :, at],
            send_sem=xas, recv_sem=xar.at[piece, k], **to({"band": heading[way]})
        )

    def c_copy(k, way):
        return pltpu.make_async_remote_copy(
            src_ref=out_c.at[way, k], dst_ref=in_c.at[way, k],
            send_sem=xcs, recv_sem=xcr.at[k], **to({"band": heading[way]})
        )

    def send(k):
        def message(way):
            passed, direct = held(across, way, k), held(heading[way], 1 - way, k)
            return (
                lambda n: passed(n) if n < parts else direct(n - parts),
                out_a.at[way, k], 2 * parts,
            )

        pack(message(0), message(1))
        for piece in range(2):
            for way in range(2):
                a_copy(k, way, piece).start()

    def arrived(k, piece):
        both = in_a.at[:, k, :, pl.ds(*pieces[piece])]
        pltpu.make_async_remote_copy(
            src_ref=both, dst_ref=both, send_sem=xas, recv_sem=xar.at[piece, k],
            **to({"band": up})
        ).wait_recv()

    def join(k):
        arrived(k, 0)
        def message(way):
            mine_at, got_at = held(heading[way], way, k), unpacker(in_a.at[way, k], 2 * parts)
            return lambda n: mine_at(n) + got_at(n), out_c.at[way, k], parts

        pack(message(0), message(1))
        for way in range(2):
            c_copy(k, way).start()

    sides = ((-2, 0, 1, 5), (-1, 0, 2, 3), (1, 0, 2, 1), (2, 1, 1, 0))

    def h_copy(k, n):
        o, source, count, target = sides[n]
        return pltpu.make_async_remote_copy(
            src_ref=out_h.at[k, source : source + count],
            dst_ref=in_h.at[k, target : target + count],
            send_sem=hs, recv_sem=hr.at[k], **to({"brick": brick_off(o)})
        )

    def out_copy(which, p, start, count):
        rows = pl.ds(start, count)
        return pltpu.make_async_copy(
            (field, result)[which].at[p, rows], (pair_ref, pot_ref)[which].at[rows, p, :],
            out_sem.at[which],
        )

    def product(k):
        arrived(k, 1)
        both = in_c.at[:, k]
        pltpu.make_async_remote_copy(
            src_ref=both, dst_ref=both, send_sem=xcs, recv_sem=xcr.at[k], **to({"band": up})
        ).wait_recv()
        rows = pl.ds(pl.multiple_of(k * 8, 8), 8)
        for p in range(2):
            direct = unpacker(in_a.at[1 - p, k], 2 * parts)
            parts_at = (
                held(band, p, k), lambda n: direct(n + parts), unpacker(in_c.at[p, k], parts)
            )
            pairs = []
            for n in range(parts):
                total = sum(values_at(n) for values_at in parts_at)
                pairs.append(total[:8, :] * total[8:, :])
            for n in range(parts):
                field[p, rows, n * GROUP : (n + 1) * GROUP] = pairs[n]

        def message(p):
            def halves(n):
                return jnp.concatenate(
                    [
                        field[p, rows, m * GROUP : (m + 1) * GROUP]
                        for m in (n, n + parts // 2)
                    ],
                    axis=0,
                )

            return halves, out_h.at[k, p], parts // 2

        pack(message(0), message(1))

        @pl.when(k == chunks - 1)
        def _():
            for p in range(2):
                out_copy(0, p, 0, fields).start()

    low_half = iota((8, LANES), 1) < NZ

    def sweep(source, e):
        tile_at = [pl.ds(t * LANES, LANES) for t in range(tiles)]
        swapped = [pltpu.roll(source[e, :, at], NZ, 1) for at in tile_at]
        news = []
        for t, at in enumerate(tile_at):
            v = source[e, :, at]
            before = swapped[(t - 1) % tiles]
            after = swapped[(t + 1) % tiles]
            alone = (1.0 - OMEGA) * v + first[e, :, at]
            along_x = coef[0, e, :, at] * source[e - 1, :, at]
            along_x = along_x + coef[1, e, :, at] * source[e + 1, :, at]
            along_y = coef[2, e, :, at] * jnp.where(low_half, before, swapped[t])
            along_y = along_y + coef[3, e, :, at] * jnp.where(low_half, swapped[t], after)
            along_z = coef[4, e, :, at] * pltpu.roll(v, 1, 1)
            along_z = along_z + coef[5, e, :, at] * pltpu.roll(v, LANES - 1, 1)
            news.append((alone + along_x) + (along_y + along_z))
        return zip(tile_at, news)

    def sweeps(k):
        come = in_h.at[k]
        pltpu.make_async_remote_copy(
            src_ref=come, dst_ref=come, send_sem=hs, recv_sem=hr.at[k],
            **to({"brick": brick_off(1)})
        ).wait_recv()
        rows = pl.ds(pl.multiple_of(k * 8, 8), 8)
        for p in range(2):
            first[3 + p] = coef[6, 3 + p] * field[p, rows, :]

        @pl.loop(0, 6)
        def _(i):
            e = i + 2 * (i // 3)
            halves = unpacker(in_h.at[k, i], parts // 2)
            values = [halves(n) for n in range(parts // 2)]
            for m in range(parts):
                at = slice(m * GROUP, (m + 1) * GROUP)
                half = values[m % (parts // 2)][8 * (m // (parts // 2)) :, :][:8, :]
                first[e, :, at] = coef[6, e, :, at] * half

        @pl.loop(1, 7)
        def _(e):
            for at, new in sweep(first, e):
                second[e, :, at] = new

        @pl.loop(2, 6)
        def _(e):
            for at, new in sweep(second, e):
                third[e, :, at] = new

        @pl.loop(3, 5)
        def _(e):
            for at, new in sweep(third, e):
                result[e - 3, rows, at] = new

        last = 8 * (chunks - 1)

        @pl.when(k == chunks - 2)
        def _():
            for p in range(2):
                out_copy(1, p, 0, last).start()

        @pl.when(k == chunks - 1)
        def _():
            for p in range(2):
                out_copy(1, p, last, 8).start()

    def coefficients():
        pltpu.make_async_remote_copy(
            src_ref=eps_all.at[0:4], dst_ref=eps_all.at[0:4], send_sem=es, recv_sem=er,
            **to({"brick": brick_off(1)})
        ).wait()
        for o in range(5):
            eps_rows[2 * o : 2 * o + 2, :] = table_ref[:2, :] if o == 2 else eps_all[o, :2, :]
        here = eps_rows[1:9, :]
        xminus = 0.5 * (here + eps_rows[0:8, :])
        xplus = 0.5 * (here + eps_rows[2:10, :])
        depth = iota((8, plane), 1) & (NZ - 1)
        above = depth < NZ - 1
        below = depth > 0
        yplus = 0.5 * (here + pltpu.roll(here, plane - NZ, 1))
        yminus = 0.5 * (here + pltpu.roll(here, NZ, 1))
        zplus = 0.5 * (here + jnp.where(above, pltpu.roll(here, plane - 1, 1), here))
        zminus = 0.5 * (here + jnp.where(below, pltpu.roll(here, 1, 1), here))
        scale = OMEGA / (xplus + xminus + yplus + yminus + zplus + zminus)
        faces = (
            xminus, xplus, yminus, yplus,
            jnp.where(below, zminus, 0.0), jnp.where(above, zplus, 0.0), FOURPI,
        )
        for n, face in enumerate(faces):
            scaled = scale * face
            for e in range(8):
                coef[n, e] = jnp.broadcast_to(scaled[e : e + 1, :], (8, plane))

    @pl.loop(0, chunks + 6)
    def _(step):
        @pl.when(step < chunks)
        def _():
            send(step)

        @pl.when((step >= 2) & (step < chunks + 2))
        def _():
            join(step - 2)

        @pl.when(step == 3)
        def _():
            coefficients()

        @pl.when((step >= 4) & (step < chunks + 4))
        def _():
            product(step - 4)
            for n in range(4):
                h_copy(step - 4, n).start()

        @pl.when(step >= 6)
        def _():
            sweeps(step - 6)

    def sent(ref, sem, recv_sem):
        pltpu.make_async_remote_copy(
            src_ref=ref, dst_ref=ref, send_sem=sem, recv_sem=recv_sem,
            **to({"brick": brick_off(1)})
        ).wait_send()

    sent(g_buf.at[core, y, pl.ds(1, nz - 1)], zs, zr.at[0])
    near = pl.ds(0, far * per)
    sent(g_buf.at[core, pl.ds(0, 3), near], ys, yr.at[0, 0])
    sent(g_buf.at[core, :, near], cs, cr.at[0])
    for dc in range(CORES):
        sent(g_buf.at[core, pl.ds(0, 3 + dc), pl.ds(far * per, per)], fs.at[dc], fr.at[dc])
    sent(out_a, xas, xar.at[0, 0])
    sent(out_c, xcs, xcr.at[0])
    sent(in_h, hs, hr.at[0])
    for which, ref in enumerate((field, result)):
        pltpu.make_async_copy(ref, ref, out_sem.at[which]).wait()


def local(bricks, nx, psi_val, psi_cond, dielectric, point_owner, point_cell):
    nb, _, plane = psi_val.shape
    npts = point_owner.shape[0]
    nz = bricks // (CHIPS_Y * CORES)
    groups = min(4, nz)
    fields = npts // nx
    chunks = fields // 8
    rows = bricks * BLOCK

    def row(values):
        return jnp.pad(values[None, :], ((0, 0), (0, plane - npts))).astype(F32)

    table = jnp.concatenate([dielectric, row(point_owner), row(point_cell)], axis=0)

    vmem = pl.BlockSpec(memory_space=pltpu.VMEM)
    dma = pltpu.SemaphoreType.DMA
    pair, potential = pl.pallas_call(
        functools.partial(kernel, nz, nx),
        out_shape=[jax.ShapeDtypeStruct((fields, 2, plane), F32)] * 2,
        in_specs=[
            vmem, pl.BlockSpec(memory_space=pl.ANY), pl.BlockSpec(memory_space=pl.ANY),
        ],
        out_specs=[pl.BlockSpec(memory_space=pl.ANY)] * 2,
        scratch_shapes=[
            pltpu.VMEM((2, nb // 8, 16, plane), BF16),
            pltpu.VMEM((CORES, CHIPS_Y, nz, BLOCK, LANES), BF16),
            pltpu.VMEM((4 * npts, rows), BF16),
            pltpu.VMEM((4 * npts, LANES), F32),
            pltpu.VMEM((nb, 4 * nb), BF16),
            pltpu.VMEM((nb, 2 * nb), BF16),
            pltpu.VMEM((2, plane, LANES), BF16),
            pltpu.VMEM((2 * nb, LANES), F32),
            pltpu.VMEM((2, 2 * npts, 2 * nb), BF16),
            pltpu.VMEM((2, 2, npts, plane), F32),
            pltpu.VMEM((2, chunks, 16, 2 * plane + LANES), jnp.int16),
            pltpu.VMEM((2, chunks, 16, 2 * plane + LANES), jnp.int16),
            pltpu.VMEM((2, chunks, 16, plane + LANES), jnp.int16),
            pltpu.VMEM((2, chunks, 16, plane + LANES), jnp.int16),
            pltpu.VMEM((5, 4, plane), F32),
            pltpu.VMEM((16, plane), F32),
            pltpu.VMEM((7, 8, 8, plane), F32),
            pltpu.VMEM((chunks, 2, 16, plane // 2 + LANES), jnp.int16),
            pltpu.VMEM((chunks, 6, 16, plane // 2 + LANES), jnp.int16),
            pltpu.VMEM((2, fields, plane), F32),
            pltpu.VMEM((8, 8, plane), F32),
            pltpu.VMEM((8, 8, plane), F32),
            pltpu.VMEM((8, 8, plane), F32),
            pltpu.VMEM((2, fields, plane), F32),
            dma((2,)),
            dma, dma((groups,)),
            dma, dma((groups, 2)),
            dma, dma((groups,)),
            dma((CORES,)), dma((CORES,)),
            dma, dma((2, chunks)),
            dma, dma((chunks,)),
            dma, dma((chunks,)),
            dma, dma,
            dma((2,)),
        ],
        compiler_params=pltpu.CompilerParams(
            collective_id=0, has_side_effects=True, vmem_limit_bytes=52 << 20
        ),
        cost_estimate=pl.CostEstimate(
            flops=2 * 2 * 2 * npts * 2 * nb * plane,
            bytes_accessed=8 * nb * plane + 16 * fields * plane,
            transcendentals=0,
        ),
    )(
        table, psi_val.reshape(nb // 8, 8, 2, plane), psi_cond.reshape(nb // 8, 8, 2, plane),
    )
    return pair, potential


def solution(mesh):
    return jax.shard_map(
        functools.partial(local, mesh.shape["brick"], mesh.shape["band"]),
        mesh=mesh,
        in_specs=(P("band", "brick", None), P("band", "brick", None), P("brick", None), P(), P()),
        out_specs=(P("band", "brick", None), P("band", "brick", None)),
        check_vma=False,
    )
```
